32 devices in a mesh: dp: 8 (over y, x, core), seq: 4 (over z).
Axes of the slice: x: 2, y: 2, z: 4, core: 2. Of those that a mesh axis runs over, the one named last changes fastest.
Arguments:
- features: bfloat16 [8, 512, 2560], P('dp', 'seq'), may hold values from -6 to 6
- head_inputs: bfloat16 [8, 512, 2560], P('dp', 'seq'), may hold values from -6 to 6
- out_grad: bfloat16 [8, 512, 2560], P('dp', 'seq'), may hold values from -6 to 6
- bc_weight: bfloat16 [2560, 128], P('dp'), may hold values from -0.125 to 0.125
- dt_weight: bfloat16 [2560, 40], P('dp'), may hold values from -0.125 to 0.125
- dt_bias: float32 [40], replicated, may hold values from -7 to -5.5
- decay_rate: float32 [40], replicated, may hold values from 0.3125 to 16
- skip_gain: float32 [40], replicated, may hold values from 0.5 to 1.5
Outputs:
- input_grad: bfloat16 [8, 512, 2560], P('dp', 'seq')
- head_grad: bfloat16 [8, 512, 2560], P('dp', 'seq')
- bc_weight_grad: float32 [2560, 128], P('dp')
- dt_weight_grad: float32 [2560, 40], P('dp')
The draws below stay inside these ranges and needn't reach their ends.
All inputs are finite; a program needn't handle non-finite values.
Results may differ from the reference program's by a relative error of at most 0.0049.
Values may be sent and summed in bfloat16 or wider, within the bound.
A program may use at most 128 MiB of HBM per device.

```python
import math
from functools import partial
import jax
import jax.numpy as jnp
from jax import lax

D = 2560
HEADS = 40
HEAD_DIM = 64
STATE = 64
TOK_DEV = 128
STREAMS = 8
SEQ_LEN = 512
INNER = 2560


def spiked(drawn, key, source, target, shards_of, factor):
    def block_of(dim):
        return (jnp.arange(drawn.shape[dim]) // (drawn.shape[dim] // shards_of)).reshape((-1,) + (1,) * (drawn.ndim - 1 - dim))

    near = jax.random.permutation(key, shards_of)[block_of(target)]
    second = (block_of(target) + shards_of // 2) % shards_of
    return jnp.where((block_of(source) == near) | (block_of(source) == second), factor * drawn, drawn)


def block_scale(rng, shape, shards, least, largest):
    factor_of, own = 1.0, jax.random.fold_in(rng, 6)
    for position, parts in shards:
        steps = jnp.exp(jax.random.uniform(jax.random.fold_in(own, position), (parts,), jnp.float32, least / len(shards), largest / len(shards)))
        factor_of = factor_of * jnp.repeat(steps, shape[position] // parts).reshape([-1 if axis == position else 1 for axis in range(len(shape))])
    return factor_of


def bell_draw(own_key, dims, spread, most, split=(), held_as=jnp.bfloat16):
    array = spread * jax.random.normal(own_key, dims, jnp.float32)
    if split:
        array = array * block_scale(own_key, dims, split, -0.22, 0.18)
    return jnp.clip(array, -most, most).astype(held_as)


def bell_draw_with(key, dims, width, limit, split, heavy, kind=jnp.bfloat16):
    entries = width * jax.random.normal(key, dims, jnp.float32)
    if split:
        entries = entries * block_scale(key, dims, split, -0.22, 0.18)
    return jnp.clip(spiked(entries, jax.random.fold_in(key, 3), *heavy), -limit, limit).astype(kind)


def setup_inputs(seed: int = 0) -> dict:
    seeds = jax.random.split(jax.random.key(seed), 9)
    features = bell_draw_with(seeds[0], (STREAMS, SEQ_LEN, D), 1.0, 6.0, ((0, 8), (1, 4)), (0, 2, 8, 2.0))
    head_inputs = bell_draw(seeds[1], (STREAMS, SEQ_LEN, INNER), 1.0, 6.0, ((0, 8), (1, 4)))
    out_grad = bell_draw(seeds[2], (STREAMS, SEQ_LEN, INNER), 1.0, 6.0, ((0, 8), (1, 4)))
    bc_weight = bell_draw(seeds[3], (D, 2 * STATE), D ** -0.5, 0.125, ((0, 8),))
    dt_weight = bell_draw(seeds[4], (D, HEADS), D ** -0.5, 0.125, ((0, 8),))
    dt_bias = jnp.clip(jax.random.uniform(seeds[5], (HEADS,), jnp.float32, -7.0, -5.5), -7.0, -5.5)
    decay_rate = jnp.clip(jnp.exp(jax.random.uniform(seeds[6], (HEADS,), jnp.float32, math.log(0.3125), math.log(16.0))), 0.3125, 16.0)
    skip_gain = jnp.clip(jax.random.uniform(seeds[7], (HEADS,), jnp.float32, 0.5, 1.5), 0.5, 1.5)
    return dict(features=features, head_inputs=head_inputs, out_grad=out_grad, bc_weight=bc_weight, dt_weight=dt_weight, dt_bias=dt_bias, decay_rate=decay_rate, skip_gain=skip_gain)


highest = lax.Precision.HIGHEST

def spread_heads(values, head_size):
    return jnp.repeat(values, head_size, axis=-1)

def block_pass(decay_rate, skip_gain, carry_state, block):
    inputs_f, step_size, b_rows, c_rows = block
    length = inputs_f.shape[0]
    log_decay = -decay_rate[None, :] * step_size
    cumulative = jnp.cumsum(log_decay, axis=0)
    total_decay = cumulative[-1]
    scaled_in = inputs_f * spread_heads(step_size, HEAD_DIM)
    positions = jnp.arange(length)
    causal = positions[:, None] >= positions[None, :]
    gap = cumulative.T[:, :, None] - cumulative.T[:, None, :]
    weights_mat = jnp.exp(jnp.where(causal[None], gap, -1e+30))
    intersection = jnp.dot(c_rows, b_rows.T, precision=highest)
    mixing = intersection[None] * weights_mat
    inner_out = jnp.einsum('htu,uhp->thp', mixing, scaled_in.reshape(length, HEADS, HEAD_DIM), precision=highest)
    inner_out = inner_out.reshape(length, INNER)
    carried_out = jnp.dot(c_rows, carry_state, precision=highest) * spread_heads(jnp.exp(cumulative), HEAD_DIM)
    output = inner_out + carried_out + inputs_f * spread_heads(skip_gain, HEAD_DIM)[None, :]
    to_end = spread_heads(jnp.exp(total_decay[None, :] - cumulative), HEAD_DIM)
    local_state = jnp.dot(b_rows.T, scaled_in * to_end, precision=highest)
    new_state = carry_state * spread_heads(jnp.exp(total_decay), HEAD_DIM)[None, :] + local_state
    return (new_state, output)

def stream_core(inputs_f, step_size, b_rows, c_rows, decay_rate, skip_gain):
    blocks = (inputs_f.reshape(-1, TOK_DEV, INNER), step_size.reshape(-1, TOK_DEV, HEADS), b_rows.reshape(-1, TOK_DEV, STATE), c_rows.reshape(-1, TOK_DEV, STATE))
    start_state = jnp.zeros((STATE, INNER), jnp.float32)
    final_state, outputs = lax.scan(partial(block_pass, decay_rate, skip_gain), start_state, blocks)
    return outputs.reshape(SEQ_LEN, INNER)

def reference(features, head_inputs, out_grad, bc_weight, dt_weight, dt_bias, decay_rate, skip_gain):
    joined = jnp.concatenate([bc_weight, dt_weight], axis=1)

    def one_stream(total, stream):
        feature_rows, input_rows, grad_rows = stream
        projection = jnp.dot(feature_rows, joined, preferred_element_type=jnp.float32)
        b_rows = projection[:, :STATE]
        c_rows = projection[:, STATE:2 * STATE]
        pre_step = projection[:, 2 * STATE:] + dt_bias[None, :]
        step_size = jax.nn.softplus(pre_step)
        inputs_f = input_rows.astype(jnp.float32)

        def core_fn(first, second, third, fourth):
            return stream_core(first, second, third, fourth, decay_rate, skip_gain)
        output, pullback = jax.vjp(core_fn, inputs_f, step_size, b_rows, c_rows)
        inputs_grad, step_grad, b_grad, c_grad = pullback(grad_rows.astype(jnp.float32))
        pre_grad = step_grad * jax.nn.sigmoid(pre_step)
        proj_grad = jnp.concatenate([b_grad, c_grad, pre_grad], axis=1).astype(jnp.bfloat16)
        feature_grad = lax.dot_general(proj_grad, joined, (((1,), (1,)), ((), ())), preferred_element_type=jnp.float32).astype(jnp.bfloat16)
        total = total + lax.dot_general(feature_rows, proj_grad, (((0,), (0,)), ((), ())), preferred_element_type=jnp.float32)
        return (total, (feature_grad, inputs_grad.astype(jnp.bfloat16)))
    start_total = jnp.zeros((D, 2 * STATE + HEADS), jnp.float32)
    total, results = lax.scan(one_stream, start_total, (features, head_inputs, out_grad))
    input_grad, head_grad = results
    total = total * (1.0 / math.sqrt(STREAMS * SEQ_LEN))
    return (input_grad, head_grad, total[:, :2 * STATE], total[:, 2 * STATE:])
```

```python
import functools
import math

import jax
import jax.numpy as jnp
from jax import lax
from jax.experimental import pallas as pl
from jax.experimental.pallas import tpu as pltpu
from jax.sharding import PartitionSpec as P

MESH = pl.DeviceIdType.MESH
F32, BF16 = jnp.float32, jnp.bfloat16
LANES = 128
CHUNK = 512
HIGHEST = lax.Precision.HIGHEST
NT = (((1,), (1,)), ((), ()))
TN = (((0,), (0,)), ((), ()))


def halves(value):
    high = value.astype(BF16)
    return high, (value - high.astype(F32)).astype(BF16)


def mm(left, right, dims=None):
    if dims is None:
        return jnp.dot(left, right, preferred_element_type=F32)
    return lax.dot_general(left, right, dims, preferred_element_type=F32)


def iota(shape, dim):
    return lax.broadcasted_iota(jnp.int32, shape, dim)


def kernel(
    dp, seq, heads, scale,
    f_ref, x_ref, g_ref, wbc_ref, wdt_ref, bias_ref, decay_ref, skip_ref,
    ig_ref, hg_ref, bcg_ref, dtg_ref, *,
    wall, par, pre_s, step_s, cum_s, cumt_s, ecum_s, toend_s, proj_s, bct_s, inter_s, rows_s,
    ig_acc, step_w, ecum_w, toend_w, end_w, wgrad, sgrad, left_s, right_s,
    fin, bin_, fout, bout, red_s, bg_s, cg_s, gp_s,
    gw, gw_out, rb1, s_out, rb2, zout, zin, final,
    ag_send, ag_recv, fw_send, fw_recv, ch_send, ch_recv,
    r1_send, r1_recv, r2_send, r2_recv, zr_send, zr_recv, za_send, za_recv,
):
    me, z = lax.axis_index("dp"), lax.axis_index("seq")
    last = seq - 1
    half = dp // 2
    sib = me + 1 - 2 * lax.rem(me, 2)
    length, inner = x_ref.shape
    rows = wbc_ref.shape[0]
    state = wbc_ref.shape[1] // 2
    head_size = inner // heads
    chunks = inner // CHUNK
    piece = -(-rows // (16 * seq)) * 16
    owners = -(-rows // piece)

    def at_dp(target):
        return (target, z)

    def peer(k):
        return lax.rem(me + 2 * k, dp)

    def source(k):
        return lax.rem(me + dp - 2 * k, dp)

    barrier = pltpu.get_barrier_semaphore()
    pl.semaphore_signal(barrier, inc=1, device_id=at_dp(sib), device_id_type=MESH)
    for k in range(1, half):
        pl.semaphore_signal(barrier, inc=1, device_id=at_dp(peer(k)), device_id_type=MESH)
    for k in range(1, seq):
        pl.semaphore_signal(barrier, inc=1, device_id=(me, lax.rem(z + k, seq)), device_id_type=MESH)

    def block(index):
        return pl.ds(pl.multiple_of(index * rows, 16), rows)

    wall[block(me), 0:LANES] = wbc_ref[...]
    wide = jnp.concatenate(
        [wdt_ref[...].astype(F32), jnp.zeros((rows, LANES - heads), F32)], axis=1
    )
    wall[block(me), LANES:] = wide.astype(BF16)
    par[...] = jnp.zeros_like(par)
    par[0:1, 0:heads] = bias_ref[...]
    par[1:2, 0:heads] = decay_ref[...]
    par[2:3, 0:heads] = skip_ref[...]
    pl.semaphore_wait(barrier, half + seq - 1)

    def ag_copy(k, owner, target):
        return pltpu.make_async_remote_copy(
            src_ref=wall.at[block(owner)], dst_ref=wall.at[block(owner)],
            send_sem=ag_send.at[k], recv_sem=ag_recv.at[k],
            device_id=at_dp(target), device_id_type=MESH,
        )

    def fw_copy(k, owner):
        return pltpu.make_async_remote_copy(
            src_ref=wall.at[block(owner)], dst_ref=wall.at[block(owner)],
            send_sem=fw_send.at[k], recv_sem=fw_recv.at[k],
            device_id=at_dp(sib), device_id_type=MESH,
        )

    for k in range(1, half):
        ag_copy(k, me, peer(k)).start()
    ag_copy(0, me, sib).start()
    for k in range(1, half):
        ag_copy(k, source(k), peer(k)).wait_recv()
        fw_copy(k, source(k)).start()
    ag_copy(0, sib, sib).wait_recv()
    for k in range(1, half):
        fw_copy(k, lax.rem(sib + dp - 2 * k, dp)).wait_recv()

    projection = mm(f_ref[...], wall[...])
    proj_s[...] = projection[:, :LANES]
    pre = projection[:, LANES:] + par[0:1, :]
    pre_s[...] = pre
    step = jnp.maximum(pre, 0.0) + jnp.log1p(jnp.exp(-jnp.abs(pre)))
    step_s[...] = step
    lower = (iota((length, length), 0) >= iota((length, length), 1)).astype(F32)
    cum = jnp.dot(
        lower, -par[1:2, :] * step, precision=HIGHEST, preferred_element_type=F32
    )
    cum_s[...] = cum
    cumt_s[...] = cum.T
    ecum_s[...] = jnp.exp(cum)
    toend_s[...] = jnp.exp(cum[length - 1 :, :] - cum)
    bct_s[...] = proj_s[...].T
    bt = bct_s[0:state, :]
    ct = bct_s[state:, :]
    bt_hi, bt_lo = halves(bt)
    ct_hi, ct_lo = halves(ct)
    bt3 = jnp.concatenate([bt_hi, bt_lo, bt_hi], axis=1)
    ct3 = jnp.concatenate([ct_hi, ct_lo, ct_hi], axis=1)
    b_rows = proj_s[:, 0:state]
    c_rows = proj_s[:, state:]
    inter_s[...] = jnp.dot(b_rows, ct, precision=HIGHEST, preferred_element_type=F32)

    def spread(value, c):
        high, low = halves(value)
        row = iota((LANES, CHUNK), 0)
        hot = (row == c * (CHUNK // head_size) + iota((LANES, CHUNK), 1) // head_size)
        hot = hot.astype(F32).astype(BF16)
        return mm(jnp.concatenate([high, low], axis=1), jnp.concatenate([hot, hot], axis=0))

    def lanes(c):
        return pl.ds(pl.multiple_of(c * CHUNK, CHUNK), CHUNK)

    @pl.loop(0, chunks)
    def _(c):
        cs = lanes(c)
        step_c = spread(step_s[...], c)
        ecum_c = spread(ecum_s[...], c)
        toend_c = spread(toend_s[...], c)
        ends = x_ref[:, cs].astype(F32) * step_c * toend_c
        weighted = g_ref[:, cs].astype(F32) * ecum_c
        step_w[:, cs] = step_c
        ecum_w[:, cs] = ecum_c
        toend_w[:, cs] = toend_c
        end_w[:, cs] = ends
        wgrad[:, cs] = weighted
        e_hi, e_lo = halves(ends)
        w_hi, w_lo = halves(weighted)
        left_s[c] = mm(bt3, jnp.concatenate([e_hi, e_hi, e_lo], axis=0))
        right_s[c] = mm(ct3, jnp.concatenate([w_hi, w_hi, w_lo], axis=0))

    def chain_copy(way, c):
        src, dst = ((fout, fin), (bout, bin_))[way]
        to = (z + 1, z + last)[way]
        return pltpu.make_async_remote_copy(
            src_ref=src.at[c], dst_ref=dst.at[c],
            send_sem=ch_send.at[way, c], recv_sem=ch_recv.at[way, c],
            device_id=(me, lax.rem(to, seq)), device_id_type=MESH,
        )

    def chain_hop(way, c):
        arrived, leaving, local = ((fin, fout, left_s), (bin_, bout, right_s))[way]
        first, final_one = ((0, last), (last, 0))[way]

        @pl.when(z == first)
        def _():
            arrived[c] = jnp.zeros((state, CHUNK), arrived.dtype)
            if seq > 1:
                leaving[c] = local[c].astype(leaving.dtype)
                chain_copy(way, c).start()

        @pl.when(z != first)
        def _():
            chain_copy(way, c).wait_recv()

            @pl.when(z != final_one)
            def _():
                decay = ecum_w[length - 1 :, lanes(c)]
                leaving[c] = (arrived[c].astype(F32) * decay + local[c]).astype(leaving.dtype)
                chain_copy(way, c).start()

    later = iota((length, length), 1) >= iota((length, length), 0)
    low_half = iota((length, LANES), 1) < head_size
    per_tile = LANES // head_size

    def tile_work(tile):
        ts = pl.ds(pl.multiple_of(tile * LANES, LANES), LANES)
        x_tile, g_tile = x_ref[:, ts].astype(F32), g_ref[:, ts].astype(F32)
        g_full = g_ref[:, ts]
        step, cum, inter = step_s[...], cum_s[...], inter_s[...]
        mixes, grads = [], []
        for part in range(per_tile):
            head = tile * per_tile + part
            pick = iota((length, LANES), 1) == head
            cum_col = jnp.sum(jnp.where(pick, cum, 0.0), axis=1, keepdims=True)
            step_col = jnp.sum(jnp.where(pick, step, 0.0), axis=1, keepdims=True)
            gap = cumt_s[pl.ds(head, 1), :] - cum_col
            weights = jnp.exp(jnp.where(later, gap, -1e30))
            mine = low_half if part == 0 else jnp.logical_not(low_half)
            x_part = jnp.where(mine, x_tile, 0.0).astype(BF16)
            g_part = jnp.where(mine, g_tile, 0.0).astype(BF16)
            mixing_grad = mm(x_part, g_full, NT) * step_col
            shared = mixing_grad * weights
            ig_acc[...] += shared
            rows_s[pl.ds(head, 1), :] = jnp.sum(shared * inter, axis=0, keepdims=True)
            mixes += list(halves(inter * weights))
            grads += [g_part, g_part]
        sgrad[:, ts] = mm(jnp.concatenate(mixes, axis=1), jnp.concatenate(grads, axis=0))

    def reduce_heads(value, c):
        lane = iota((LANES, CHUNK), 0)
        hot = lane == c * (CHUNK // head_size) + iota((LANES, CHUNK), 1) // head_size
        hot = hot.astype(F32).astype(BF16)
        high, low = halves(value)
        return mm(jnp.concatenate([high, low], axis=1), jnp.concatenate([hot, hot], axis=1), NT)

    b_hi, b_lo = halves(b_rows)
    c_hi, c_lo = halves(c_rows)
    bpair = jnp.concatenate([b_hi, b_lo], axis=1)
    cpair = jnp.concatenate([c_hi, c_lo], axis=1)

    def carried_work(c):
        cs = lanes(c)
        state_in, state_grad = fin[c], bin_[c]
        weighted, ends = wgrad[:, cs], end_w[:, cs]
        inter_out = mm(cpair, jnp.concatenate([state_in, state_in], axis=0))
        reach = mm(bpair, jnp.concatenate([state_grad, state_grad], axis=0))
        w_hi, w_lo = halves(weighted)
        e_hi, e_lo = halves(ends)
        cg_s[...] += mm(w_hi, state_in, NT) + mm(w_lo, state_in, NT)
        bg_s[...] += mm(e_hi, state_grad, NT) + mm(e_lo, state_grad, NT)
        total = sgrad[:, cs] + toend_w[:, cs] * reach
        x_part, g_part = x_ref[:, cs].astype(F32), g_ref[:, cs].astype(F32)
        decay = ecum_w[length - 1 :, cs]
        product = state_grad.astype(F32) * state_in.astype(F32)
        at_end = jnp.sum(ends * reach, axis=0, keepdims=True) + decay * jnp.sum(
            product, axis=0, keepdims=True
        )
        stacked = jnp.concatenate(
            [weighted * inter_out, x_part * total, jnp.broadcast_to(at_end, (8, CHUNK))], axis=0
        )
        red_s[...] += reduce_heads(stacked, c)
        skip_c = spread(jnp.broadcast_to(par[2:3, :], (8, LANES)), c)[0:1, :]
        hg_ref[:, cs] = (g_part * skip_c + step_w[:, cs] * total).astype(BF16)

    ig_acc[...] = jnp.zeros_like(ig_acc)
    rows_s[...] = jnp.zeros_like(rows_s)
    cg_s[...] = jnp.zeros_like(cg_s)
    bg_s[...] = jnp.zeros_like(bg_s)
    red_s[...] = jnp.zeros_like(red_s)
    tiles = CHUNK // LANES

    @pl.loop(0, chunks + last)
    def _(s):
        forward, back = s - z, s - (last - z)

        @pl.when(jnp.logical_and(forward >= 0, forward < chunks))
        def _():
            chain_hop(0, forward)

        @pl.when(jnp.logical_and(back >= 0, back < chunks))
        def _():
            chain_hop(1, back)

        @pl.when(s < chunks)
        def _():
            for tile in range(tiles):
                tile_work(s * tiles + tile)

        both = s - jnp.maximum(z, last - z)

        @pl.when(jnp.logical_and(both >= 0, both < chunks))
        def _():
            carried_work(both)

    acc = ig_acc[...]
    c_grad = cg_s[...] + lax.dot_general(
        acc, b_rows, TN, precision=HIGHEST, preferred_element_type=F32
    )
    b_grad = bg_s[...] + jnp.dot(acc, c_rows, precision=HIGHEST, preferred_element_type=F32)
    step = step_s[...]
    direct = red_s[length : 2 * length, :]
    cum_grad = rows_s[...].T + red_s[0:length, :] - step * direct
    is_last = iota((length, LANES), 0) == length - 1
    cum_grad = cum_grad + jnp.where(is_last, red_s[2 * length : 2 * length + 1, :], 0.0)
    upper = later.astype(F32)
    decay_grad = jnp.dot(upper, cum_grad, precision=HIGHEST, preferred_element_type=F32)
    step_grad = direct - par[1:2, :] * decay_grad
    pre_grad = step_grad / (1.0 + jnp.exp(-pre_s[...]))
    gp_s[:, 0:LANES] = jnp.concatenate([b_grad, c_grad], axis=1).astype(BF16)
    gp_s[:, LANES:] = pre_grad.astype(BF16)
    gproj = gp_s[...]

    for c in range(chunks):
        part = mm(f_ref[:, c * CHUNK : (c + 1) * CHUNK], gproj, TN)
        gw[c * CHUNK : (c + 1) * CHUNK, :] = part
        gw_out[c * CHUNK : (c + 1) * CHUNK, :] = part.astype(BF16)

    def r1_copy(k, owner):
        return pltpu.make_async_remote_copy(
            src_ref=gw_out.at[block(owner)], dst_ref=rb1.at[k],
            send_sem=r1_send.at[k], recv_sem=r1_recv.at[k],
            device_id=at_dp(sib), device_id_type=MESH,
        )

    def r2_copy(k, target):
        return pltpu.make_async_remote_copy(
            src_ref=s_out.at[k], dst_ref=rb2.at[k],
            send_sem=r2_send.at[k], recv_sem=r2_recv.at[k],
            device_id=at_dp(target), device_id_type=MESH,
        )

    order = list(range(1, half)) + [0]
    for k in order:
        r1_copy(k, lax.rem(sib + 2 * k, dp)).start()
    for k in order[:-1]:
        r1_copy(k, sib).wait_recv()
        s_out[k] = (gw[block(peer(k)), :] + rb1[k].astype(F32)).astype(BF16)
        r2_copy(k, peer(k)).start()

    for c in range(chunks):
        cs = slice(c * CHUNK, (c + 1) * CHUNK)
        ig_ref[:, cs] = mm(gproj, wall[cs, :], NT).astype(BF16)

    r1_copy(0, sib).wait_recv()
    total = gw[block(me), :] + rb1[0].astype(F32)
    for k in range(1, half):
        r2_copy(k, peer(k)).wait_recv()
        total = total + rb2[k].astype(F32)

    zout[...] = total.astype(zout.dtype)

    def z_piece(index):
        return pl.ds(pl.multiple_of(index * piece, 16), piece)

    def to_z(k):
        return lax.rem(z + k, seq)

    def from_z(k):
        return lax.rem(z + seq - k, seq)

    def zr_copy(k):
        return pltpu.make_async_remote_copy(
            src_ref=zout.at[z_piece(to_z(k))], dst_ref=zin.at[k],
            send_sem=zr_send.at[k], recv_sem=zr_recv.at[k],
            device_id=(me, to_z(k)), device_id_type=MESH,
        )

    def za_copy(k, owner):
        return pltpu.make_async_remote_copy(
            src_ref=final.at[z_piece(owner)], dst_ref=final.at[z_piece(owner)],
            send_sem=za_send.at[k], recv_sem=za_recv.at[k],
            device_id=(me, to_z(k)), device_id_type=MESH,
        )

    owner_here = z < owners
    for k in range(1, seq):
        @pl.when(to_z(k) < owners)
        def _():
            zr_copy(k).start()

    @pl.when(owner_here)
    def _():
        mine = zout[z_piece(z), :].astype(F32)
        for k in range(1, seq):
            zr_copy(k).wait_recv()
            mine = mine + zin[k].astype(F32)
        final[z_piece(z), :] = mine * scale
        for k in range(1, seq):
            za_copy(k, z).start()

    for k in range(1, seq):
        @pl.when(from_z(k) < owners)
        def _():
            za_copy(k, from_z(k)).wait_recv()

    bcg_ref[...] = final[:, 0:LANES]
    dtg_ref[...] = final[:, LANES : LANES + heads]

    ag_copy(0, me, sib).wait_send()
    for k in range(1, half):
        ag_copy(k, me, peer(k)).wait_send()
        fw_copy(k, source(k)).wait_send()
        r2_copy(k, peer(k)).wait_send()
    for k in range(half):
        r1_copy(k, sib).wait_send()
    for k in range(1, seq):
        @pl.when(to_z(k) < owners)
        def _():
            zr_copy(k).wait_send()

    @pl.when(owner_here)
    def _():
        for k in range(1, seq):
            za_copy(k, z).wait_send()

    for way, final_one in ((0, last), (1, 0)):
        @pl.when(z != final_one)
        def _():
            @pl.loop(0, chunks)
            def _(c):
                chain_copy(way, c).wait_send()


def body(dp, seq, features, head_inputs, out_grad, bc_weight, dt_weight, dt_bias, decay_rate, skip_gain):
    _, length, width = features.shape
    inner = head_inputs.shape[2]
    heads = dt_bias.shape[0]
    rows, both = bc_weight.shape
    state = both // 2
    half = dp // 2
    chunks = inner // CHUNK
    piece = -(-rows // (16 * seq)) * 16
    scale = 1.0 / math.sqrt(dp * seq * length)
    vmem, dma = pltpu.VMEM, pltpu.SemaphoreType.DMA
    square = vmem((length, LANES), F32)
    broad = vmem((length, inner), F32)
    states = vmem((chunks, state, CHUNK), F32)
    wire = vmem((chunks, state, CHUNK), BF16)
    narrow = vmem((length, state), F32)
    scratch = dict(
        wall=vmem((width, 2 * LANES), BF16), par=vmem((8, LANES), F32),
        pre_s=square, step_s=square, cum_s=square, cumt_s=square, ecum_s=square,
        toend_s=square, proj_s=square, bct_s=square, inter_s=square, rows_s=square,
        ig_acc=square,
        step_w=broad, ecum_w=broad, toend_w=broad, end_w=broad, wgrad=broad, sgrad=broad,
        left_s=states, right_s=states,
        fin=wire, bin_=wire, fout=wire, bout=wire,
        red_s=vmem((2 * length + 8, LANES), F32), bg_s=narrow, cg_s=narrow,
        gp_s=vmem((length, 2 * LANES), BF16),
        gw=vmem((width, 2 * LANES), F32), gw_out=vmem((width, 2 * LANES), BF16),
        rb1=vmem((half, rows, 2 * LANES), BF16), s_out=vmem((half, rows, 2 * LANES), BF16),
        rb2=vmem((half, rows, 2 * LANES), BF16),
        zout=vmem((rows, 2 * LANES), BF16), zin=vmem((seq, piece, 2 * LANES), BF16),
        final=vmem((rows, 2 * LANES), F32),
        ag_send=dma((half,)), ag_recv=dma((half,)), fw_send=dma((half,)), fw_recv=dma((half,)),
        ch_send=dma((2, chunks)), ch_recv=dma((2, chunks)),
        r1_send=dma((half,)), r1_recv=dma((half,)), r2_send=dma((half,)), r2_recv=dma((half,)),
        zr_send=dma((seq,)), zr_recv=dma((seq,)), za_send=dma((seq,)), za_recv=dma((seq,)),
    )
    whole = pl.BlockSpec(memory_space=pltpu.VMEM)
    results = pl.pallas_call(
        functools.partial(kernel, dp, seq, heads, scale),
        out_shape=(
            jax.ShapeDtypeStruct((length, width), BF16),
            jax.ShapeDtypeStruct((length, inner), BF16),
            jax.ShapeDtypeStruct((rows, both), F32),
            jax.ShapeDtypeStruct((rows, heads), F32),
        ),
        in_specs=[whole] * 8,
        out_specs=(whole,) * 4,
        scratch_shapes=scratch,
        compiler_params=pltpu.CompilerParams(
            collective_id=0, has_side_effects=True, vmem_limit_bytes=48 * 2**20
        ),
        name="mixer_backward",
    )(
        features[0], head_inputs[0], out_grad[0], bc_weight, dt_weight,
        dt_bias[None, :], decay_rate[None, :], skip_gain[None, :],
    )
    input_grad, head_grad, bc_grad, dt_grad = results
    return input_grad[None], head_grad[None], bc_grad, dt_grad


def solution(mesh):
    tokens = P("dp", "seq", None)
    return jax.shard_map(
        functools.partial(body, mesh.shape["dp"], mesh.shape["seq"]),
        mesh=mesh,
        in_specs=(tokens, tokens, tokens, P("dp", None), P("dp", None), P(), P(), P()),
        out_specs=(tokens, tokens, P("dp", None), P("dp", None)),
        check_vma=False,
    )
```

```python
import functools
import math

import jax
import jax.numpy as jnp
from jax import lax
from jax.experimental import pallas as pl
from jax.experimental.pallas import tpu as pltpu
from jax.sharding import PartitionSpec as P

MESH = pl.DeviceIdType.MESH
F32, BF16 = jnp.float32, jnp.bfloat16
LANES = 128
CHUNK = 512
HIGHEST = lax.Precision.HIGHEST
NT = (((1,), (1,)), ((), ()))
TN = (((0,), (0,)), ((), ()))


def halves(value):
    high = value.astype(BF16)
    return high, (value - high.astype(F32)).astype(BF16)


def mm(left, right, dims=None):
    if dims is None:
        return jnp.dot(left, right, preferred_element_type=F32)
    return lax.dot_general(left, right, dims, preferred_element_type=F32)


def iota(shape, dim):
    return lax.broadcasted_iota(jnp.int32, shape, dim)


def kernel(
    dp, seq, heads, scale,
    f_hbm, x_hbm, g_hbm, wbc_ref, wdt_ref, bias_ref, decay_ref, skip_ref,
    ig_ref, hg_ref, bcg_ref, dtg_ref, *,
    f_ref, x_ref, g_ref, in_sem, ft_s, m_s, cum_w,
    wall, par, pre_s, step_s, cum_s, cumt_s, ecum_s, toend_s, proj_s, bct_s, inter_s, rows_s,
    ig_acc, step_w, ecum_w, toend_w, end_w, wgrad, sgrad, left_s, right_s,
    fin, bin_, fout, bout, red_s, bg_s, cg_s, gp_s,
    gw, gw_out, rb1, s_out, rb2, zout, zin, final,
    ag_send, ag_recv, fw_send, fw_recv, ch_send, ch_recv,
    r1_send, r1_recv, r2_send, r2_recv, zr_send, zr_recv, za_send, za_recv,
):
    me, z = lax.axis_index("dp"), lax.axis_index("seq")
    last = seq - 1
    half = dp // 2
    sib = me + 1 - 2 * lax.rem(me, 2)
    length, inner = x_ref.shape
    width = f_ref.shape[1]
    rows = wbc_ref.shape[0]
    state = wbc_ref.shape[1] // 2
    head_size = inner // heads
    chunks = inner // CHUNK
    piece = -(-rows // (16 * seq)) * 16
    owners = -(-rows // piece)

    def at_dp(target):
        return (target, z)

    def peer(k):
        return lax.rem(me + 2 * k, dp)

    def source(k):
        return lax.rem(me + dp - 2 * k, dp)

    loads = [
        pltpu.make_async_copy(src, dst, in_sem.at[i])
        for i, (src, dst) in enumerate(((x_hbm, x_ref), (g_hbm, g_ref), (f_hbm, f_ref)))
    ]
    for load in loads:
        load.start()
    barrier = pltpu.get_barrier_semaphore()
    pl.semaphore_signal(barrier, inc=1, device_id=at_dp(sib), device_id_type=MESH)
    for k in range(1, half):
        pl.semaphore_signal(barrier, inc=1, device_id=at_dp(peer(k)), device_id_type=MESH)
    for k in range(1, seq):
        pl.semaphore_signal(barrier, inc=1, device_id=(me, lax.rem(z + k, seq)), device_id_type=MESH)

    def block(index):
        return pl.ds(pl.multiple_of(index * rows, 16), rows)

    wall[block(me), 0:LANES] = wbc_ref[...]
    padded = -(-rows // LANES) * LANES
    wide = jnp.concatenate(
        [wdt_ref[...].astype(F32), jnp.zeros((LANES - heads, rows), F32)], axis=0
    )
    if padded > rows:
        wide = jnp.concatenate([wide, jnp.zeros((LANES, padded - rows), F32)], axis=1)
    wall[block(me), LANES:] = wide.T[0:rows, :].astype(BF16)
    par[...] = jnp.zeros_like(par)
    par[0:1, 0:heads] = bias_ref[...]
    par[1:2, 0:heads] = decay_ref[...]
    par[2:3, 0:heads] = skip_ref[...]
    pl.semaphore_wait(barrier, half + seq - 1)

    def ag_copy(k, owner, target):
        return pltpu.make_async_remote_copy(
            src_ref=wall.at[block(owner)], dst_ref=wall.at[block(owner)],
            send_sem=ag_send.at[k], recv_sem=ag_recv.at[k],
            device_id=at_dp(target), device_id_type=MESH,
        )

    def fw_copy(k, owner):
        return pltpu.make_async_remote_copy(
            src_ref=wall.at[block(owner)], dst_ref=wall.at[block(owner)],
            send_sem=fw_send.at[k], recv_sem=fw_recv.at[k],
            device_id=at_dp(sib), device_id_type=MESH,
        )

    for k in range(1, half):
        ag_copy(k, me, peer(k)).start()
    ag_copy(0, me, sib).start()
    for load in loads:
        load.wait()

    low_half = iota((length, LANES), 1) < head_size
    per_tile = LANES // head_size
    tile_count = inner // LANES

    def early_work(tile):
        ts = pl.ds(pl.multiple_of(tile * LANES, LANES), LANES)
        x_tile, g_full = x_ref[:, ts].astype(F32), g_ref[:, ts]
        for part in range(per_tile):
            mine = low_half if part == 0 else jnp.logical_not(low_half)
            x_part = jnp.where(mine, x_tile, 0.0).astype(BF16)
            m_s[tile * per_tile + part] = mm(x_part, g_full, NT)

    @pl.loop(0, width // CHUNK)
    def _(c):
        cs = pl.ds(pl.multiple_of(c * CHUNK, CHUNK), CHUNK)
        ft_s[cs, :] = f_ref[:, cs].T

    for k in range(1, half):
        pl.loop(tile_count * (k - 1) // (half - 1), tile_count * k // (half - 1))(early_work)
        ag_copy(k, source(k), peer(k)).wait_recv()
        fw_copy(k, source(k)).start()
    ag_copy(0, sib, sib).wait_recv()
    for k in range(1, half):
        fw_copy(k, lax.rem(sib + dp - 2 * k, dp)).wait_recv()

    projection = mm(f_ref[...], wall[...])
    proj_s[...] = projection[:, :LANES]
    pre = projection[:, LANES:] + par[0:1, :]
    pre_s[...] = pre
    step = jnp.maximum(pre, 0.0) + jnp.log1p(jnp.exp(-jnp.abs(pre)))
    step_s[...] = step
    lower = (iota((length, length), 0) >= iota((length, length), 1)).astype(F32)
    cum = jnp.dot(
        lower, -par[1:2, :] * step, precision=HIGHEST, preferred_element_type=F32
    )
    cum_s[...] = cum
    cumt_s[...] = cum.T
    ecum_s[...] = jnp.exp(cum)
    toend_s[...] = jnp.exp(cum[length - 1 :, :] - cum)
    bct_s[...] = proj_s[...].T
    bt = bct_s[0:state, :]
    ct = bct_s[state:, :]
    bt_hi, bt_lo = halves(bt)
    ct_hi, ct_lo = halves(ct)
    bt3 = jnp.concatenate([bt_hi, bt_lo, bt_hi], axis=1)
    ct3 = jnp.concatenate([ct_hi, ct_lo, ct_hi], axis=1)
    b_rows = proj_s[:, 0:state]
    c_rows = proj_s[:, state:]
    inter_s[...] = jnp.dot(b_rows, ct, precision=HIGHEST, preferred_element_type=F32)

    def spread(value, c, exact=False):
        high, low = halves(value)
        row = iota((LANES, CHUNK), 0)
        hot = (row == c * (CHUNK // head_size) + iota((LANES, CHUNK), 1) // head_size)
        hot = hot.astype(F32).astype(BF16)
        result = mm(jnp.concatenate([high, low], axis=1), jnp.concatenate([hot, hot], axis=0))
        if exact:
            rest = value - high.astype(F32) - low.astype(F32)
            result = result + mm(rest.astype(BF16), hot)
        return result

    def lanes(c):
        return pl.ds(pl.multiple_of(c * CHUNK, CHUNK), CHUNK)

    def chain_copy(way, c):
        src, dst = ((fout, fin), (bout, bin_))[way]
        to = (z + 1, z + last)[way]
        return pltpu.make_async_remote_copy(
            src_ref=src.at[c], dst_ref=dst.at[c],
            send_sem=ch_send.at[way, c], recv_sem=ch_recv.at[way, c],
            device_id=(me, lax.rem(to, seq)), device_id_type=MESH,
        )

    @pl.loop(0, chunks)
    def _(c):
        cs = lanes(c)
        step_c = spread(step_s[...], c)
        ecum_c = spread(ecum_s[...], c)
        toend_c = spread(toend_s[...], c)
        ends = x_ref[:, cs].astype(F32) * step_c * toend_c
        weighted = g_ref[:, cs].astype(F32) * ecum_c
        step_w[:, cs] = step_c
        ecum_w[:, cs] = ecum_c
        toend_w[:, cs] = toend_c
        cum_w[:, cs] = spread(cum_s[...], c, exact=True)
        end_w[:, cs] = ends
        wgrad[:, cs] = weighted
        e_hi, e_lo = halves(ends)
        w_hi, w_lo = halves(weighted)
        left_s[c] = mm(bt3, jnp.concatenate([e_hi, e_hi, e_lo], axis=0))
        right_s[c] = mm(ct3, jnp.concatenate([w_hi, w_hi, w_lo], axis=0))

        for way, first in ((0, 0), (1, last)):
            @pl.when(z == first)
            def _():
                arrived, leaving, here = ((fin, fout, left_s), (bin_, bout, right_s))[way]
                arrived[c] = jnp.zeros((state, CHUNK), BF16)
                if seq > 1:
                    leaving[c] = here[c].astype(BF16)
                    chain_copy(way, c).start()

    def chain_hop(way, c):
        arrived, leaving, local = ((fin, fout, left_s), (bin_, bout, right_s))[way]
        chain_copy(way, c).wait_recv()

        @pl.when(z != (last, 0)[way])
        def _():
            decay = ecum_w[length - 1 :, lanes(c)]
            leaving[c] = (arrived[c].astype(F32) * decay + local[c]).astype(BF16)
            chain_copy(way, c).start()

    later = iota((length, length), 1) >= iota((length, length), 0)
    def by_head(tile):
        turned = pltpu.roll(tile, head_size, 1)
        return jnp.where(low_half, tile, turned), jnp.where(low_half, turned, tile)

    def tile_work(tile):
        ts = pl.ds(pl.multiple_of(tile * LANES, LANES), LANES)
        g_tile = g_ref[:, ts].astype(F32)
        inter = inter_s[...]
        cums, steps = by_head(cum_w[:, ts]), by_head(step_w[:, ts])
        mixes, grads, sums = [], [], []
        for part in range(per_tile):
            head = tile * per_tile + part
            gap = cumt_s[pl.ds(head, 1), :] - cums[part]
            weights = jnp.exp(jnp.where(later, gap, -1e30))
            mine = low_half if part == 0 else jnp.logical_not(low_half)
            g_part = jnp.where(mine, g_tile, 0.0).astype(BF16)
            shared = m_s[head] * steps[part] * weights
            sums.append(shared)
            rows_s[pl.ds(head, 1), :] = jnp.sum(shared * inter, axis=0, keepdims=True)
            mixes += list(halves(inter * weights))
            grads += [g_part, g_part]
        ig_acc[...] += sum(sums[1:], sums[0])
        sgrad[:, ts] = mm(jnp.concatenate(mixes, axis=1), jnp.concatenate(grads, axis=0))

    def reduce_heads(value, c):
        lane = iota((LANES, CHUNK), 0)
        hot = lane == c * (CHUNK // head_size) + iota((LANES, CHUNK), 1) // head_size
        hot = hot.astype(F32).astype(BF16)
        high, low = halves(value)
        return mm(jnp.concatenate([high, low], axis=1), jnp.concatenate([hot, hot], axis=1), NT)

    b_hi, b_lo = halves(b_rows)
    c_hi, c_lo = halves(c_rows)
    bpair = jnp.concatenate([b_hi, b_lo], axis=1)
    cpair = jnp.concatenate([c_hi, c_lo], axis=1)

    def carried_work(c):
        cs = lanes(c)
        state_in, state_grad = fin[c], bin_[c]
        weighted, ends = wgrad[:, cs], end_w[:, cs]
        inter_out = mm(cpair, jnp.concatenate([state_in, state_in], axis=0))
        reach = mm(bpair, jnp.concatenate([state_grad, state_grad], axis=0))
        w_hi, w_lo = halves(weighted)
        e_hi, e_lo = halves(ends)
        cg_s[...] += mm(w_hi, state_in, NT) + mm(w_lo, state_in, NT)
        bg_s[...] += mm(e_hi, state_grad, NT) + mm(e_lo, state_grad, NT)
        total = sgrad[:, cs] + toend_w[:, cs] * reach
        x_part, g_part = x_ref[:, cs].astype(F32), g_ref[:, cs].astype(F32)
        decay = ecum_w[length - 1 :, cs]
        product = state_grad.astype(F32) * state_in.astype(F32)
        at_end = jnp.sum(ends * reach, axis=0, keepdims=True) + decay * jnp.sum(
            product, axis=0, keepdims=True
        )
        stacked = jnp.concatenate(
            [weighted * inter_out, x_part * total, jnp.broadcast_to(at_end, (8, CHUNK))], axis=0
        )
        red_s[...] += reduce_heads(stacked, c)
        skip_c = spread(jnp.broadcast_to(par[2:3, :], (8, LANES)), c)[0:1, :]
        hg_ref[:, cs] = (g_part * skip_c + step_w[:, cs] * total).astype(BF16)

    ig_acc[...] = jnp.zeros_like(ig_acc)
    rows_s[...] = jnp.zeros_like(rows_s)
    cg_s[...] = jnp.zeros_like(cg_s)
    bg_s[...] = jnp.zeros_like(bg_s)
    red_s[...] = jnp.zeros_like(red_s)
    tiles = CHUNK // LANES

    early = tiles // 2

    @pl.loop(0, chunks + max(last - 1, 0))
    def _(s):
        forward, back = s - (z - 1), s - (last - 1 - z)

        @pl.when(s < chunks)
        def _():
            for tile in range(early):
                tile_work(s * tiles + tile)

        if seq > 1:
            @pl.when(jnp.logical_and(z > 0, jnp.logical_and(forward >= 0, forward < chunks)))
            def _():
                chain_hop(0, forward)

            @pl.when(jnp.logical_and(z < last, jnp.logical_and(back >= 0, back < chunks)))
            def _():
                chain_hop(1, back)

        @pl.when(s < chunks)
        def _():
            for tile in range(early, tiles):
                tile_work(s * tiles + tile)

        both = s - jnp.maximum(z, last - z) + min(last, 1)

        @pl.when(jnp.logical_and(both >= 0, both < chunks))
        def _():
            carried_work(both)

    acc = ig_acc[...]
    c_grad = cg_s[...] + lax.dot_general(
        acc, b_rows, TN, precision=HIGHEST, preferred_element_type=F32
    )
    b_grad = bg_s[...] + jnp.dot(acc, c_rows, precision=HIGHEST, preferred_element_type=F32)
    step = step_s[...]
    direct = red_s[length : 2 * length, :]
    cum_grad = rows_s[...].T + red_s[0:length, :] - step * direct
    is_last = iota((length, LANES), 0) == length - 1
    cum_grad = cum_grad + jnp.where(is_last, red_s[2 * length : 2 * length + 1, :], 0.0)
    upper = later.astype(F32)
    decay_grad = jnp.dot(upper, cum_grad, precision=HIGHEST, preferred_element_type=F32)
    step_grad = direct - par[1:2, :] * decay_grad
    pre_grad = step_grad / (1.0 + jnp.exp(-pre_s[...]))
    gp_s[:, 0:LANES] = jnp.concatenate([b_grad, c_grad], axis=1).astype(BF16)
    gp_s[:, LANES:] = pre_grad.astype(BF16)
    gproj = gp_s[...]

    @pl.loop(0, width // CHUNK)
    def _(c):
        cs = pl.ds(pl.multiple_of(c * CHUNK, CHUNK), CHUNK)
        part = mm(ft_s[cs, :], gproj)
        gw[cs, :] = part
        gw_out[cs, :] = part.astype(BF16)

    def r1_copy(k, owner):
        return pltpu.make_async_remote_copy(
            src_ref=gw_out.at[block(owner)], dst_ref=rb1.at[k],
            send_sem=r1_send.at[k], recv_sem=r1_recv.at[k],
            device_id=at_dp(sib), device_id_type=MESH,
        )

    def r2_copy(k, target):
        return pltpu.make_async_remote_copy(
            src_ref=s_out.at[k], dst_ref=rb2.at[k],
            send_sem=r2_send.at[k], recv_sem=r2_recv.at[k],
            device_id=at_dp(target), device_id_type=MESH,
        )

    order = list(range(1, half)) + [0]
    for k in order:
        r1_copy(k, lax.rem(sib + 2 * k, dp)).start()
    for k in order[:-1]:
        r1_copy(k, sib).wait_recv()
        s_out[k] = (gw[block(peer(k)), :] + rb1[k].astype(F32)).astype(BF16)
        r2_copy(k, peer(k)).start()

    for c in range(width // CHUNK):
        cs = slice(c * CHUNK, (c + 1) * CHUNK)
        ig_ref[:, cs] = mm(gproj, wall[cs, :], NT).astype(BF16)

    r1_copy(0, sib).wait_recv()
    total = gw[block(me), :] + rb1[0].astype(F32)
    for k in range(1, half):
        r2_copy(k, peer(k)).wait_recv()
        total = total + rb2[k].astype(F32)

    zout[...] = total.astype(zout.dtype)

    def z_piece(index):
        return pl.ds(pl.multiple_of(index * piece, 16), piece)

    def to_z(k):
        return lax.rem(z + k, seq)

    def from_z(k):
        return lax.rem(z + seq - k, seq)

    def zr_copy(k):
        return pltpu.make_async_remote_copy(
            src_ref=zout.at[z_piece(to_z(k))], dst_ref=zin.at[k],
            send_sem=zr_send.at[k], recv_sem=zr_recv.at[k],
            device_id=(me, to_z(k)), device_id_type=MESH,
        )

    def za_copy(k, owner):
        return pltpu.make_async_remote_copy(
            src_ref=final.at[z_piece(owner)], dst_ref=final.at[z_piece(owner)],
            send_sem=za_send.at[k], recv_sem=za_recv.at[k],
            device_id=(me, to_z(k)), device_id_type=MESH,
        )

    owner_here = z < owners
    for k in range(1, seq):
        @pl.when(to_z(k) < owners)
        def _():
            zr_copy(k).start()

    @pl.when(owner_here)
    def _():
        mine = zout[z_piece(z), :].astype(F32)
        for k in range(1, seq):
            zr_copy(k).wait_recv()
            mine = mine + zin[k].astype(F32)
        final[z_piece(z), :] = (mine * scale).astype(BF16)
        for k in range(1, seq):
            za_copy(k, z).start()

    for k in range(1, seq):
        @pl.when(from_z(k) < owners)
        def _():
            za_copy(k, from_z(k)).wait_recv()

    bcg_ref[...] = final[:, 0:LANES].astype(F32)
    tail = final[:, LANES:].astype(F32)
    if padded > rows:
        tail = jnp.concatenate([tail, jnp.zeros((padded - rows, LANES), F32)], axis=0)
    dtg_ref[...] = tail.T[0:heads, 0:rows]

    ag_copy(0, me, sib).wait_send()
    for k in range(1, half):
        ag_copy(k, me, peer(k)).wait_send()
        fw_copy(k, source(k)).wait_send()
        r2_copy(k, peer(k)).wait_send()
    for k in range(half):
        r1_copy(k, sib).wait_send()
    for k in range(1, seq):
        @pl.when(to_z(k) < owners)
        def _():
            zr_copy(k).wait_send()

    @pl.when(owner_here)
    def _():
        for k in range(1, seq):
            za_copy(k, z).wait_send()

    for way, final_one in ((0, last), (1, 0)):
        @pl.when(z != final_one)
        def _():
            @pl.loop(0, chunks)
            def _(c):
                chain_copy(way, c).wait_send()


def body(dp, seq, features, head_inputs, out_grad, bc_weight, dt_weight, dt_bias, decay_rate, skip_gain):
    _, length, width = features.shape
    inner = head_inputs.shape[2]
    heads = dt_bias.shape[0]
    rows, both = bc_weight.shape
    state = both // 2
    half = dp // 2
    chunks = inner // CHUNK
    piece = -(-rows // (16 * seq)) * 16
    scale = 1.0 / math.sqrt(dp * seq * length)
    vmem, dma = pltpu.VMEM, pltpu.SemaphoreType.DMA
    square = vmem((length, LANES), F32)
    broad = vmem((length, inner), F32)
    states = vmem((chunks, state, CHUNK), F32)
    wire = vmem((chunks, state, CHUNK), BF16)
    narrow = vmem((length, state), F32)
    scratch = dict(
        f_ref=vmem((length, width), BF16), x_ref=vmem((length, inner), BF16),
        g_ref=vmem((length, inner), BF16), in_sem=dma((3,)),
        ft_s=vmem((width, length), BF16), m_s=vmem((heads, length, length), F32),
        cum_w=broad,
        wall=vmem((width, 2 * LANES), BF16), par=vmem((8, LANES), F32),
        pre_s=square, step_s=square, cum_s=square, cumt_s=square, ecum_s=square,
        toend_s=square, proj_s=square, bct_s=square, inter_s=square, rows_s=square,
        ig_acc=square,
        step_w=broad, ecum_w=broad, toend_w=broad, end_w=broad, wgrad=broad, sgrad=broad,
        left_s=states, right_s=states,
        fin=wire, bin_=wire, fout=wire, bout=wire,
        red_s=vmem((2 * length + 8, LANES), F32), bg_s=narrow, cg_s=narrow,
        gp_s=vmem((length, 2 * LANES), BF16),
        gw=vmem((width, 2 * LANES), F32), gw_out=vmem((width, 2 * LANES), BF16),
        rb1=vmem((half, rows, 2 * LANES), BF16), s_out=vmem((half, rows, 2 * LANES), BF16),
        rb2=vmem((half, rows, 2 * LANES), BF16),
        zout=vmem((rows, 2 * LANES), BF16), zin=vmem((seq, piece, 2 * LANES), BF16),
        final=vmem((rows, 2 * LANES), BF16),
        ag_send=dma((half,)), ag_recv=dma((half,)), fw_send=dma((half,)), fw_recv=dma((half,)),
        ch_send=dma((2, chunks)), ch_recv=dma((2, chunks)),
        r1_send=dma((half,)), r1_recv=dma((half,)), r2_send=dma((half,)), r2_recv=dma((half,)),
        zr_send=dma((seq,)), zr_recv=dma((seq,)), za_send=dma((seq,)), za_recv=dma((seq,)),
    )
    whole = pl.BlockSpec(memory_space=pltpu.VMEM)
    results = pl.pallas_call(
        functools.partial(kernel, dp, seq, heads, scale),
        out_shape=(
            jax.ShapeDtypeStruct((length, width), BF16),
            jax.ShapeDtypeStruct((length, inner), BF16),
            jax.ShapeDtypeStruct((rows, both), F32),
            jax.ShapeDtypeStruct((heads, rows), F32),
        ),
        in_specs=[pl.BlockSpec(memory_space=pltpu.HBM)] * 3 + [whole] * 5,
        out_specs=(whole,) * 4,
        scratch_shapes=scratch,
        compiler_params=pltpu.CompilerParams(
            collective_id=0, has_side_effects=True, vmem_limit_bytes=56 * 2**20
        ),
        name="mixer_backward",
    )(
        features[0], head_inputs[0], out_grad[0], bc_weight, dt_weight.T,
        dt_bias[None, :], decay_rate[None, :], skip_gain[None, :],
    )
    input_grad, head_grad, bc_grad, dt_grad = results
    return input_grad[None], head_grad[None], bc_grad, dt_grad.T


def solution(mesh):
    tokens = P("dp", "seq", None)
    return jax.shard_map(
        functools.partial(body, mesh.shape["dp"], mesh.shape["seq"]),
        mesh=mesh,
        in_specs=(tokens, tokens, tokens, P("dp", None), P("dp", None), P(), P(), P()),
        out_specs=(tokens, tokens, P("dp", None), P("dp", None)),
        check_vma=False,
    )
```

```python
import functools
import math

import jax
import jax.numpy as jnp
from jax import lax
from jax.experimental import pallas as pl
from jax.experimental.pallas import tpu as pltpu
from jax.sharding import PartitionSpec as P

MESH = pl.DeviceIdType.MESH
F32, BF16 = jnp.float32, jnp.bfloat16
LANES = 128
CHUNK = 512
HIGHEST = lax.Precision.HIGHEST
NT = (((1,), (1,)), ((), ()))
TN = (((0,), (0,)), ((), ()))


def halves(value):
    high = value.astype(BF16)
    return high, (value - high.astype(F32)).astype(BF16)


def mm(left, right, dims=None):
    if dims is None:
        return jnp.dot(left, right, preferred_element_type=F32)
    return lax.dot_general(left, right, dims, preferred_element_type=F32)


def iota(shape, dim):
    return lax.broadcasted_iota(jnp.int32, shape, dim)


def kernel(
    dp, seq, heads, scale,
    f_hbm, x_hbm, g_hbm, wbc_ref, wdt_ref, bias_ref, decay_ref, skip_ref,
    ig_hbm, hg_hbm, bcg_ref, dtg_ref, *,
    ig_ref, hg_ref, out_sem,
    f_ref, x_ref, g_ref, in_sem, ft_s, m_s, cum_w, hot_s, wpack, ftin, gpin, fa_send, fa_recv,
    wall, par, pre_s, step_s, cum_s, cumt_s, ecum_s, toend_s, proj_s, bct_s, inter_s, rows_s,
    ig_acc, step_w, ecum_w, toend_w, end_w, wgrad, sgrad, left_s, right_s,
    fin, bin_, fout, bout, red_s, bg_s, cg_s,
    zout, zin, final,
    ag_send, ag_recv, fw_send, fw_recv, ch_send, ch_recv,
    gp_send, gp_recv, gf_send, gf_recv, zr_send, zr_recv, za_send, za_recv,
):
    me, z = lax.axis_index("dp"), lax.axis_index("seq")
    last = seq - 1
    half = dp // 2
    sib = me + 1 - 2 * lax.rem(me, 2)
    length, inner = x_ref.shape
    width = f_ref.shape[1]
    rows = wbc_ref.shape[0]
    state = wbc_ref.shape[1] // 2
    head_size = inner // heads
    chunks = inner // CHUNK
    groups = LANES // heads
    share = -(-rows // (16 * groups)) * 16
    packed = rows + share
    piece = -(-packed // (16 * seq)) * 16
    owners = -(-packed // piece)

    def pack(value):
        parts = []
        for g in range(groups):
            part = value[g * share : min((g + 1) * share, rows), :]
            if part.shape[0] < share:
                empty = jnp.zeros((share - part.shape[0], LANES), F32)
                part = jnp.concatenate([part, empty], axis=0)
            parts.append(pltpu.roll(part, g * heads, 1) if g else part)
        return sum(parts[1:], parts[0])

    def unpack(value):
        parts = []
        for g in range(groups):
            part = pltpu.roll(value, LANES - g * heads, 1) if g else value
            parts.append(part[0 : min(share, rows - g * share), :])
        return jnp.concatenate(parts, axis=0)

    def at_dp(target):
        return (target, z)

    def peer(k):
        return lax.rem(me + 2 * k, dp)

    def source(k):
        return lax.rem(me + dp - 2 * k, dp)

    loads = [
        pltpu.make_async_copy(src, dst, in_sem.at[i])
        for i, (src, dst) in enumerate(((x_hbm, x_ref), (g_hbm, g_ref), (f_hbm, f_ref)))
    ]
    for load in loads:
        load.start()
    barrier = pltpu.get_barrier_semaphore()
    for k in range(1, dp):
        pl.semaphore_signal(
            barrier, inc=1, device_id=at_dp(lax.rem(me + k, dp)), device_id_type=MESH
        )
    for k in range(1, seq):
        pl.semaphore_signal(barrier, inc=1, device_id=(me, lax.rem(z + k, seq)), device_id_type=MESH)

    def block(index):
        return pl.ds(pl.multiple_of(index * rows, 16), rows)

    wpack[me, 0:rows, :] = wbc_ref[...]
    padded = -(-rows // LANES) * LANES
    wide = jnp.concatenate(
        [wdt_ref[...].astype(F32), jnp.zeros((LANES - heads, rows), F32)], axis=0
    )
    if padded > rows:
        wide = jnp.concatenate([wide, jnp.zeros((LANES, padded - rows), F32)], axis=1)
    wpack[me, rows:, :] = pack(wide.T[0:rows, :]).astype(BF16)
    par[...] = jnp.zeros_like(par)
    par[0:1, 0:heads] = bias_ref[...]
    par[1:2, 0:heads] = decay_ref[...]
    par[2:3, 0:heads] = skip_ref[...]
    pl.semaphore_wait(barrier, dp + seq - 2)

    def ag_copy(k, owner, target):
        return pltpu.make_async_remote_copy(
            src_ref=wpack.at[owner], dst_ref=wpack.at[owner],
            send_sem=ag_send.at[k], recv_sem=ag_recv.at[k],
            device_id=at_dp(target), device_id_type=MESH,
        )

    def fw_copy(k, owner):
        return pltpu.make_async_remote_copy(
            src_ref=wpack.at[owner], dst_ref=wpack.at[owner],
            send_sem=fw_send.at[k], recv_sem=fw_recv.at[k],
            device_id=at_dp(sib), device_id_type=MESH,
        )

    for k in range(1, half):
        ag_copy(k, me, peer(k)).start()
    ag_copy(0, me, sib).start()
    for load in loads:
        load.wait()

    low_half = iota((length, LANES), 1) < head_size
    per_tile = LANES // head_size
    tile_count = inner // LANES

    def early_work(tile):
        ts = pl.ds(pl.multiple_of(tile * LANES, LANES), LANES)
        x_tile, g_full = x_ref[:, ts].astype(F32), g_ref[:, ts]
        for part in range(per_tile):
            mine = low_half if part == 0 else jnp.logical_not(low_half)
            x_part = jnp.where(mine, x_tile, 0.0).astype(BF16)
            m_s[tile * per_tile + part] = mm(x_part, g_full, NT)

    @pl.loop(0, width // CHUNK)
    def _(c):
        cs = pl.ds(pl.multiple_of(c * CHUNK, CHUNK), CHUNK)
        ft_s[cs, :] = f_ref[:, cs].T

    @pl.loop(0, chunks)
    def _(c):
        lane = c * CHUNK + iota((LANES, CHUNK), 1)
        hot = (iota((LANES, CHUNK), 0) == lane // head_size).astype(F32).astype(BF16)
        hot_s[c, 0:LANES, :] = hot
        hot_s[c, LANES:, :] = hot

    for k in range(1, half):
        pl.loop(tile_count * (k - 1) // (half - 1), tile_count * k // (half - 1))(early_work)
        ag_copy(k, source(k), peer(k)).wait_recv()
        fw_copy(k, source(k)).start()
    ag_copy(0, sib, sib).wait_recv()
    for k in range(1, half):
        fw_copy(k, lax.rem(sib + dp - 2 * k, dp)).wait_recv()

    def fa_copy(k):
        target = lax.rem(me + k, dp)
        return pltpu.make_async_remote_copy(
            src_ref=ft_s.at[block(target)], dst_ref=ftin.at[me],
            send_sem=fa_send.at[k], recv_sem=fa_recv.at[k],
            device_id=at_dp(target), device_id_type=MESH,
        )

    for k in range(1, dp):
        fa_copy(k).start()
    ftin[me] = ft_s[block(me), :]

    @pl.loop(0, dp)
    def _(i):
        wall[block(i), 0:LANES] = wpack[i, 0:rows, :]
        wall[block(i), LANES:] = unpack(wpack[i, rows:, :].astype(F32)).astype(BF16)

    projection = mm(f_ref[...], wall[...])
    proj_s[...] = projection[:, :LANES]
    pre = projection[:, LANES:] + par[0:1, :]
    pre_s[...] = pre
    step = jnp.maximum(pre, 0.0) + jnp.log1p(jnp.exp(-jnp.abs(pre)))
    step_s[...] = step
    lower = (iota((length, length), 0) >= iota((length, length), 1)).astype(F32)
    cum = jnp.dot(
        lower, -par[1:2, :] * step, precision=HIGHEST, preferred_element_type=F32
    )
    cum_s[...] = cum
    cumt_s[...] = cum.T
    ecum_s[...] = jnp.exp(cum)
    toend_s[...] = jnp.exp(cum[length - 1 :, :] - cum)
    bct_s[...] = proj_s[...].T
    bt = bct_s[0:state, :]
    ct = bct_s[state:, :]
    bt_hi, bt_lo = halves(bt)
    ct_hi, ct_lo = halves(ct)
    bt3 = jnp.concatenate([bt_hi, bt_lo, bt_hi], axis=1)
    ct3 = jnp.concatenate([ct_hi, ct_lo, ct_hi], axis=1)
    b_rows = proj_s[:, 0:state]
    c_rows = proj_s[:, state:]
    inter_s[...] = jnp.dot(b_rows, ct, precision=HIGHEST, preferred_element_type=F32)

    def spread(value, c, exact=False):
        high, low = halves(value)
        result = mm(jnp.concatenate([high, low], axis=1), hot_s[c])
        if exact:
            rest = value - high.astype(F32) - low.astype(F32)
            result = result + mm(rest.astype(BF16), hot_s[c, 0:LANES, :])
        return result

    def lanes(c):
        return pl.ds(pl.multiple_of(c * CHUNK, CHUNK), CHUNK)

    def chain_copy(way, c):
        src, dst = ((fout, fin), (bout, bin_))[way]
        to = (z + 1, z + last)[way]
        return pltpu.make_async_remote_copy(
            src_ref=src.at[c], dst_ref=dst.at[c],
            send_sem=ch_send.at[way, c], recv_sem=ch_recv.at[way, c],
            device_id=(me, lax.rem(to, seq)), device_id_type=MESH,
        )

    @pl.loop(0, chunks)
    def _(c):
        cs = lanes(c)
        step_c = spread(step_s[...], c)
        ecum_c = spread(ecum_s[...], c)
        toend_c = spread(toend_s[...], c)
        ends = x_ref[:, cs].astype(F32) * step_c * toend_c
        weighted = g_ref[:, cs].astype(F32) * ecum_c
        step_w[:, cs] = step_c
        ecum_w[:, cs] = ecum_c
        toend_w[:, cs] = toend_c
        cum_w[:, cs] = spread(cum_s[...], c, exact=True)
        end_w[:, cs] = ends
        wgrad[:, cs] = weighted
        e_hi, e_lo = halves(ends)
        w_hi, w_lo = halves(weighted)
        left_s[c] = mm(bt3, jnp.concatenate([e_hi, e_hi, e_lo], axis=0))
        right_s[c] = mm(ct3, jnp.concatenate([w_hi, w_hi, w_lo], axis=0))

        for way, first in ((0, 0), (1, last)):
            @pl.when(z == first)
            def _():
                arrived, leaving, here = ((fin, fout, left_s), (bin_, bout, right_s))[way]
                arrived[c] = jnp.zeros((state, CHUNK), BF16)
                if seq > 1:
                    leaving[c] = here[c].astype(BF16)
                    chain_copy(way, c).start()

    def chain_hop(way, c):
        arrived, leaving, local = ((fin, fout, left_s), (bin_, bout, right_s))[way]
        chain_copy(way, c).wait_recv()

        @pl.when(z != (last, 0)[way])
        def _():
            decay = ecum_w[length - 1 :, lanes(c)]
            leaving[c] = (arrived[c].astype(F32) * decay + local[c]).astype(BF16)
            chain_copy(way, c).start()

    later = iota((length, length), 1) >= iota((length, length), 0)
    def by_head(tile):
        turned = pltpu.roll(tile, head_size, 1)
        return jnp.where(low_half, tile, turned), jnp.where(low_half, turned, tile)

    def tile_work(tile):
        ts = pl.ds(pl.multiple_of(tile * LANES, LANES), LANES)
        g_tile = g_ref[:, ts].astype(F32)
        inter = inter_s[...]
        cums, steps = by_head(cum_w[:, ts]), by_head(step_w[:, ts])
        mixes, grads, sums = [], [], []
        for part in range(per_tile):
            head = tile * per_tile + part
            gap = cumt_s[pl.ds(head, 1), :] - cums[part]
            weights = jnp.exp(jnp.where(later, gap, -1e30))
            mine = low_half if part == 0 else jnp.logical_not(low_half)
            g_part = jnp.where(mine, g_tile, 0.0).astype(BF16)
            shared = m_s[head] * steps[part] * weights
            sums.append(shared)
            rows_s[pl.ds(head, 1), :] = jnp.sum(shared * inter, axis=0, keepdims=True)
            mixes += list(halves(inter * weights))
            grads += [g_part, g_part]
        ig_acc[...] += sum(sums[1:], sums[0])
        sgrad[:, ts] = mm(jnp.concatenate(mixes, axis=1), jnp.concatenate(grads, axis=0))

    def reduce_heads(value, c):
        hot = hot_s[c, 0:LANES, :]
        high, low = halves(value)
        return mm(high, hot, NT) + mm(low, hot, NT)

    b_hi, b_lo = halves(b_rows)
    c_hi, c_lo = halves(c_rows)
    bpair = jnp.concatenate([b_hi, b_lo], axis=1)
    cpair = jnp.concatenate([c_hi, c_lo], axis=1)

    def carried_work(c):
        cs = lanes(c)
        state_in, state_grad = fin[c], bin_[c]
        weighted, ends = wgrad[:, cs], end_w[:, cs]
        inter_out = mm(cpair, jnp.concatenate([state_in, state_in], axis=0))
        reach = mm(bpair, jnp.concatenate([state_grad, state_grad], axis=0))
        w_hi, w_lo = halves(weighted)
        e_hi, e_lo = halves(ends)
        cg_s[...] += mm(w_hi, state_in, NT) + mm(w_lo, state_in, NT)
        bg_s[...] += mm(e_hi, state_grad, NT) + mm(e_lo, state_grad, NT)
        total = sgrad[:, cs] + toend_w[:, cs] * reach
        x_part, g_part = x_ref[:, cs].astype(F32), g_ref[:, cs].astype(F32)
        decay = ecum_w[length - 1 :, cs]
        product = state_grad.astype(F32) * state_in.astype(F32)
        at_end = jnp.sum(ends * reach, axis=0, keepdims=True) + decay * jnp.sum(
            product, axis=0, keepdims=True
        )
        stacked = jnp.concatenate(
            [weighted * inter_out, x_part * total, jnp.broadcast_to(at_end, (8, CHUNK))], axis=0
        )
        red_s[...] += reduce_heads(stacked, c)
        skip_c = spread(jnp.broadcast_to(par[2:3, :], (8, LANES)), c)[0:1, :]
        hg_ref[:, cs] = (g_part * skip_c + step_w[:, cs] * total).astype(BF16)

    ig_acc[...] = jnp.zeros_like(ig_acc)
    rows_s[...] = jnp.zeros_like(rows_s)
    cg_s[...] = jnp.zeros_like(cg_s)
    bg_s[...] = jnp.zeros_like(bg_s)
    red_s[...] = jnp.zeros_like(red_s)
    tiles = CHUNK // LANES

    early = tiles // 2

    @pl.loop(0, chunks + max(last - 1, 0))
    def _(s):
        forward, back = s - (z - 1), s - (last - 1 - z)

        @pl.when(s < chunks)
        def _():
            for tile in range(early):
                tile_work(s * tiles + tile)

        if seq > 1:
            @pl.when(jnp.logical_and(z > 0, jnp.logical_and(forward >= 0, forward < chunks)))
            def _():
                chain_hop(0, forward)

            @pl.when(jnp.logical_and(z < last, jnp.logical_and(back >= 0, back < chunks)))
            def _():
                chain_hop(1, back)

        @pl.when(s < chunks)
        def _():
            for tile in range(early, tiles):
                tile_work(s * tiles + tile)

        both = s - jnp.maximum(z, last - z) + min(last, 1)

        @pl.when(jnp.logical_and(both >= 0, both < chunks))
        def _():
            carried_work(both)

    store_hg = pltpu.make_async_copy(hg_ref, hg_hbm, out_sem.at[0])
    store_hg.start()
    acc = ig_acc[...]
    c_grad = cg_s[...] + lax.dot_general(
        acc, b_rows, TN, precision=HIGHEST, preferred_element_type=F32
    )
    b_grad = bg_s[...] + jnp.dot(acc, c_rows, precision=HIGHEST, preferred_element_type=F32)
    step = step_s[...]
    direct = red_s[length : 2 * length, :]
    cum_grad = rows_s[...].T + red_s[0:length, :] - step * direct
    is_last = iota((length, LANES), 0) == length - 1
    cum_grad = cum_grad + jnp.where(is_last, red_s[2 * length : 2 * length + 1, :], 0.0)
    upper = later.astype(F32)
    decay_grad = jnp.dot(upper, cum_grad, precision=HIGHEST, preferred_element_type=F32)
    step_grad = direct - par[1:2, :] * decay_grad
    pre_grad = step_grad / (1.0 + jnp.exp(-pre_s[...]))
    gpin[me, :, 0:LANES] = jnp.concatenate([b_grad, c_grad], axis=1).astype(BF16)
    gpin[me, :, LANES:] = pre_grad.astype(BF16)

    def gp_copy(k, owner, target):
        return pltpu.make_async_remote_copy(
            src_ref=gpin.at[owner], dst_ref=gpin.at[owner],
            send_sem=gp_send.at[k], recv_sem=gp_recv.at[k],
            device_id=at_dp(target), device_id_type=MESH,
        )

    def gf_copy(k, owner):
        return pltpu.make_async_remote_copy(
            src_ref=gpin.at[owner], dst_ref=gpin.at[owner],
            send_sem=gf_send.at[k], recv_sem=gf_recv.at[k],
            device_id=at_dp(sib), device_id_type=MESH,
        )

    for k in range(1, half):
        gp_copy(k, me, peer(k)).start()
    gp_copy(0, me, sib).start()

    gproj = gpin[me]
    for c in range(width // CHUNK):
        cs = slice(c * CHUNK, (c + 1) * CHUNK)
        ig_ref[:, cs] = mm(gproj, wall[cs, :], NT).astype(BF16)
    store_ig = pltpu.make_async_copy(ig_ref, ig_hbm, out_sem.at[1])
    store_ig.start()

    for k in range(1, dp):
        fa_copy(k).wait_recv()

    def gradient_of(index):
        return mm(ftin[index], gpin[index])

    total = gradient_of(me)
    gp_copy(0, sib, sib).wait_recv()
    total = total + gradient_of(sib)
    for k in range(1, half):
        gp_copy(k, source(k), peer(k)).wait_recv()
        gf_copy(k, source(k)).start()
        total = total + gradient_of(source(k))
    for k in range(1, half):
        other = lax.rem(sib + dp - 2 * k, dp)
        gf_copy(k, other).wait_recv()
        total = total + gradient_of(other)

    zout[0:rows, :] = total[:, 0:LANES].astype(BF16)
    zout[rows:packed, :] = pack(total[:, LANES:]).astype(BF16)
    if owners * piece > packed:
        zout[packed:, :] = jnp.zeros((owners * piece - packed, LANES), BF16)

    def z_piece(index):
        return pl.ds(pl.multiple_of(index * piece, 16), piece)

    def to_z(k):
        return lax.rem(z + k, seq)

    def from_z(k):
        return lax.rem(z + seq - k, seq)

    def zr_copy(k):
        return pltpu.make_async_remote_copy(
            src_ref=zout.at[z_piece(to_z(k))], dst_ref=zin.at[k],
            send_sem=zr_send.at[k], recv_sem=zr_recv.at[k],
            device_id=(me, to_z(k)), device_id_type=MESH,
        )

    def za_copy(k, owner):
        return pltpu.make_async_remote_copy(
            src_ref=final.at[z_piece(owner)], dst_ref=final.at[z_piece(owner)],
            send_sem=za_send.at[k], recv_sem=za_recv.at[k],
            device_id=(me, to_z(k)), device_id_type=MESH,
        )

    owner_here = z < owners
    for k in range(1, seq):
        @pl.when(to_z(k) < owners)
        def _():
            zr_copy(k).start()

    @pl.when(owner_here)
    def _():
        mine = zout[z_piece(z), :].astype(F32)
        for k in range(1, seq):
            zr_copy(k).wait_recv()
            mine = mine + zin[k].astype(F32)
        final[z_piece(z), :] = (mine * scale).astype(BF16)
        for k in range(1, seq):
            za_copy(k, z).start()

    for k in range(1, seq):
        @pl.when(from_z(k) < owners)
        def _():
            za_copy(k, from_z(k)).wait_recv()

    bcg_ref[...] = final[0:rows, :].astype(F32)
    tail = unpack(final[rows:packed, :].astype(F32))
    if padded > rows:
        tail = jnp.concatenate([tail, jnp.zeros((padded - rows, LANES), F32)], axis=0)
    dtg_ref[...] = tail.T[0:heads, 0:rows]

    store_hg.wait()
    store_ig.wait()
    ag_copy(0, me, sib).wait_send()
    for k in range(1, half):
        ag_copy(k, me, peer(k)).wait_send()
        fw_copy(k, source(k)).wait_send()
        gp_copy(k, me, peer(k)).wait_send()
        gf_copy(k, source(k)).wait_send()
    gp_copy(0, me, sib).wait_send()
    for k in range(1, dp):
        fa_copy(k).wait_send()
    for k in range(1, seq):
        @pl.when(to_z(k) < owners)
        def _():
            zr_copy(k).wait_send()

    @pl.when(owner_here)
    def _():
        for k in range(1, seq):
            za_copy(k, z).wait_send()

    for way, final_one in ((0, last), (1, 0)):
        @pl.when(z != final_one)
        def _():
            @pl.loop(0, chunks)
            def _(c):
                chain_copy(way, c).wait_send()


def place(*refs):
    sem = refs[8]
    copies = [pltpu.make_async_copy(refs[i], refs[i + 4], sem.at[i]) for i in range(4)]
    for copy in copies:
        copy.start()
    for copy in copies:
        copy.wait()


def body(dp, seq, features, head_inputs, out_grad, bc_weight, dt_weight, dt_bias, decay_rate, skip_gain):
    _, length, width = features.shape
    inner = head_inputs.shape[2]
    heads = dt_bias.shape[0]
    rows, both = bc_weight.shape
    state = both // 2
    half = dp // 2
    chunks = inner // CHUNK
    share = -(-rows // (16 * (LANES // heads))) * 16
    packed = rows + share
    piece = -(-packed // (16 * seq)) * 16
    owners = -(-packed // piece)
    scale = 1.0 / math.sqrt(dp * seq * length)
    vmem, dma = pltpu.VMEM, pltpu.SemaphoreType.DMA
    square = vmem((length, LANES), F32)
    broad = vmem((length, inner), F32)
    states = vmem((chunks, state, CHUNK), F32)
    wire = vmem((chunks, state, CHUNK), BF16)
    narrow = vmem((length, state), F32)
    scratch = dict(
        f_ref=vmem((length, width), BF16), x_ref=vmem((length, inner), BF16),
        g_ref=vmem((length, inner), BF16), in_sem=dma((3,)),
        ig_ref=vmem((length, width), BF16), hg_ref=vmem((length, inner), BF16), out_sem=dma((2,)),
        ft_s=vmem((width, length), BF16), m_s=vmem((heads, length, length), F32),
        cum_w=broad,
        wall=vmem((width, 2 * LANES), BF16), par=vmem((8, LANES), F32),
        pre_s=square, step_s=square, cum_s=square, cumt_s=square, ecum_s=square,
        toend_s=square, proj_s=square, bct_s=square, inter_s=square, rows_s=square,
        ig_acc=square,
        step_w=broad, ecum_w=broad, toend_w=broad, end_w=broad, wgrad=broad, sgrad=broad,
        left_s=states, right_s=states,
        fin=wire, bin_=wire, fout=wire, bout=wire,
        red_s=vmem((2 * length + 8, LANES), F32), bg_s=narrow, cg_s=narrow,
        hot_s=vmem((chunks, 2 * LANES, CHUNK), BF16), wpack=vmem((dp, packed, LANES), BF16),
        ftin=vmem((dp, rows, length), BF16), gpin=vmem((dp, length, 2 * LANES), BF16),
        fa_send=dma((dp,)), fa_recv=dma((dp,)),
        zout=vmem((owners * piece, LANES), BF16), zin=vmem((seq, piece, LANES), BF16),
        final=vmem((owners * piece, LANES), BF16),
        ag_send=dma((half,)), ag_recv=dma((half,)), fw_send=dma((half,)), fw_recv=dma((half,)),
        ch_send=dma((2, chunks)), ch_recv=dma((2, chunks)),
        gp_send=dma((half,)), gp_recv=dma((half,)), gf_send=dma((half,)), gf_recv=dma((half,)),
        zr_send=dma((seq,)), zr_recv=dma((seq,)), za_send=dma((seq,)), za_recv=dma((seq,)),
    )
    whole = pl.BlockSpec(memory_space=pltpu.VMEM)
    results = pl.pallas_call(
        functools.partial(kernel, dp, seq, heads, scale),
        out_shape=(
            jax.ShapeDtypeStruct((length, width), BF16),
            jax.ShapeDtypeStruct((length, inner), BF16),
            jax.ShapeDtypeStruct((rows, both), F32),
            jax.ShapeDtypeStruct((heads, rows), F32),
        ),
        in_specs=[pl.BlockSpec(memory_space=pltpu.HBM)] * 3 + [whole] * 5,
        out_specs=(pl.BlockSpec(memory_space=pltpu.HBM),) * 2 + (whole,) * 2,
        scratch_shapes=scratch,
        compiler_params=pltpu.CompilerParams(
            collective_id=0, has_side_effects=True, vmem_limit_bytes=56 * 2**20
        ),
        name="mixer_backward",
    )(
        features[0], head_inputs[0], out_grad[0], bc_weight, dt_weight.T,
        dt_bias[None, :], decay_rate[None, :], skip_gain[None, :],
    )
    hbm = pl.BlockSpec(memory_space=pltpu.HBM)
    results = pl.pallas_call(
        place,
        out_shape=tuple(jax.ShapeDtypeStruct(part.shape, part.dtype) for part in results),
        in_specs=[pl.BlockSpec(memory_space=pl.ANY)] * 4,
        out_specs=(hbm,) * 4,
        scratch_shapes=[dma((4,))],
        name="place_results",
    )(*results)
    input_grad, head_grad, bc_grad, dt_grad = results
    return input_grad[None], head_grad[None], bc_grad, dt_grad.T


def solution(mesh):
    tokens = P("dp", "seq", None)
    return jax.shard_map(
        functools.partial(body, mesh.shape["dp"], mesh.shape["seq"]),
        mesh=mesh,
        in_specs=(tokens, tokens, tokens, P("dp", None), P("dp", None), P(), P(), P()),
        out_specs=(tokens, tokens, P("dp", None), P("dp", None)),
        check_vma=False,
    )
```

```python
import functools
import math

import jax
import jax.numpy as jnp
from jax import lax
from jax.experimental import pallas as pl
from jax.experimental.pallas import tpu as pltpu
from jax.sharding import PartitionSpec as P

MESH = pl.DeviceIdType.MESH
F32, BF16 = jnp.float32, jnp.bfloat16
LANES = 128
CHUNK = 256
HIGHEST = lax.Precision.HIGHEST
NT = (((1,), (1,)), ((), ()))
TN = (((0,), (0,)), ((), ()))


def halves(value):
    high = value.astype(BF16)
    return high, (value - high.astype(F32)).astype(BF16)


def mm(left, right, dims=None):
    if dims is None:
        return jnp.dot(left, right, preferred_element_type=F32)
    return lax.dot_general(left, right, dims, preferred_element_type=F32)


def iota(shape, dim):
    return lax.broadcasted_iota(jnp.int32, shape, dim)


def kernel(
    dp, seq, heads, scale,
    f_hbm, x_hbm, g_hbm, wbc_ref, wdt_ref, bias_ref, decay_ref, skip_ref,
    ig_hbm, hg_hbm, bcg_ref, dtg_ref, *,
    ig_ref, hg_ref, out_sem,
    f_ref, x_ref, g_ref, in_sem, ft_s, m_s, cum_w, hot_s, wpack, ftin, gpin, fa_send, fa_recv,
    wall, par, pre_s, step_s, cum_s, cumt_s, ecum_s, toend_s, proj_s, bct_s, inter_s, rows_s,
    ig_acc, step_w, ecum_w, toend_w, end_w, wgrad, sgrad, left_s, right_s,
    fin, bin_, fout, bout, red_s, bg_s, cg_s,
    zout, zin, final,
    ag_send, ag_recv, fw_send, fw_recv, ch_send, ch_recv,
    gp_send, gp_recv, gf_send, gf_recv, zr_send, zr_recv, za_send, za_recv,
):
    me, z = lax.axis_index("dp"), lax.axis_index("seq")
    last = seq - 1
    half = dp // 2
    sib = me + 1 - 2 * lax.rem(me, 2)
    length, inner = x_ref.shape
    width = f_ref.shape[1]
    rows = wbc_ref.shape[0]
    state = wbc_ref.shape[1] // 2
    head_size = inner // heads
    chunks = inner // CHUNK
    groups = LANES // heads
    share = -(-rows // (16 * groups)) * 16
    packed = rows + share
    piece = -(-packed // (16 * seq)) * 16
    owners = -(-packed // piece)

    def pack(value):
        parts = []
        for g in range(groups):
            part = value[g * share : min((g + 1) * share, rows), :]
            if part.shape[0] < share:
                empty = jnp.zeros((share - part.shape[0], LANES), F32)
                part = jnp.concatenate([part, empty], axis=0)
            parts.append(pltpu.roll(part, g * heads, 1) if g else part)
        return sum(parts[1:], parts[0])

    def unpack(value):
        parts = []
        for g in range(groups):
            part = pltpu.roll(value, LANES - g * heads, 1) if g else value
            parts.append(part[0 : min(share, rows - g * share), :])
        return jnp.concatenate(parts, axis=0)

    def at_dp(target):
        return (target, z)

    def peer(k):
        return lax.rem(me + 2 * k, dp)

    def source(k):
        return lax.rem(me + dp - 2 * k, dp)

    loads = [
        pltpu.make_async_copy(src, dst, in_sem.at[i])
        for i, (src, dst) in enumerate(((x_hbm, x_ref), (g_hbm, g_ref), (f_hbm, f_ref)))
    ]
    for load in loads:
        load.start()
    barrier = pltpu.get_barrier_semaphore()
    for k in range(1, dp):
        pl.semaphore_signal(
            barrier, inc=1, device_id=at_dp(lax.rem(me + k, dp)), device_id_type=MESH
        )
    for k in range(1, seq):
        pl.semaphore_signal(barrier, inc=1, device_id=(me, lax.rem(z + k, seq)), device_id_type=MESH)

    def block(index):
        return pl.ds(pl.multiple_of(index * rows, 16), rows)

    wpack[me, 0:rows, :] = wbc_ref[...]
    padded = -(-rows // LANES) * LANES
    wide = jnp.concatenate(
        [wdt_ref[...].astype(F32), jnp.zeros((LANES - heads, rows), F32)], axis=0
    )
    if padded > rows:
        wide = jnp.concatenate([wide, jnp.zeros((LANES, padded - rows), F32)], axis=1)
    wpack[me, rows:, :] = pack(wide.T[0:rows, :]).astype(BF16)
    par[...] = jnp.zeros_like(par)
    par[0:1, 0:heads] = bias_ref[...]
    par[1:2, 0:heads] = decay_ref[...]
    par[2:3, 0:heads] = skip_ref[...]
    pl.semaphore_wait(barrier, dp + seq - 2)

    def ag_copy(k, owner, target):
        return pltpu.make_async_remote_copy(
            src_ref=wpack.at[owner], dst_ref=wpack.at[owner],
            send_sem=ag_send.at[k], recv_sem=ag_recv.at[k],
            device_id=at_dp(target), device_id_type=MESH,
        )

    def fw_copy(k, owner):
        return pltpu.make_async_remote_copy(
            src_ref=wpack.at[owner], dst_ref=wpack.at[owner],
            send_sem=fw_send.at[k], recv_sem=fw_recv.at[k],
            device_id=at_dp(sib), device_id_type=MESH,
        )

    for k in range(1, half):
        ag_copy(k, me, peer(k)).start()
    ag_copy(0, me, sib).start()
    for load in loads:
        load.wait()

    low_half = iota((length, LANES), 1) < head_size
    per_tile = LANES // head_size
    tile_count = inner // LANES

    def early_work(tile):
        ts = pl.ds(pl.multiple_of(tile * LANES, LANES), LANES)
        x_tile, g_full = x_ref[:, ts].astype(F32), g_ref[:, ts]
        for part in range(per_tile):
            mine = low_half if part == 0 else jnp.logical_not(low_half)
            x_part = jnp.where(mine, x_tile, 0.0).astype(BF16)
            m_s[tile * per_tile + part] = mm(x_part, g_full, NT)

    @pl.loop(0, width // CHUNK)
    def _(c):
        cs = pl.ds(pl.multiple_of(c * CHUNK, CHUNK), CHUNK)
        ft_s[cs, :] = f_ref[:, cs].T

    @pl.loop(0, chunks)
    def _(c):
        lane = c * CHUNK + iota((LANES, CHUNK), 1)
        hot = (iota((LANES, CHUNK), 0) == lane // head_size).astype(F32).astype(BF16)
        hot_s[c, 0:LANES, :] = hot
        hot_s[c, LANES:, :] = hot

    for k in range(1, half):
        pl.loop(tile_count * (k - 1) // (half - 1), tile_count * k // (half - 1))(early_work)
        ag_copy(k, source(k), peer(k)).wait_recv()
        fw_copy(k, source(k)).start()
    ag_copy(0, sib, sib).wait_recv()
    for k in range(1, half):
        fw_copy(k, lax.rem(sib + dp - 2 * k, dp)).wait_recv()

    def fa_copy(k):
        target = lax.rem(me + k, dp)
        return pltpu.make_async_remote_copy(
            src_ref=ft_s.at[block(target)], dst_ref=ftin.at[me],
            send_sem=fa_send.at[k], recv_sem=fa_recv.at[k],
            device_id=at_dp(target), device_id_type=MESH,
        )

    for k in range(1, dp):
        fa_copy(k).start()
    ftin[me] = ft_s[block(me), :]

    @pl.loop(0, dp)
    def _(i):
        wall[block(i), 0:LANES] = wpack[i, 0:rows, :]
        wall[block(i), LANES:] = unpack(wpack[i, rows:, :].astype(F32)).astype(BF16)

    projection = mm(f_ref[...], wall[...])
    proj_s[...] = projection[:, :LANES]
    pre = projection[:, LANES:] + par[0:1, :]
    pre_s[...] = pre
    step = jnp.maximum(pre, 0.0) + jnp.log1p(jnp.exp(-jnp.abs(pre)))
    step_s[...] = step
    lower = (iota((length, length), 0) >= iota((length, length), 1)).astype(F32)
    cum = jnp.dot(
        lower, -par[1:2, :] * step, precision=HIGHEST, preferred_element_type=F32
    )
    cum_s[...] = cum
    cumt_s[...] = cum.T
    ecum_s[...] = jnp.exp(cum)
    toend_s[...] = jnp.exp(cum[length - 1 :, :] - cum)
    bct_s[...] = proj_s[...].T
    bt = bct_s[0:state, :]
    ct = bct_s[state:, :]
    bt_hi, bt_lo = halves(bt)
    ct_hi, ct_lo = halves(ct)
    bt3 = jnp.concatenate([bt_hi, bt_lo, bt_hi], axis=1)
    ct3 = jnp.concatenate([ct_hi, ct_lo, ct_hi], axis=1)
    b_rows = proj_s[:, 0:state]
    c_rows = proj_s[:, state:]
    inter_s[...] = jnp.dot(b_rows, ct, precision=HIGHEST, preferred_element_type=F32)

    def spread(value, c, exact=False):
        high, low = halves(value)
        result = mm(jnp.concatenate([high, low], axis=1), hot_s[c])
        if exact:
            rest = value - high.astype(F32) - low.astype(F32)
            result = result + mm(rest.astype(BF16), hot_s[c, 0:LANES, :])
        return result

    def lanes(c):
        return pl.ds(pl.multiple_of(c * CHUNK, CHUNK), CHUNK)

    def chain_copy(way, c):
        src, dst = ((fout, fin), (bout, bin_))[way]
        to = (z + 1, z + last)[way]
        return pltpu.make_async_remote_copy(
            src_ref=src.at[c], dst_ref=dst.at[c],
            send_sem=ch_send.at[way, c], recv_sem=ch_recv.at[way, c],
            device_id=(me, lax.rem(to, seq)), device_id_type=MESH,
        )

    @pl.loop(0, chunks)
    def _(c):
        cs = lanes(c)
        step_c = spread(step_s[...], c)
        ecum_c = spread(ecum_s[...], c)
        toend_c = spread(toend_s[...], c)
        ends = x_ref[:, cs].astype(F32) * step_c * toend_c
        weighted = g_ref[:, cs].astype(F32) * ecum_c
        step_w[:, cs] = step_c
        ecum_w[:, cs] = ecum_c
        toend_w[:, cs] = toend_c
        cum_w[:, cs] = spread(cum_s[...], c, exact=True)
        end_w[:, cs] = ends
        wgrad[:, cs] = weighted
        e_hi, e_lo = halves(ends)
        w_hi, w_lo = halves(weighted)
        left_s[c] = mm(bt3, jnp.concatenate([e_hi, e_hi, e_lo], axis=0))
        right_s[c] = mm(ct3, jnp.concatenate([w_hi, w_hi, w_lo], axis=0))

        for way, first in ((0, 0), (1, last)):
            @pl.when(z == first)
            def _():
                arrived, leaving, here = ((fin, fout, left_s), (bin_, bout, right_s))[way]
                arrived[c] = jnp.zeros((state, CHUNK), BF16)
                if seq > 1:
                    leaving[c] = here[c].astype(BF16)
                    chain_copy(way, c).start()

    def chain_hop(way, c):
        arrived, leaving, local = ((fin, fout, left_s), (bin_, bout, right_s))[way]
        chain_copy(way, c).wait_recv()

        @pl.when(z != (last, 0)[way])
        def _():
            decay = ecum_w[length - 1 :, lanes(c)]
            leaving[c] = (arrived[c].astype(F32) * decay + local[c]).astype(BF16)
            chain_copy(way, c).start()

    later = iota((length, length), 1) >= iota((length, length), 0)
    def by_head(tile):
        turned = pltpu.roll(tile, head_size, 1)
        return jnp.where(low_half, tile, turned), jnp.where(low_half, turned, tile)

    def tile_work(tile):
        ts = pl.ds(pl.multiple_of(tile * LANES, LANES), LANES)
        g_tile = g_ref[:, ts].astype(F32)
        inter = inter_s[...]
        cums, steps = by_head(cum_w[:, ts]), by_head(step_w[:, ts])
        mixes, grads, sums = [], [], []
        for part in range(per_tile):
            head = tile * per_tile + part
            gap = cumt_s[pl.ds(head, 1), :] - cums[part]
            weights = jnp.exp(jnp.where(later, gap, -1e30))
            mine = low_half if part == 0 else jnp.logical_not(low_half)
            g_part = jnp.where(mine, g_tile, 0.0).astype(BF16)
            shared = m_s[head] * steps[part] * weights
            sums.append(shared)
            rows_s[pl.ds(head, 1), :] = jnp.sum(shared * inter, axis=0, keepdims=True)
            mixes += list(halves(inter * weights))
            grads += [g_part, g_part]
        ig_acc[...] += sum(sums[1:], sums[0])
        sgrad[:, ts] = mm(jnp.concatenate(mixes, axis=1), jnp.concatenate(grads, axis=0))

    def reduce_heads(value, c):
        hot = hot_s[c, 0:LANES, :]
        high, low = halves(value)
        return mm(high, hot, NT) + mm(low, hot, NT)

    b_hi, b_lo = halves(b_rows)
    c_hi, c_lo = halves(c_rows)
    bpair = jnp.concatenate([b_hi, b_lo], axis=1)
    cpair = jnp.concatenate([c_hi, c_lo], axis=1)

    def carried_work(c):
        cs = lanes(c)
        state_in, state_grad = fin[c], bin_[c]
        weighted, ends = wgrad[:, cs], end_w[:, cs]
        inter_out = mm(cpair, jnp.concatenate([state_in, state_in], axis=0))
        reach = mm(bpair, jnp.concatenate([state_grad, state_grad], axis=0))
        w_hi, w_lo = halves(weighted)
        e_hi, e_lo = halves(ends)
        cg_s[...] += mm(w_hi, state_in, NT) + mm(w_lo, state_in, NT)
        bg_s[...] += mm(e_hi, state_grad, NT) + mm(e_lo, state_grad, NT)
        total = sgrad[:, cs] + toend_w[:, cs] * reach
        x_part, g_part = x_ref[:, cs].astype(F32), g_ref[:, cs].astype(F32)
        decay = ecum_w[length - 1 :, cs]
        product = state_grad.astype(F32) * state_in.astype(F32)
        at_end = jnp.sum(ends * reach, axis=0, keepdims=True) + decay * jnp.sum(
            product, axis=0, keepdims=True
        )
        stacked = jnp.concatenate(
            [weighted * inter_out, x_part * total, jnp.broadcast_to(at_end, (8, CHUNK))], axis=0
        )
        red_s[...] += reduce_heads(stacked, c)
        skip_c = spread(jnp.broadcast_to(par[2:3, :], (8, LANES)), c)[0:1, :]
        hg_ref[:, cs] = (g_part * skip_c + step_w[:, cs] * total).astype(BF16)

    ig_acc[...] = jnp.zeros_like(ig_acc)
    rows_s[...] = jnp.zeros_like(rows_s)
    cg_s[...] = jnp.zeros_like(cg_s)
    bg_s[...] = jnp.zeros_like(bg_s)
    red_s[...] = jnp.zeros_like(red_s)
    tiles = CHUNK // LANES

    early = tiles // 2

    @pl.loop(0, chunks + max(last - 1, 0))
    def _(s):
        forward, back = s - (z - 1), s - (last - 1 - z)

        @pl.when(s < chunks)
        def _():
            for tile in range(early):
                tile_work(s * tiles + tile)

        if seq > 1:
            @pl.when(jnp.logical_and(z > 0, jnp.logical_and(forward >= 0, forward < chunks)))
            def _():
                chain_hop(0, forward)

            @pl.when(jnp.logical_and(z < last, jnp.logical_and(back >= 0, back < chunks)))
            def _():
                chain_hop(1, back)

        @pl.when(s < chunks)
        def _():
            for tile in range(early, tiles):
                tile_work(s * tiles + tile)

        both = s - jnp.maximum(z, last - z) + min(last, 1)

        @pl.when(jnp.logical_and(both >= 0, both < chunks))
        def _():
            carried_work(both)

    store_hg = pltpu.make_async_copy(hg_ref, hg_hbm, out_sem.at[0])
    store_hg.start()
    acc = ig_acc[...]
    c_grad = cg_s[...] + lax.dot_general(
        acc, b_rows, TN, precision=HIGHEST, preferred_element_type=F32
    )
    b_grad = bg_s[...] + jnp.dot(acc, c_rows, precision=HIGHEST, preferred_element_type=F32)
    step = step_s[...]
    direct = red_s[length : 2 * length, :]
    cum_grad = rows_s[...].T + red_s[0:length, :] - step * direct
    is_last = iota((length, LANES), 0) == length - 1
    cum_grad = cum_grad + jnp.where(is_last, red_s[2 * length : 2 * length + 1, :], 0.0)
    upper = later.astype(F32)
    decay_grad = jnp.dot(upper, cum_grad, precision=HIGHEST, preferred_element_type=F32)
    step_grad = direct - par[1:2, :] * decay_grad
    pre_grad = step_grad / (1.0 + jnp.exp(-pre_s[...]))
    gpin[me, :, 0:LANES] = jnp.concatenate([b_grad, c_grad], axis=1).astype(BF16)
    gpin[me, :, LANES:] = pre_grad.astype(BF16)

    def gp_copy(k, owner, target):
        return pltpu.make_async_remote_copy(
            src_ref=gpin.at[owner], dst_ref=gpin.at[owner],
            send_sem=gp_send.at[k], recv_sem=gp_recv.at[k],
            device_id=at_dp(target), device_id_type=MESH,
        )

    def gf_copy(k, owner):
        return pltpu.make_async_remote_copy(
            src_ref=gpin.at[owner], dst_ref=gpin.at[owner],
            send_sem=gf_send.at[k], recv_sem=gf_recv.at[k],
            device_id=at_dp(sib), device_id_type=MESH,
        )

    for k in range(1, half):
        gp_copy(k, me, peer(k)).start()
    gp_copy(0, me, sib).start()

    gproj = gpin[me]
    for c in range(width // CHUNK):
        cs = slice(c * CHUNK, (c + 1) * CHUNK)
        ig_ref[:, cs] = mm(gproj, wall[cs, :], NT).astype(BF16)
    store_ig = pltpu.make_async_copy(ig_ref, ig_hbm, out_sem.at[1])
    store_ig.start()

    for k in range(1, dp):
        fa_copy(k).wait_recv()

    def gradient_of(index):
        return mm(ftin[index], gpin[index])

    total = gradient_of(me)
    gp_copy(0, sib, sib).wait_recv()
    total = total + gradient_of(sib)
    for k in range(1, half):
        gp_copy(k, source(k), peer(k)).wait_recv()
        gf_copy(k, source(k)).start()
        total = total + gradient_of(source(k))
    for k in range(1, half):
        other = lax.rem(sib + dp - 2 * k, dp)
        gf_copy(k, other).wait_recv()
        total = total + gradient_of(other)

    zout[0:rows, :] = total[:, 0:LANES].astype(BF16)
    zout[rows:packed, :] = pack(total[:, LANES:]).astype(BF16)
    if owners * piece > packed:
        zout[packed:, :] = jnp.zeros((owners * piece - packed, LANES), BF16)

    def z_piece(index):
        return pl.ds(pl.multiple_of(index * piece, 16), piece)

    def to_z(k):
        return lax.rem(z + k, seq)

    def from_z(k):
        return lax.rem(z + seq - k, seq)

    def zr_copy(k):
        return pltpu.make_async_remote_copy(
            src_ref=zout.at[z_piece(to_z(k))], dst_ref=zin.at[k],
            send_sem=zr_send.at[k], recv_sem=zr_recv.at[k],
            device_id=(me, to_z(k)), device_id_type=MESH,
        )

    def za_copy(k, owner):
        return pltpu.make_async_remote_copy(
            src_ref=final.at[z_piece(owner)], dst_ref=final.at[z_piece(owner)],
            send_sem=za_send.at[k], recv_sem=za_recv.at[k],
            device_id=(me, to_z(k)), device_id_type=MESH,
        )

    owner_here = z < owners
    for k in range(1, seq):
        @pl.when(to_z(k) < owners)
        def _():
            zr_copy(k).start()

    @pl.when(owner_here)
    def _():
        mine = zout[z_piece(z), :].astype(F32)
        for k in range(1, seq):
            zr_copy(k).wait_recv()
            mine = mine + zin[k].astype(F32)
        final[z_piece(z), :] = (mine * scale).astype(BF16)
        for k in range(1, seq):
            za_copy(k, z).start()

    for k in range(1, seq):
        @pl.when(from_z(k) < owners)
        def _():
            za_copy(k, from_z(k)).wait_recv()

    bcg_ref[...] = final[0:rows, :].astype(F32)
    tail = unpack(final[rows:packed, :].astype(F32))
    if padded > rows:
        tail = jnp.concatenate([tail, jnp.zeros((padded - rows, LANES), F32)], axis=0)
    dtg_ref[...] = tail.T[0:heads, 0:rows]

    store_hg.wait()
    store_ig.wait()
    ag_copy(0, me, sib).wait_send()
    for k in range(1, half):
        ag_copy(k, me, peer(k)).wait_send()
        fw_copy(k, source(k)).wait_send()
        gp_copy(k, me, peer(k)).wait_send()
        gf_copy(k, source(k)).wait_send()
    gp_copy(0, me, sib).wait_send()
    for k in range(1, dp):
        fa_copy(k).wait_send()
    for k in range(1, seq):
        @pl.when(to_z(k) < owners)
        def _():
            zr_copy(k).wait_send()

    @pl.when(owner_here)
    def _():
        for k in range(1, seq):
            za_copy(k, z).wait_send()

    for way, final_one in ((0, last), (1, 0)):
        @pl.when(z != final_one)
        def _():
            @pl.loop(0, chunks)
            def _(c):
                chain_copy(way, c).wait_send()


def place(*refs):
    sources, targets, held, sem = refs[0:4], refs[4:8], refs[8:12], refs[12]
    slots = []
    for index, source in enumerate(sources):
        parts = 4 if source.dtype == BF16 else 1
        step = source.shape[0] // parts
        slots += [(index, slice(part * step, (part + 1) * step)) for part in range(parts)]
    loads, stores = [], []
    for slot, (index, part) in enumerate(slots):
        source, middle, target = sources[index].at[part], held[index].at[part], targets[index].at[part]
        loads.append(pltpu.make_async_copy(source, middle, sem.at[0, slot]))
        stores.append(pltpu.make_async_copy(middle, target, sem.at[1, slot]))
        loads[-1].start()
    for load, store in zip(loads, stores):
        load.wait()
        store.start()
    for store in stores:
        store.wait()


def body(dp, seq, features, head_inputs, out_grad, bc_weight, dt_weight, dt_bias, decay_rate, skip_gain):
    _, length, width = features.shape
    inner = head_inputs.shape[2]
    heads = dt_bias.shape[0]
    rows, both = bc_weight.shape
    state = both // 2
    half = dp // 2
    chunks = inner // CHUNK
    share = -(-rows // (16 * (LANES // heads))) * 16
    packed = rows + share
    piece = -(-packed // (16 * seq)) * 16
    owners = -(-packed // piece)
    scale = 1.0 / math.sqrt(dp * seq * length)
    vmem, dma = pltpu.VMEM, pltpu.SemaphoreType.DMA
    square = vmem((length, LANES), F32)
    broad = vmem((length, inner), F32)
    states = vmem((chunks, state, CHUNK), F32)
    wire = vmem((chunks, state, CHUNK), BF16)
    narrow = vmem((length, state), F32)
    scratch = dict(
        f_ref=vmem((length, width), BF16), x_ref=vmem((length, inner), BF16),
        g_ref=vmem((length, inner), BF16), in_sem=dma((3,)),
        ig_ref=vmem((length, width), BF16), hg_ref=vmem((length, inner), BF16), out_sem=dma((2,)),
        ft_s=vmem((width, length), BF16), m_s=vmem((heads, length, length), F32),
        cum_w=broad,
        wall=vmem((width, 2 * LANES), BF16), par=vmem((8, LANES), F32),
        pre_s=square, step_s=square, cum_s=square, cumt_s=square, ecum_s=square,
        toend_s=square, proj_s=square, bct_s=square, inter_s=square, rows_s=square,
        ig_acc=square,
        step_w=broad, ecum_w=broad, toend_w=broad, end_w=broad, wgrad=broad, sgrad=broad,
        left_s=states, right_s=states,
        fin=wire, bin_=wire, fout=wire, bout=wire,
        red_s=vmem((2 * length + 8, LANES), F32), bg_s=narrow, cg_s=narrow,
        hot_s=vmem((chunks, 2 * LANES, CHUNK), BF16), wpack=vmem((dp, packed, LANES), BF16),
        ftin=vmem((dp, rows, length), BF16), gpin=vmem((dp, length, 2 * LANES), BF16),
        fa_send=dma((dp,)), fa_recv=dma((dp,)),
        zout=vmem((owners * piece, LANES), BF16), zin=vmem((seq, piece, LANES), BF16),
        final=vmem((owners * piece, LANES), BF16),
        ag_send=dma((half,)), ag_recv=dma((half,)), fw_send=dma((half,)), fw_recv=dma((half,)),
        ch_send=dma((2, chunks)), ch_recv=dma((2, chunks)),
        gp_send=dma((half,)), gp_recv=dma((half,)), gf_send=dma((half,)), gf_recv=dma((half,)),
        zr_send=dma((seq,)), zr_recv=dma((seq,)), za_send=dma((seq,)), za_recv=dma((seq,)),
    )
    whole = pl.BlockSpec(memory_space=pltpu.VMEM)
    results = pl.pallas_call(
        functools.partial(kernel, dp, seq, heads, scale),
        out_shape=(
            jax.ShapeDtypeStruct((length, width), BF16),
            jax.ShapeDtypeStruct((length, inner), BF16),
            jax.ShapeDtypeStruct((rows, both), F32),
            jax.ShapeDtypeStruct((heads, rows), F32),
        ),
        in_specs=[pl.BlockSpec(memory_space=pltpu.HBM)] * 3 + [whole] * 5,
        out_specs=(pl.BlockSpec(memory_space=pltpu.HBM),) * 2 + (whole,) * 2,
        scratch_shapes=scratch,
        compiler_params=pltpu.CompilerParams(
            collective_id=0, has_side_effects=True, vmem_limit_bytes=56 * 2**20
        ),
        name="mixer_backward",
    )(
        features[0], head_inputs[0], out_grad[0], bc_weight, dt_weight.T,
        dt_bias[None, :], decay_rate[None, :], skip_gain[None, :],
    )
    hbm = pl.BlockSpec(memory_space=pltpu.HBM)
    results = pl.pallas_call(
        place,
        out_shape=tuple(jax.ShapeDtypeStruct(part.shape, part.dtype) for part in results),
        in_specs=[hbm] * 4,
        out_specs=(hbm,) * 4,
        scratch_shapes=[vmem(part.shape, part.dtype) for part in results] + [dma((2, 10))],
        name="place_results",
    )(*results)
    input_grad, head_grad, bc_grad, dt_grad = results
    return input_grad[None], head_grad[None], bc_grad, dt_grad.T


def solution(mesh):
    tokens = P("dp", "seq", None)
    return jax.shard_map(
        functools.partial(body, mesh.shape["dp"], mesh.shape["seq"]),
        mesh=mesh,
        in_specs=(tokens, tokens, tokens, P("dp", None), P("dp", None), P(), P(), P()),
        out_specs=(tokens, tokens, P("dp", None), P("dp", None)),
        check_vma=False,
    )
```

```python
import functools
import math

import jax
import jax.numpy as jnp
from jax import lax
from jax.experimental import pallas as pl
from jax.experimental.pallas import tpu as pltpu
from jax.sharding import PartitionSpec as P

MESH = pl.DeviceIdType.MESH
F32, BF16 = jnp.float32, jnp.bfloat16
LANES = 128
CHUNK = 512
HIGHEST = lax.Precision.HIGHEST
NT = (((1,), (1,)), ((), ()))
TN = (((0,), (0,)), ((), ()))


def halves(value):
    high = value.astype(BF16)
    return high, (value - high.astype(F32)).astype(BF16)


def mm(left, right, dims=None):
    if dims is None:
        return jnp.dot(left, right, preferred_element_type=F32)
    return lax.dot_general(left, right, dims, preferred_element_type=F32)


def iota(shape, dim):
    return lax.broadcasted_iota(jnp.int32, shape, dim)


def kernel(
    dp, seq, heads, scale,
    f_hbm, x_hbm, g_hbm, wbc_ref, wdt_ref, bias_ref, decay_ref, skip_ref,
    ig_hbm, hg_hbm, bcg_ref, dtg_ref, *,
    ig_ref, hg_ref, out_sem,
    f_ref, x_ref, g_ref, in_sem, ft_s, m_s, cum_w, hot_s, wpack, ftin, gpin, fa_send, fa_recv,
    wall, par, pre_s, step_s, cum_s, cumt_s, ecum_s, toend_s, proj_s, bct_s, inter_s, rows_s,
    ig_acc, step_w, ecum_w, toend_w, end_w, wgrad, sgrad, left_s, right_s,
    fin, bin_, fout, bout, red_s, bg_s, cg_s,
    zout, zin, final,
    ag_send, ag_recv, fw_send, fw_recv, ch_send, ch_recv,
    gp_send, gp_recv, gf_send, gf_recv, zr_send, zr_recv, za_send, za_recv,
):
    me, z = lax.axis_index("dp"), lax.axis_index("seq")
    last = seq - 1
    half = dp // 2
    sib = me + 1 - 2 * lax.rem(me, 2)
    length, inner = x_ref.shape
    width = f_ref.shape[1]
    rows = wbc_ref.shape[0]
    state = wbc_ref.shape[1] // 2
    head_size = inner // heads
    chunks = inner // CHUNK
    groups = LANES // heads
    share = -(-rows // (16 * groups)) * 16
    packed = rows + share
    piece = -(-packed // (16 * seq)) * 16
    owners = -(-packed // piece)

    part_rows = -(-length // (16 * groups)) * 16

    def pack(value, each):
        value = jnp.where(iota(value.shape, 1) < heads, value, 0.0)
        parts = []
        for g in range(groups):
            part = value[g * each : min((g + 1) * each, value.shape[0]), :]
            if part.shape[0] < each:
                empty = jnp.zeros((each - part.shape[0], LANES), F32)
                part = jnp.concatenate([part, empty], axis=0)
            parts.append(pltpu.roll(part, g * heads, 1) if g else part)
        return sum(parts[1:], parts[0])

    def unpack(value, count):
        each = value.shape[0]
        parts = []
        for g in range(groups):
            part = pltpu.roll(value, LANES - g * heads, 1) if g else value
            parts.append(part[0 : min(each, count - g * each), :])
        return jnp.concatenate(parts, axis=0)

    def at_dp(target):
        return (target, z)

    def peer(k):
        return lax.rem(me + 2 * k, dp)

    def source(k):
        return lax.rem(me + dp - 2 * k, dp)

    loads = [
        pltpu.make_async_copy(src, dst, in_sem.at[i])
        for i, (src, dst) in enumerate(((x_hbm, x_ref), (g_hbm, g_ref), (f_hbm, f_ref)))
    ]
    for load in loads:
        load.start()
    barrier = pltpu.get_barrier_semaphore()
    for k in range(1, dp):
        pl.semaphore_signal(
            barrier, inc=1, device_id=at_dp(lax.rem(me + k, dp)), device_id_type=MESH
        )
    for k in range(1, seq):
        pl.semaphore_signal(barrier, inc=1, device_id=(me, lax.rem(z + k, seq)), device_id_type=MESH)

    def block(index):
        return pl.ds(pl.multiple_of(index * rows, 16), rows)

    wpack[me, 0:rows, :] = wbc_ref[...]
    padded = -(-rows // LANES) * LANES
    wide = jnp.concatenate(
        [wdt_ref[...].astype(F32), jnp.zeros((LANES - heads, rows), F32)], axis=0
    )
    if padded > rows:
        wide = jnp.concatenate([wide, jnp.zeros((LANES, padded - rows), F32)], axis=1)
    wpack[me, rows:, :] = pack(wide.T[0:rows, :], share).astype(BF16)
    par[...] = jnp.zeros_like(par)
    par[0:1, 0:heads] = bias_ref[...]
    par[1:2, 0:heads] = decay_ref[...]
    par[2:3, 0:heads] = skip_ref[...]
    pl.semaphore_wait(barrier, dp + seq - 2)

    def ag_copy(k, owner, target):
        return pltpu.make_async_remote_copy(
            src_ref=wpack.at[owner], dst_ref=wpack.at[owner],
            send_sem=ag_send.at[k], recv_sem=ag_recv.at[k],
            device_id=at_dp(target), device_id_type=MESH,
        )

    def fw_copy(k, owner):
        return pltpu.make_async_remote_copy(
            src_ref=wpack.at[owner], dst_ref=wpack.at[owner],
            send_sem=fw_send.at[k], recv_sem=fw_recv.at[k],
            device_id=at_dp(sib), device_id_type=MESH,
        )

    for k in range(1, half):
        ag_copy(k, me, peer(k)).start()
    ag_copy(0, me, sib).start()
    for load in loads:
        load.wait()

    low_half = iota((length, LANES), 1) < head_size
    per_tile = LANES // head_size
    tile_count = inner // LANES

    def early_work(tile):
        ts = slice(tile * LANES, (tile + 1) * LANES)
        x_tile, g_full = x_ref[:, ts].astype(F32), g_ref[:, ts]
        for part in range(per_tile):
            mine = low_half if part == 0 else jnp.logical_not(low_half)
            x_part = jnp.where(mine, x_tile, 0.0).astype(BF16)
            m_s[tile * per_tile + part] = mm(x_part, g_full, NT)

    @pl.loop(0, width // CHUNK)
    def _(c):
        cs = pl.ds(pl.multiple_of(c * CHUNK, CHUNK), CHUNK)
        ft_s[cs, :] = f_ref[:, cs].T

    @pl.loop(0, chunks)
    def _(c):
        lane = c * CHUNK + iota((LANES, CHUNK), 1)
        hot = (iota((LANES, CHUNK), 0) == lane // head_size).astype(F32).astype(BF16)
        hot_s[c, 0:LANES, :] = hot
        hot_s[c, LANES:, :] = hot

    for k in range(1, half):
        for tile in range(tile_count * (k - 1) // (half - 1), tile_count * k // (half - 1)):
            early_work(tile)
        ag_copy(k, source(k), peer(k)).wait_recv()
        fw_copy(k, source(k)).start()
    ag_copy(0, sib, sib).wait_recv()
    for k in range(1, half):
        fw_copy(k, lax.rem(sib + dp - 2 * k, dp)).wait_recv()

    def fa_copy(k):
        target = lax.rem(me + k, dp)
        return pltpu.make_async_remote_copy(
            src_ref=ft_s.at[block(target)], dst_ref=ftin.at[me],
            send_sem=fa_send.at[k], recv_sem=fa_recv.at[k],
            device_id=at_dp(target), device_id_type=MESH,
        )

    for k in range(1, dp):
        fa_copy(k).start()
    ftin[me] = ft_s[block(me), :]

    @pl.loop(0, dp, unroll=4)
    def _(i):
        wall[block(i), 0:LANES] = wpack[i, 0:rows, :]
        wall[block(i), LANES:] = unpack(wpack[i, rows:, :].astype(F32), rows).astype(BF16)

    projection = mm(f_ref[...], wall[...])
    proj_s[...] = projection[:, :LANES]
    pre = projection[:, LANES:] + par[0:1, :]
    pre_s[...] = pre
    step = jnp.maximum(pre, 0.0) + jnp.log1p(jnp.exp(-jnp.abs(pre)))
    step_s[...] = step
    lower = (iota((length, length), 0) >= iota((length, length), 1)).astype(F32)
    cum = jnp.dot(
        lower, -par[1:2, :] * step, precision=HIGHEST, preferred_element_type=F32
    )
    cum_s[...] = cum
    cumt_s[...] = cum.T
    ecum_s[...] = jnp.exp(cum)
    toend_s[...] = jnp.exp(cum[length - 1 :, :] - cum)
    bct_s[...] = proj_s[...].T
    bt = bct_s[0:state, :]
    ct = bct_s[state:, :]
    bt_hi, bt_lo = halves(bt)
    ct_hi, ct_lo = halves(ct)
    bt3 = jnp.concatenate([bt_hi, bt_lo, bt_hi], axis=1)
    ct3 = jnp.concatenate([ct_hi, ct_lo, ct_hi], axis=1)
    b_rows = proj_s[:, 0:state]
    c_rows = proj_s[:, state:]
    inter_s[...] = jnp.dot(b_rows, ct, precision=HIGHEST, preferred_element_type=F32)

    def spread(value, c, exact=False):
        high, low = halves(value)
        result = mm(jnp.concatenate([high, low], axis=1), hot_s[c])
        if exact:
            rest = value - high.astype(F32) - low.astype(F32)
            result = result + mm(rest.astype(BF16), hot_s[c, 0:LANES, :])
        return result

    def lanes(c):
        return pl.ds(pl.multiple_of(c * CHUNK, CHUNK), CHUNK)

    def chain_copy(way, c):
        src, dst = ((fout, fin), (bout, bin_))[way]
        to = (z + 1, z + last)[way]
        return pltpu.make_async_remote_copy(
            src_ref=src.at[c], dst_ref=dst.at[c],
            send_sem=ch_send.at[way, c], recv_sem=ch_recv.at[way, c],
            device_id=(me, lax.rem(to, seq)), device_id_type=MESH,
        )

    def local_work(c):
        cs = lanes(c)
        step_c = spread(step_s[...], c)
        ecum_c = spread(ecum_s[...], c)
        toend_c = spread(toend_s[...], c)
        ends = x_ref[:, cs].astype(F32) * step_c * toend_c
        weighted = g_ref[:, cs].astype(F32) * ecum_c
        step_w[:, cs] = step_c
        ecum_w[:, cs] = ecum_c
        toend_w[:, cs] = toend_c
        cum_w[:, cs] = spread(cum_s[...], c, exact=True)
        end_w[:, cs] = ends
        wgrad[:, cs] = weighted
        e_hi, e_lo = halves(ends)
        w_hi, w_lo = halves(weighted)
        left_s[c] = mm(bt3, jnp.concatenate([e_hi, e_hi, e_lo], axis=0))
        right_s[c] = mm(ct3, jnp.concatenate([w_hi, w_hi, w_lo], axis=0))

    def chain_start(c):
        for way, first in ((0, 0), (1, last)):
            @pl.when(z == first)
            def _():
                arrived, leaving, here = ((fin, fout, left_s), (bin_, bout, right_s))[way]
                arrived[c] = jnp.zeros((state, CHUNK), BF16)
                if seq > 1:
                    leaving[c] = here[c].astype(BF16)
                    chain_copy(way, c).start()

    def chain_hop(way, c):
        arrived, leaving, local = ((fin, fout, left_s), (bin_, bout, right_s))[way]
        chain_copy(way, c).wait_recv()

        @pl.when(z != (last, 0)[way])
        def _():
            decay = ecum_w[length - 1 :, lanes(c)]
            leaving[c] = (arrived[c].astype(F32) * decay + local[c]).astype(BF16)
            chain_copy(way, c).start()

    later = iota((length, length), 1) >= iota((length, length), 0)
    def by_head(tile):
        turned = pltpu.roll(tile, head_size, 1)
        return jnp.where(low_half, tile, turned), jnp.where(low_half, turned, tile)

    def tile_work(tile):
        ts = pl.ds(pl.multiple_of(tile * LANES, LANES), LANES)
        g_tile = g_ref[:, ts].astype(F32)
        inter = inter_s[...]
        cums, steps = by_head(cum_w[:, ts]), by_head(step_w[:, ts])
        mixes, grads, sums = [], [], []
        for part in range(per_tile):
            head = tile * per_tile + part
            gap = cumt_s[pl.ds(head, 1), :] - cums[part]
            weights = jnp.exp(jnp.where(later, gap, -1e30))
            mine = low_half if part == 0 else jnp.logical_not(low_half)
            g_part = jnp.where(mine, g_tile, 0.0).astype(BF16)
            shared = m_s[head] * steps[part] * weights
            sums.append(shared)
            rows_s[pl.ds(head, 1), :] = jnp.sum(shared * inter, axis=0, keepdims=True)
            mixes += list(halves(inter * weights))
            grads += [g_part, g_part]
        ig_acc[...] += sum(sums[1:], sums[0])
        sgrad[:, ts] = mm(jnp.concatenate(mixes, axis=1), jnp.concatenate(grads, axis=0))

    def reduce_heads(value, c):
        hot = hot_s[c, 0:LANES, :]
        high, low = halves(value)
        return mm(high, hot, NT) + mm(low, hot, NT)

    b_hi, b_lo = halves(b_rows)
    c_hi, c_lo = halves(c_rows)
    bpair = jnp.concatenate([b_hi, b_lo], axis=1)
    cpair = jnp.concatenate([c_hi, c_lo], axis=1)

    def carried_work(c):
        cs = lanes(c)
        state_in, state_grad = fin[c], bin_[c]
        weighted, ends = wgrad[:, cs], end_w[:, cs]
        inter_out = mm(cpair, jnp.concatenate([state_in, state_in], axis=0))
        reach = mm(bpair, jnp.concatenate([state_grad, state_grad], axis=0))
        w_hi, w_lo = halves(weighted)
        e_hi, e_lo = halves(ends)
        cg_s[...] += mm(w_hi, state_in, NT) + mm(w_lo, state_in, NT)
        bg_s[...] += mm(e_hi, state_grad, NT) + mm(e_lo, state_grad, NT)
        total = sgrad[:, cs] + toend_w[:, cs] * reach
        x_part, g_part = x_ref[:, cs].astype(F32), g_ref[:, cs].astype(F32)
        decay = ecum_w[length - 1 :, cs]
        product = state_grad.astype(F32) * state_in.astype(F32)
        at_end = jnp.sum(ends * reach, axis=0, keepdims=True) + decay * jnp.sum(
            product, axis=0, keepdims=True
        )
        stacked = jnp.concatenate(
            [weighted * inter_out, x_part * total, jnp.broadcast_to(at_end, (8, CHUNK))], axis=0
        )
        red_s[...] += reduce_heads(stacked, c)
        skip_c = spread(jnp.broadcast_to(par[2:3, :], (8, LANES)), c)[0:1, :]
        hg_ref[:, cs] = (g_part * skip_c + step_w[:, cs] * total).astype(BF16)

    ig_acc[...] = jnp.zeros_like(ig_acc)
    rows_s[...] = jnp.zeros_like(rows_s)
    cg_s[...] = jnp.zeros_like(cg_s)
    bg_s[...] = jnp.zeros_like(bg_s)
    red_s[...] = jnp.zeros_like(red_s)
    tiles = CHUNK // LANES

    local_work(0)
    chain_start(0)

    @pl.loop(0, chunks + max(last - 1, 0))
    def _(s):
        forward, back = s - (z - 1), s - (last - 1 - z)

        @pl.when(s < chunks)
        def _():
            local_work(jnp.minimum(s + 1, chunks - 1))
            for tile in range(tiles):
                tile_work(s * tiles + tile)

        @pl.when(s < chunks - 1)
        def _():
            chain_start(s + 1)

        if seq > 1:
            @pl.when(jnp.logical_and(z > 0, jnp.logical_and(forward >= 0, forward < chunks)))
            def _():
                chain_hop(0, forward)

            @pl.when(jnp.logical_and(z < last, jnp.logical_and(back >= 0, back < chunks)))
            def _():
                chain_hop(1, back)

        both = s - jnp.maximum(z, last - z) + min(last, 1)

        @pl.when(jnp.logical_and(both >= 0, both < chunks))
        def _():
            carried_work(both)

    store_hg = pltpu.make_async_copy(hg_ref, hg_hbm, out_sem.at[0])
    store_hg.start()
    acc = ig_acc[...]
    c_grad = cg_s[...] + lax.dot_general(
        acc, b_rows, TN, precision=HIGHEST, preferred_element_type=F32
    )
    b_grad = bg_s[...] + jnp.dot(acc, c_rows, precision=HIGHEST, preferred_element_type=F32)
    pair = (pl.ds(0, length), pl.ds(length, part_rows))

    def gp_copy(p, k, owner, target):
        return pltpu.make_async_remote_copy(
            src_ref=gpin.at[owner, pair[p]], dst_ref=gpin.at[owner, pair[p]],
            send_sem=gp_send.at[p, k], recv_sem=gp_recv.at[p, k],
            device_id=at_dp(target), device_id_type=MESH,
        )

    def gf_copy(p, k, owner):
        return pltpu.make_async_remote_copy(
            src_ref=gpin.at[owner, pair[p]], dst_ref=gpin.at[owner, pair[p]],
            send_sem=gf_send.at[p, k], recv_sem=gf_recv.at[p, k],
            device_id=at_dp(sib), device_id_type=MESH,
        )

    def gp_start(p):
        for k in range(1, half):
            gp_copy(p, k, me, peer(k)).start()
        gp_copy(p, 0, me, sib).start()

    state_part = jnp.concatenate([b_grad, c_grad], axis=1).astype(BF16)
    gpin[me, 0:length, :] = state_part
    gp_start(0)
    step = step_s[...]
    direct = red_s[length : 2 * length, :]
    cum_grad = rows_s[...].T + red_s[0:length, :] - step * direct
    is_last = iota((length, LANES), 0) == length - 1
    cum_grad = cum_grad + jnp.where(is_last, red_s[2 * length : 2 * length + 1, :], 0.0)
    upper = later.astype(F32)
    decay_grad = jnp.dot(upper, cum_grad, precision=HIGHEST, preferred_element_type=F32)
    step_grad = direct - par[1:2, :] * decay_grad
    pre_grad = step_grad / (1.0 + jnp.exp(-pre_s[...]))
    gpin[me, length:, :] = pack(pre_grad, part_rows).astype(BF16)
    gp_start(1)
    gproj = jnp.concatenate([state_part, pre_grad.astype(BF16)], axis=1)
    for c in range(width // CHUNK):
        cs = slice(c * CHUNK, (c + 1) * CHUNK)
        ig_ref[:, cs] = mm(gproj, wall[cs, :], NT).astype(BF16)
    store_ig = pltpu.make_async_copy(ig_ref, ig_hbm, out_sem.at[1])
    store_ig.start()

    for k in range(1, dp):
        fa_copy(k).wait_recv()

    def gradient_of(index):
        steps = unpack(gpin[index, length:, :].astype(F32), length).astype(BF16)
        return mm(ftin[index], jnp.concatenate([gpin[index, 0:length, :], steps], axis=1))

    total = mm(ftin[me], gproj)
    for k in range(1, half):
        for p in range(2):
            gp_copy(p, k, source(k), peer(k)).wait_recv()
            gf_copy(p, k, source(k)).start()
        total = total + gradient_of(source(k))
    for p in range(2):
        gp_copy(p, 0, sib, sib).wait_recv()
    total = total + gradient_of(sib)
    for k in range(1, half):
        other = lax.rem(sib + dp - 2 * k, dp)
        for p in range(2):
            gf_copy(p, k, other).wait_recv()
        total = total + gradient_of(other)

    zout[0:rows, :] = total[:, 0:LANES].astype(BF16)
    zout[rows:packed, :] = pack(total[:, LANES:], share).astype(BF16)
    if owners * piece > packed:
        zout[packed:, :] = jnp.zeros((owners * piece - packed, LANES), BF16)

    def z_piece(index):
        return pl.ds(pl.multiple_of(index * piece, 16), piece)

    def to_z(k):
        return lax.rem(z + k, seq)

    def from_z(k):
        return lax.rem(z + seq - k, seq)

    def zr_copy(k):
        return pltpu.make_async_remote_copy(
            src_ref=zout.at[z_piece(to_z(k))], dst_ref=zin.at[k],
            send_sem=zr_send.at[k], recv_sem=zr_recv.at[k],
            device_id=(me, to_z(k)), device_id_type=MESH,
        )

    def za_copy(k, owner):
        return pltpu.make_async_remote_copy(
            src_ref=final.at[z_piece(owner)], dst_ref=final.at[z_piece(owner)],
            send_sem=za_send.at[k], recv_sem=za_recv.at[k],
            device_id=(me, to_z(k)), device_id_type=MESH,
        )

    owner_here = z < owners
    for k in range(1, seq):
        @pl.when(to_z(k) < owners)
        def _():
            zr_copy(k).start()

    @pl.when(owner_here)
    def _():
        mine = zout[z_piece(z), :].astype(F32)
        for k in range(1, seq):
            zr_copy(k).wait_recv()
            mine = mine + zin[k].astype(F32)
        final[z_piece(z), :] = (mine * scale).astype(BF16)
        for k in range(1, seq):
            za_copy(k, z).start()

    for k in range(1, seq):
        @pl.when(from_z(k) < owners)
        def _():
            za_copy(k, from_z(k)).wait_recv()

    bcg_ref[...] = final[0:rows, :].astype(F32)
    tail = unpack(final[rows:packed, :].astype(F32), rows)
    if padded > rows:
        tail = jnp.concatenate([tail, jnp.zeros((padded - rows, LANES), F32)], axis=0)
    dtg_ref[...] = tail.T[0:heads, 0:rows]

    store_hg.wait()
    store_ig.wait()
    ag_copy(0, me, sib).wait_send()
    for k in range(1, half):
        ag_copy(k, me, peer(k)).wait_send()
        fw_copy(k, source(k)).wait_send()
        for p in range(2):
            gp_copy(p, k, me, peer(k)).wait_send()
            gf_copy(p, k, source(k)).wait_send()
    for p in range(2):
        gp_copy(p, 0, me, sib).wait_send()
    for k in range(1, dp):
        fa_copy(k).wait_send()
    for k in range(1, seq):
        @pl.when(to_z(k) < owners)
        def _():
            zr_copy(k).wait_send()

    @pl.when(owner_here)
    def _():
        for k in range(1, seq):
            za_copy(k, z).wait_send()

    for way, final_one in ((0, last), (1, 0)):
        @pl.when(z != final_one)
        def _():
            @pl.loop(0, chunks)
            def _(c):
                chain_copy(way, c).wait_send()


def place(*refs):
    sources, targets, held, sem = refs[0:4], refs[4:8], refs[8:12], refs[12]
    slots = []
    for index, source in enumerate(sources):
        parts = 4 if source.dtype == BF16 else 1
        step = source.shape[0] // parts
        slots += [(index, slice(part * step, (part + 1) * step)) for part in range(parts)]
    loads, stores = [], []
    for slot, (index, part) in enumerate(slots):
        source, middle, target = sources[index].at[part], held[index].at[part], targets[index].at[part]
        loads.append(pltpu.make_async_copy(source, middle, sem.at[0, slot]))
        stores.append(pltpu.make_async_copy(middle, target, sem.at[1, slot]))
        loads[-1].start()
    for load, store in zip(loads, stores):
        load.wait()
        store.start()
    for store in stores:
        store.wait()


def body(dp, seq, features, head_inputs, out_grad, bc_weight, dt_weight, dt_bias, decay_rate, skip_gain):
    _, length, width = features.shape
    inner = head_inputs.shape[2]
    heads = dt_bias.shape[0]
    rows, both = bc_weight.shape
    state = both // 2
    half = dp // 2
    chunks = inner // CHUNK
    share = -(-rows // (16 * (LANES // heads))) * 16
    part_rows = -(-length // (16 * (LANES // heads))) * 16
    packed = rows + share
    piece = -(-packed // (16 * seq)) * 16
    owners = -(-packed // piece)
    scale = 1.0 / math.sqrt(dp * seq * length)
    vmem, dma = pltpu.VMEM, pltpu.SemaphoreType.DMA
    square = vmem((length, LANES), F32)
    broad = vmem((length, inner), F32)
    states = vmem((chunks, state, CHUNK), F32)
    wire = vmem((chunks, state, CHUNK), BF16)
    narrow = vmem((length, state), F32)
    scratch = dict(
        f_ref=vmem((length, width), BF16), x_ref=vmem((length, inner), BF16),
        g_ref=vmem((length, inner), BF16), in_sem=dma((3,)),
        ig_ref=vmem((length, width), BF16), hg_ref=vmem((length, inner), BF16), out_sem=dma((2,)),
        ft_s=vmem((width, length), BF16), m_s=vmem((heads, length, length), F32),
        cum_w=broad,
        wall=vmem((width, 2 * LANES), BF16), par=vmem((8, LANES), F32),
        pre_s=square, step_s=square, cum_s=square, cumt_s=square, ecum_s=square,
        toend_s=square, proj_s=square, bct_s=square, inter_s=square, rows_s=square,
        ig_acc=square,
        step_w=broad, ecum_w=broad, toend_w=broad, end_w=broad, wgrad=broad, sgrad=broad,
        left_s=states, right_s=states,
        fin=wire, bin_=wire, fout=wire, bout=wire,
        red_s=vmem((2 * length + 8, LANES), F32), bg_s=narrow, cg_s=narrow,
        hot_s=vmem((chunks, 2 * LANES, CHUNK), BF16), wpack=vmem((dp, packed, LANES), BF16),
        ftin=vmem((dp, rows, length), BF16), gpin=vmem((dp, length + part_rows, LANES), BF16),
        fa_send=dma((dp,)), fa_recv=dma((dp,)),
        zout=vmem((owners * piece, LANES), BF16), zin=vmem((seq, piece, LANES), BF16),
        final=vmem((owners * piece, LANES), BF16),
        ag_send=dma((half,)), ag_recv=dma((half,)), fw_send=dma((half,)), fw_recv=dma((half,)),
        ch_send=dma((2, chunks)), ch_recv=dma((2, chunks)),
        gp_send=dma((2, half)), gp_recv=dma((2, half)),
        gf_send=dma((2, half)), gf_recv=dma((2, half)),
        zr_send=dma((seq,)), zr_recv=dma((seq,)), za_send=dma((seq,)), za_recv=dma((seq,)),
    )
    whole = pl.BlockSpec(memory_space=pltpu.VMEM)
    results = pl.pallas_call(
        functools.partial(kernel, dp, seq, heads, scale),
        out_shape=(
            jax.ShapeDtypeStruct((length, width), BF16),
            jax.ShapeDtypeStruct((length, inner), BF16),
            jax.ShapeDtypeStruct((rows, both), F32),
            jax.ShapeDtypeStruct((heads, rows), F32),
        ),
        in_specs=[pl.BlockSpec(memory_space=pltpu.HBM)] * 3 + [whole] * 5,
        out_specs=(pl.BlockSpec(memory_space=pltpu.HBM),) * 2 + (whole,) * 2,
        scratch_shapes=scratch,
        compiler_params=pltpu.CompilerParams(
            collective_id=0, has_side_effects=True, vmem_limit_bytes=56 * 2**20
        ),
        name="mixer_backward",
    )(
        features[0], head_inputs[0], out_grad[0], bc_weight, dt_weight.T,
        dt_bias[None, :], decay_rate[None, :], skip_gain[None, :],
    )
    hbm = pl.BlockSpec(memory_space=pltpu.HBM)
    results = pl.pallas_call(
        place,
        out_shape=tuple(jax.ShapeDtypeStruct(part.shape, part.dtype) for part in results),
        in_specs=[hbm] * 4,
        out_specs=(hbm,) * 4,
        scratch_shapes=[vmem(part.shape, part.dtype) for part in results] + [dma((2, 10))],
        name="place_results",
    )(*results)
    input_grad, head_grad, bc_grad, dt_grad = results
    return input_grad[None], head_grad[None], bc_grad, dt_grad.T


def solution(mesh):
    tokens = P("dp", "seq", None)
    return jax.shard_map(
        functools.partial(body, mesh.shape["dp"], mesh.shape["seq"]),
        mesh=mesh,
        in_specs=(tokens, tokens, tokens, P("dp", None), P("dp", None), P(), P(), P()),
        out_specs=(tokens, tokens, P("dp", None), P("dp", None)),
        check_vma=False,
    )
```

```python
import functools
import math

import jax
import jax.numpy as jnp
from jax import lax
from jax.experimental import pallas as pl
from jax.experimental.pallas import tpu as pltpu
from jax.sharding import PartitionSpec as P

MESH = pl.DeviceIdType.MESH
F32, BF16 = jnp.float32, jnp.bfloat16
LANES = 128
CHUNK = 512
HIGHEST = lax.Precision.HIGHEST
NT = (((1,), (1,)), ((), ()))
TN = (((0,), (0,)), ((), ()))


def halves(value):
    high = value.astype(BF16)
    return high, (value - high.astype(F32)).astype(BF16)


def mm(left, right, dims=None):
    if dims is None:
        return jnp.dot(left, right, preferred_element_type=F32)
    return lax.dot_general(left, right, dims, preferred_element_type=F32)


def iota(shape, dim):
    return lax.broadcasted_iota(jnp.int32, shape, dim)


def kernel(
    dp, seq, heads, scale,
    f_hbm, x_hbm, g_hbm, wbc_ref, wdt_ref, bias_ref, decay_ref, skip_ref,
    ig_hbm, hg_hbm, bcg_ref, dtg_ref, *,
    ig_ref, hg_ref, out_sem,
    f_ref, x_ref, g_ref, in_sem, ft_s, m_s, cum_w, hot_s, wpack, ftin, gpin, fa_send, fa_recv,
    wall, par, pre_s, step_s, cum_s, cumt_s, ecum_s, toend_s, proj_s, bct_s, inter_s, rows_s,
    ig_acc, step_w, ecum_w, toend_w, end_w, wgrad, sgrad, left_s, right_s,
    fin, bin_, fout, bout, red_s, bg_s, cg_s,
    zout, zin, final,
    ag_send, ag_recv, fw_send, fw_recv, ch_send, ch_recv,
    gp_send, gp_recv, gf_send, gf_recv, zr_send, zr_recv, za_send, za_recv,
):
    me, z = lax.axis_index("dp"), lax.axis_index("seq")
    last = seq - 1
    half = dp // 2
    sib = me + 1 - 2 * lax.rem(me, 2)
    length, inner = x_ref.shape
    width = f_ref.shape[1]
    rows = wbc_ref.shape[0]
    state = wbc_ref.shape[1] // 2
    head_size = inner // heads
    chunks = inner // CHUNK
    groups = LANES // heads
    share = -(-rows // (16 * groups)) * 16
    packed = rows + share
    piece = -(-packed // (16 * seq)) * 16
    owners = -(-packed // piece)

    part_rows = -(-length // (16 * groups)) * 16

    def pack(value, each):
        value = jnp.where(iota(value.shape, 1) < heads, value, 0.0)
        parts = []
        for g in range(groups):
            part = value[g * each : min((g + 1) * each, value.shape[0]), :]
            if part.shape[0] < each:
                empty = jnp.zeros((each - part.shape[0], LANES), F32)
                part = jnp.concatenate([part, empty], axis=0)
            parts.append(pltpu.roll(part, g * heads, 1) if g else part)
        return sum(parts[1:], parts[0])

    def unpack(value, count):
        each = value.shape[0]
        parts = []
        for g in range(groups):
            part = pltpu.roll(value, LANES - g * heads, 1) if g else value
            parts.append(part[0 : min(each, count - g * each), :])
        return jnp.concatenate(parts, axis=0)

    def at_dp(target):
        return (target, z)

    def peer(k):
        return lax.rem(me + 2 * k, dp)

    def source(k):
        return lax.rem(me + dp - 2 * k, dp)

    loads = [
        pltpu.make_async_copy(src, dst, in_sem.at[i])
        for i, (src, dst) in enumerate(((x_hbm, x_ref), (g_hbm, g_ref), (f_hbm, f_ref)))
    ]
    for load in loads:
        load.start()
    barrier = pltpu.get_barrier_semaphore()
    for k in range(1, dp):
        pl.semaphore_signal(
            barrier, inc=1, device_id=at_dp(lax.rem(me + k, dp)), device_id_type=MESH
        )
    for k in range(1, seq):
        pl.semaphore_signal(barrier, inc=1, device_id=(me, lax.rem(z + k, seq)), device_id_type=MESH)

    def block(index):
        return pl.ds(pl.multiple_of(index * rows, 16), rows)

    wpack[me, 0:rows, :] = wbc_ref[...]
    padded = -(-rows // LANES) * LANES
    wide = jnp.concatenate(
        [wdt_ref[...].astype(F32), jnp.zeros((LANES - heads, rows), F32)], axis=0
    )
    if padded > rows:
        wide = jnp.concatenate([wide, jnp.zeros((LANES, padded - rows), F32)], axis=1)
    wpack[me, rows:, :] = pack(wide.T[0:rows, :], share).astype(BF16)
    par[...] = jnp.zeros_like(par)
    par[0:1, 0:heads] = bias_ref[...]
    par[1:2, 0:heads] = decay_ref[...]
    par[2:3, 0:heads] = skip_ref[...]
    pl.semaphore_wait(barrier, dp + seq - 2)

    def ag_copy(k, owner, target):
        return pltpu.make_async_remote_copy(
            src_ref=wpack.at[owner], dst_ref=wpack.at[owner],
            send_sem=ag_send.at[k], recv_sem=ag_recv.at[k],
            device_id=at_dp(target), device_id_type=MESH,
        )

    def fw_copy(k, owner):
        return pltpu.make_async_remote_copy(
            src_ref=wpack.at[owner], dst_ref=wpack.at[owner],
            send_sem=fw_send.at[k], recv_sem=fw_recv.at[k],
            device_id=at_dp(sib), device_id_type=MESH,
        )

    for k in range(1, half):
        ag_copy(k, me, peer(k)).start()
    ag_copy(0, me, sib).start()
    for load in loads:
        load.wait()

    low_half = iota((length, LANES), 1) < head_size
    per_tile = LANES // head_size
    tile_count = inner // LANES

    def early_work(tile):
        ts = slice(tile * LANES, (tile + 1) * LANES)
        x_tile, g_full = x_ref[:, ts].astype(F32), g_ref[:, ts]
        for part in range(per_tile):
            mine = low_half if part == 0 else jnp.logical_not(low_half)
            x_part = jnp.where(mine, x_tile, 0.0).astype(BF16)
            m_s[tile * per_tile + part] = mm(x_part, g_full, NT)

    @pl.loop(0, width // CHUNK)
    def _(c):
        cs = pl.ds(pl.multiple_of(c * CHUNK, CHUNK), CHUNK)
        ft_s[cs, :] = f_ref[:, cs].T

    @pl.loop(0, chunks)
    def _(c):
        lane = c * CHUNK + iota((LANES, CHUNK), 1)
        hot = (iota((LANES, CHUNK), 0) == lane // head_size).astype(F32).astype(BF16)
        hot_s[c, 0:LANES, :] = hot
        hot_s[c, LANES:, :] = hot

    for k in range(1, half):
        for tile in range(tile_count * (k - 1) // (half - 1), tile_count * k // (half - 1)):
            early_work(tile)
        ag_copy(k, source(k), peer(k)).wait_recv()
        fw_copy(k, source(k)).start()
    ag_copy(0, sib, sib).wait_recv()
    for k in range(1, half):
        fw_copy(k, lax.rem(sib + dp - 2 * k, dp)).wait_recv()

    def fa_copy(k):
        target = lax.rem(me + k, dp)
        return pltpu.make_async_remote_copy(
            src_ref=ft_s.at[block(target)], dst_ref=ftin.at[me],
            send_sem=fa_send.at[k], recv_sem=fa_recv.at[k],
            device_id=at_dp(target), device_id_type=MESH,
        )

    for k in range(1, dp):
        fa_copy(k).start()
    ftin[me] = ft_s[block(me), :]

    @pl.loop(0, dp, unroll=4)
    def _(i):
        wall[block(i), 0:LANES] = wpack[i, 0:rows, :]
        wall[block(i), LANES:] = unpack(wpack[i, rows:, :].astype(F32), rows).astype(BF16)

    projection = mm(f_ref[...], wall[...])
    proj_s[...] = projection[:, :LANES]
    pre = projection[:, LANES:] + par[0:1, :]
    pre_s[...] = pre
    step = jnp.maximum(pre, 0.0) + jnp.log1p(jnp.exp(-jnp.abs(pre)))
    step_s[...] = step
    lower = (iota((length, length), 0) >= iota((length, length), 1)).astype(F32)
    cum = jnp.dot(
        lower, -par[1:2, :] * step, precision=HIGHEST, preferred_element_type=F32
    )
    cum_s[...] = cum
    cumt_s[...] = cum.T
    ecum_s[...] = jnp.exp(cum)
    toend_s[...] = jnp.exp(cum[length - 1 :, :] - cum)
    bct_s[...] = proj_s[...].T
    bt = bct_s[0:state, :]
    ct = bct_s[state:, :]
    bt_hi, bt_lo = halves(bt)
    ct_hi, ct_lo = halves(ct)
    bt3 = jnp.concatenate([bt_hi, bt_lo, bt_hi], axis=1)
    ct3 = jnp.concatenate([ct_hi, ct_lo, ct_hi], axis=1)
    b_rows = proj_s[:, 0:state]
    c_rows = proj_s[:, state:]
    inter_s[...] = jnp.dot(b_rows, ct, precision=HIGHEST, preferred_element_type=F32)

    def spread(value, c, exact=False):
        high, low = halves(value)
        result = mm(jnp.concatenate([high, low], axis=1), hot_s[c])
        if exact:
            rest = value - high.astype(F32) - low.astype(F32)
            result = result + mm(rest.astype(BF16), hot_s[c, 0:LANES, :])
        return result

    def lanes(c):
        if isinstance(c, int):
            return slice(c * CHUNK, (c + 1) * CHUNK)
        return pl.ds(pl.multiple_of(c * CHUNK, CHUNK), CHUNK)

    def chain_copy(way, c):
        src, dst = ((fout, fin), (bout, bin_))[way]
        to = (z + 1, z + last)[way]
        return pltpu.make_async_remote_copy(
            src_ref=src.at[c], dst_ref=dst.at[c],
            send_sem=ch_send.at[way, c], recv_sem=ch_recv.at[way, c],
            device_id=(me, lax.rem(to, seq)), device_id_type=MESH,
        )

    def local_work(c):
        cs = lanes(c)
        step_c = spread(step_s[...], c)
        ecum_c = spread(ecum_s[...], c)
        toend_c = spread(toend_s[...], c)
        ends = x_ref[:, cs].astype(F32) * step_c * toend_c
        weighted = g_ref[:, cs].astype(F32) * ecum_c
        step_w[:, cs] = step_c
        ecum_w[:, cs] = ecum_c
        toend_w[:, cs] = toend_c
        cum_w[:, cs] = spread(cum_s[...], c, exact=True)
        end_w[:, cs] = ends
        wgrad[:, cs] = weighted
        e_hi, e_lo = halves(ends)
        w_hi, w_lo = halves(weighted)
        left_s[c] = mm(bt3, jnp.concatenate([e_hi, e_hi, e_lo], axis=0))
        right_s[c] = mm(ct3, jnp.concatenate([w_hi, w_hi, w_lo], axis=0))

    def chain_start(c):
        for way, first in ((0, 0), (1, last)):
            @pl.when(z == first)
            def _():
                arrived, leaving, here = ((fin, fout, left_s), (bin_, bout, right_s))[way]
                arrived[c] = jnp.zeros((state, CHUNK), BF16)
                if seq > 1:
                    leaving[c] = here[c].astype(BF16)
                    chain_copy(way, c).start()

    def chain_hop(way, c):
        arrived, leaving, local = ((fin, fout, left_s), (bin_, bout, right_s))[way]
        chain_copy(way, c).wait_recv()

        @pl.when(z != (last, 0)[way])
        def _():
            decay = ecum_w[length - 1 :, lanes(c)]
            leaving[c] = (arrived[c].astype(F32) * decay + local[c]).astype(BF16)
            chain_copy(way, c).start()

    later = iota((length, length), 1) >= iota((length, length), 0)
    def by_head(tile):
        turned = pltpu.roll(tile, head_size, 1)
        return jnp.where(low_half, tile, turned), jnp.where(low_half, turned, tile)

    def tile_work(tile):
        ts = slice(tile * LANES, (tile + 1) * LANES)
        g_tile = g_ref[:, ts].astype(F32)
        inter = inter_s[...]
        cums, steps = by_head(cum_w[:, ts]), by_head(step_w[:, ts])
        mixes, grads, sums = [], [], []
        for part in range(per_tile):
            head = tile * per_tile + part
            gap = cumt_s[head : head + 1, :] - cums[part]
            weights = jnp.exp(jnp.where(later, gap, -1e30))
            mine = low_half if part == 0 else jnp.logical_not(low_half)
            g_part = jnp.where(mine, g_tile, 0.0).astype(BF16)
            shared = m_s[head] * steps[part] * weights
            sums.append(shared)
            rows_s[head : head + 1, :] = jnp.sum(shared * inter, axis=0, keepdims=True)
            mixes += list(halves(inter * weights))
            grads += [g_part, g_part]
        ig_acc[...] += sum(sums[1:], sums[0])
        sgrad[:, ts] = mm(jnp.concatenate(mixes, axis=1), jnp.concatenate(grads, axis=0))

    def reduce_heads(value, c):
        hot = hot_s[c, 0:LANES, :]
        high, low = halves(value)
        return mm(high, hot, NT) + mm(low, hot, NT)

    b_hi, b_lo = halves(b_rows)
    c_hi, c_lo = halves(c_rows)
    bpair = jnp.concatenate([b_hi, b_lo], axis=1)
    cpair = jnp.concatenate([c_hi, c_lo], axis=1)

    def carried_work(c):
        cs = lanes(c)
        state_in, state_grad = fin[c], bin_[c]
        weighted, ends = wgrad[:, cs], end_w[:, cs]
        inter_out = mm(cpair, jnp.concatenate([state_in, state_in], axis=0))
        reach = mm(bpair, jnp.concatenate([state_grad, state_grad], axis=0))
        w_hi, w_lo = halves(weighted)
        e_hi, e_lo = halves(ends)
        cg_s[...] += mm(w_hi, state_in, NT) + mm(w_lo, state_in, NT)
        bg_s[...] += mm(e_hi, state_grad, NT) + mm(e_lo, state_grad, NT)
        total = sgrad[:, cs] + toend_w[:, cs] * reach
        x_part, g_part = x_ref[:, cs].astype(F32), g_ref[:, cs].astype(F32)
        decay = ecum_w[length - 1 :, cs]
        product = state_grad.astype(F32) * state_in.astype(F32)
        at_end = jnp.sum(ends * reach, axis=0, keepdims=True) + decay * jnp.sum(
            product, axis=0, keepdims=True
        )
        stacked = jnp.concatenate(
            [weighted * inter_out, x_part * total, jnp.broadcast_to(at_end, (8, CHUNK))], axis=0
        )
        red_s[...] += reduce_heads(stacked, c)
        skip_c = spread(jnp.broadcast_to(par[2:3, :], (8, LANES)), c)[0:1, :]
        hg_ref[:, cs] = (g_part * skip_c + step_w[:, cs] * total).astype(BF16)

    ig_acc[...] = jnp.zeros_like(ig_acc)
    rows_s[...] = jnp.zeros_like(rows_s)
    cg_s[...] = jnp.zeros_like(cg_s)
    bg_s[...] = jnp.zeros_like(bg_s)
    red_s[...] = jnp.zeros_like(red_s)
    tiles = CHUNK // LANES

    for c in range(chunks):
        local_work(c)
        chain_start(c)

    steps = chunks + last
    budget = -(-(chunks * tiles + 2 * chunks) // steps)
    done = 0
    for s in range(steps):
        due = budget if s < last else max(budget - 2, 0)
        if s == steps - 1:
            due = chunks * tiles
        for tile in range(done, min(done + due, chunks * tiles)):
            tile_work(tile)
        done = min(done + due, chunks * tiles)
        if s >= last:
            carried_work(s - last)
        if seq > 1 and s < steps - 1:
            forward, back = s - (z - 1), s - (last - 1 - z)

            @pl.when(jnp.logical_and(z > 0, jnp.logical_and(forward >= 0, forward < chunks)))
            def _():
                chain_hop(0, forward)

            @pl.when(jnp.logical_and(z < last, jnp.logical_and(back >= 0, back < chunks)))
            def _():
                chain_hop(1, back)

    store_hg = pltpu.make_async_copy(hg_ref, hg_hbm, out_sem.at[0])
    store_hg.start()
    acc = ig_acc[...]
    c_grad = cg_s[...] + lax.dot_general(
        acc, b_rows, TN, precision=HIGHEST, preferred_element_type=F32
    )
    b_grad = bg_s[...] + jnp.dot(acc, c_rows, precision=HIGHEST, preferred_element_type=F32)
    pair = (pl.ds(0, length), pl.ds(length, part_rows))

    def gp_copy(p, k, owner, target):
        return pltpu.make_async_remote_copy(
            src_ref=gpin.at[owner, pair[p]], dst_ref=gpin.at[owner, pair[p]],
            send_sem=gp_send.at[p, k], recv_sem=gp_recv.at[p, k],
            device_id=at_dp(target), device_id_type=MESH,
        )

    def gf_copy(p, k, owner):
        return pltpu.make_async_remote_copy(
            src_ref=gpin.at[owner, pair[p]], dst_ref=gpin.at[owner, pair[p]],
            send_sem=gf_send.at[p, k], recv_sem=gf_recv.at[p, k],
            device_id=at_dp(sib), device_id_type=MESH,
        )

    def gp_start(p):
        for k in range(1, half):
            gp_copy(p, k, me, peer(k)).start()
        gp_copy(p, 0, me, sib).start()

    state_part = jnp.concatenate([b_grad, c_grad], axis=1).astype(BF16)
    gpin[me, 0:length, :] = state_part
    gp_start(0)
    step = step_s[...]
    direct = red_s[length : 2 * length, :]
    cum_grad = rows_s[...].T + red_s[0:length, :] - step * direct
    is_last = iota((length, LANES), 0) == length - 1
    cum_grad = cum_grad + jnp.where(is_last, red_s[2 * length : 2 * length + 1, :], 0.0)
    upper = later.astype(F32)
    decay_grad = jnp.dot(upper, cum_grad, precision=HIGHEST, preferred_element_type=F32)
    step_grad = direct - par[1:2, :] * decay_grad
    pre_grad = step_grad / (1.0 + jnp.exp(-pre_s[...]))
    gpin[me, length:, :] = pack(pre_grad, part_rows).astype(BF16)
    gp_start(1)
    gproj = jnp.concatenate([state_part, pre_grad.astype(BF16)], axis=1)
    for c in range(width // CHUNK):
        cs = slice(c * CHUNK, (c + 1) * CHUNK)
        ig_ref[:, cs] = mm(gproj, wall[cs, :], NT).astype(BF16)
    store_ig = pltpu.make_async_copy(ig_ref, ig_hbm, out_sem.at[1])
    store_ig.start()

    for k in range(1, dp):
        fa_copy(k).wait_recv()

    def gradient_of(index):
        steps = unpack(gpin[index, length:, :].astype(F32), length).astype(BF16)
        return mm(ftin[index], jnp.concatenate([gpin[index, 0:length, :], steps], axis=1))

    total = mm(ftin[me], gproj)
    for k in range(1, half):
        for p in range(2):
            gp_copy(p, k, source(k), peer(k)).wait_recv()
            gf_copy(p, k, source(k)).start()
        total = total + gradient_of(source(k))
    for p in range(2):
        gp_copy(p, 0, sib, sib).wait_recv()
    total = total + gradient_of(sib)
    for k in range(1, half):
        other = lax.rem(sib + dp - 2 * k, dp)
        for p in range(2):
            gf_copy(p, k, other).wait_recv()
        total = total + gradient_of(other)

    zout[0:rows, :] = total[:, 0:LANES].astype(BF16)
    zout[rows:packed, :] = pack(total[:, LANES:], share).astype(BF16)
    if owners * piece > packed:
        zout[packed:, :] = jnp.zeros((owners * piece - packed, LANES), BF16)

    def z_piece(index):
        return pl.ds(pl.multiple_of(index * piece, 16), piece)

    def to_z(k):
        return lax.rem(z + k, seq)

    def from_z(k):
        return lax.rem(z + seq - k, seq)

    def zr_copy(k):
        return pltpu.make_async_remote_copy(
            src_ref=zout.at[z_piece(to_z(k))], dst_ref=zin.at[k],
            send_sem=zr_send.at[k], recv_sem=zr_recv.at[k],
            device_id=(me, to_z(k)), device_id_type=MESH,
        )

    def za_copy(k, owner):
        return pltpu.make_async_remote_copy(
            src_ref=final.at[z_piece(owner)], dst_ref=final.at[z_piece(owner)],
            send_sem=za_send.at[k], recv_sem=za_recv.at[k],
            device_id=(me, to_z(k)), device_id_type=MESH,
        )

    owner_here = z < owners
    for k in range(1, seq):
        @pl.when(to_z(k) < owners)
        def _():
            zr_copy(k).start()

    @pl.when(owner_here)
    def _():
        mine = zout[z_piece(z), :].astype(F32)
        for k in range(1, seq):
            zr_copy(k).wait_recv()
            mine = mine + zin[k].astype(F32)
        final[z_piece(z), :] = (mine * scale).astype(BF16)
        for k in range(1, seq):
            za_copy(k, z).start()

    for k in range(1, seq):
        @pl.when(from_z(k) < owners)
        def _():
            za_copy(k, from_z(k)).wait_recv()

    bcg_ref[...] = final[0:rows, :].astype(F32)
    tail = unpack(final[rows:packed, :].astype(F32), rows)
    if padded > rows:
        tail = jnp.concatenate([tail, jnp.zeros((padded - rows, LANES), F32)], axis=0)
    dtg_ref[...] = tail.T[0:heads, 0:rows]

    store_hg.wait()
    store_ig.wait()
    ag_copy(0, me, sib).wait_send()
    for k in range(1, half):
        ag_copy(k, me, peer(k)).wait_send()
        fw_copy(k, source(k)).wait_send()
        for p in range(2):
            gp_copy(p, k, me, peer(k)).wait_send()
            gf_copy(p, k, source(k)).wait_send()
    for p in range(2):
        gp_copy(p, 0, me, sib).wait_send()
    for k in range(1, dp):
        fa_copy(k).wait_send()
    for k in range(1, seq):
        @pl.when(to_z(k) < owners)
        def _():
            zr_copy(k).wait_send()

    @pl.when(owner_here)
    def _():
        for k in range(1, seq):
            za_copy(k, z).wait_send()

    for way, final_one in ((0, last), (1, 0)):
        @pl.when(z != final_one)
        def _():
            @pl.loop(0, chunks)
            def _(c):
                chain_copy(way, c).wait_send()


def place(*refs):
    sources, targets, held, sem = refs[0:4], refs[4:8], refs[8:12], refs[12]
    slots = []
    for index, source in enumerate(sources):
        parts = 4 if source.dtype == BF16 else 1
        step = source.shape[0] // parts
        slots += [(index, slice(part * step, (part + 1) * step)) for part in range(parts)]
    loads, stores = [], []
    for slot, (index, part) in enumerate(slots):
        source, middle, target = sources[index].at[part], held[index].at[part], targets[index].at[part]
        loads.append(pltpu.make_async_copy(source, middle, sem.at[0, slot]))
        stores.append(pltpu.make_async_copy(middle, target, sem.at[1, slot]))
        loads[-1].start()
    for load, store in zip(loads, stores):
        load.wait()
        store.start()
    for store in stores:
        store.wait()


def body(dp, seq, features, head_inputs, out_grad, bc_weight, dt_weight, dt_bias, decay_rate, skip_gain):
    _, length, width = features.shape
    inner = head_inputs.shape[2]
    heads = dt_bias.shape[0]
    rows, both = bc_weight.shape
    state = both // 2
    half = dp // 2
    chunks = inner // CHUNK
    share = -(-rows // (16 * (LANES // heads))) * 16
    part_rows = -(-length // (16 * (LANES // heads))) * 16
    packed = rows + share
    piece = -(-packed // (16 * seq)) * 16
    owners = -(-packed // piece)
    scale = 1.0 / math.sqrt(dp * seq * length)
    vmem, dma = pltpu.VMEM, pltpu.SemaphoreType.DMA
    square = vmem((length, LANES), F32)
    broad = vmem((length, inner), F32)
    states = vmem((chunks, state, CHUNK), F32)
    wire = vmem((chunks, state, CHUNK), BF16)
    narrow = vmem((length, state), F32)
    scratch = dict(
        f_ref=vmem((length, width), BF16), x_ref=vmem((length, inner), BF16),
        g_ref=vmem((length, inner), BF16), in_sem=dma((3,)),
        ig_ref=vmem((length, width), BF16), hg_ref=vmem((length, inner), BF16), out_sem=dma((2,)),
        ft_s=vmem((width, length), BF16), m_s=vmem((heads, length, length), F32),
        cum_w=broad,
        wall=vmem((width, 2 * LANES), BF16), par=vmem((8, LANES), F32),
        pre_s=square, step_s=square, cum_s=square, cumt_s=square, ecum_s=square,
        toend_s=square, proj_s=square, bct_s=square, inter_s=square, rows_s=square,
        ig_acc=square,
        step_w=broad, ecum_w=broad, toend_w=broad, end_w=broad, wgrad=broad, sgrad=broad,
        left_s=states, right_s=states,
        fin=wire, bin_=wire, fout=wire, bout=wire,
        red_s=vmem((2 * length + 8, LANES), F32), bg_s=narrow, cg_s=narrow,
        hot_s=vmem((chunks, 2 * LANES, CHUNK), BF16), wpack=vmem((dp, packed, LANES), BF16),
        ftin=vmem((dp, rows, length), BF16), gpin=vmem((dp, length + part_rows, LANES), BF16),
        fa_send=dma((dp,)), fa_recv=dma((dp,)),
        zout=vmem((owners * piece, LANES), BF16), zin=vmem((seq, piece, LANES), BF16),
        final=vmem((owners * piece, LANES), BF16),
        ag_send=dma((half,)), ag_recv=dma((half,)), fw_send=dma((half,)), fw_recv=dma((half,)),
        ch_send=dma((2, chunks)), ch_recv=dma((2, chunks)),
        gp_send=dma((2, half)), gp_recv=dma((2, half)),
        gf_send=dma((2, half)), gf_recv=dma((2, half)),
        zr_send=dma((seq,)), zr_recv=dma((seq,)), za_send=dma((seq,)), za_recv=dma((seq,)),
    )
    whole = pl.BlockSpec(memory_space=pltpu.VMEM)
    results = pl.pallas_call(
        functools.partial(kernel, dp, seq, heads, scale),
        out_shape=(
            jax.ShapeDtypeStruct((length, width), BF16),
            jax.ShapeDtypeStruct((length, inner), BF16),
            jax.ShapeDtypeStruct((rows, both), F32),
            jax.ShapeDtypeStruct((heads, rows), F32),
        ),
        in_specs=[pl.BlockSpec(memory_space=pltpu.HBM)] * 3 + [whole] * 5,
        out_specs=(pl.BlockSpec(memory_space=pltpu.HBM),) * 2 + (whole,) * 2,
        scratch_shapes=scratch,
        compiler_params=pltpu.CompilerParams(
            collective_id=0, has_side_effects=True, vmem_limit_bytes=56 * 2**20
        ),
        name="mixer_backward",
    )(
        features[0], head_inputs[0], out_grad[0], bc_weight, dt_weight.T,
        dt_bias[None, :], decay_rate[None, :], skip_gain[None, :],
    )
    hbm = pl.BlockSpec(memory_space=pltpu.HBM)
    results = pl.pallas_call(
        place,
        out_shape=tuple(jax.ShapeDtypeStruct(part.shape, part.dtype) for part in results),
        in_specs=[hbm] * 4,
        out_specs=(hbm,) * 4,
        scratch_shapes=[vmem(part.shape, part.dtype) for part in results] + [dma((2, 10))],
        name="place_results",
    )(*results)
    input_grad, head_grad, bc_grad, dt_grad = results
    return input_grad[None], head_grad[None], bc_grad, dt_grad.T


def solution(mesh):
    tokens = P("dp", "seq", None)
    return jax.shard_map(
        functools.partial(body, mesh.shape["dp"], mesh.shape["seq"]),
        mesh=mesh,
        in_specs=(tokens, tokens, tokens, P("dp", None), P("dp", None), P(), P(), P()),
        out_specs=(tokens, tokens, P("dp", None), P("dp", None)),
        check_vma=False,
    )
```

```python
import functools
import math

import jax
import jax.numpy as jnp
from jax import lax
from jax.experimental import pallas as pl
from jax.experimental.pallas import tpu as pltpu
from jax.sharding import PartitionSpec as P

MESH = pl.DeviceIdType.MESH
F32, BF16 = jnp.float32, jnp.bfloat16
LANES = 128
CHUNK = 512
HIGHEST = lax.Precision.HIGHEST
NT = (((1,), (1,)), ((), ()))
TN = (((0,), (0,)), ((), ()))


def halves(value):
    high = value.astype(BF16)
    return high, (value - high.astype(F32)).astype(BF16)


def mm(left, right, dims=None):
    if dims is None:
        return jnp.dot(left, right, preferred_element_type=F32)
    return lax.dot_general(left, right, dims, preferred_element_type=F32)


def iota(shape, dim):
    return lax.broadcasted_iota(jnp.int32, shape, dim)


def kernel(
    dp, seq, heads, scale,
    f_hbm, x_hbm, g_hbm, wbc_ref, wdt_ref, bias_ref, decay_ref, skip_ref,
    ig_hbm, hg_hbm, bcg_ref, dtg_ref, *,
    ig_ref, hg_ref, out_sem,
    f_ref, x_ref, g_ref, in_sem, ft_s, m_s, cum_w, hot_s, wpack, ftin, gpin, fa_send, fa_recv,
    wall, par, pre_s, step_s, cum_s, cumt_s, ecum_s, toend_s, proj_s, bct_s, inter_s, rows_s,
    ig_acc, step_w, ecum_w, toend_w, end_w, wgrad, sgrad, left_s, right_s,
    fin, bin_, fout, bout, red_s, bg_s, cg_s,
    zout, zin, final,
    ag_send, ag_recv, fw_send, fw_recv, ch_send, ch_recv,
    gp_send, gp_recv, gf_send, gf_recv, zr_send, zr_recv, za_send, za_recv,
):
    me, z = lax.axis_index("dp"), lax.axis_index("seq")
    last = seq - 1
    half = dp // 2
    sib = me + 1 - 2 * lax.rem(me, 2)
    length, inner = x_ref.shape
    width = f_ref.shape[1]
    rows = wbc_ref.shape[0]
    state = wbc_ref.shape[1] // 2
    head_size = inner // heads
    chunks = inner // CHUNK
    groups = LANES // heads
    share = -(-rows // (16 * groups)) * 16
    packed = rows + share
    piece = -(-packed // (16 * seq)) * 16
    owners = -(-packed // piece)

    part_rows = -(-length // (16 * groups)) * 16

    def pack(value, each):
        value = jnp.where(iota(value.shape, 1) < heads, value, 0.0)
        parts = []
        for g in range(groups):
            part = value[g * each : min((g + 1) * each, value.shape[0]), :]
            if part.shape[0] < each:
                empty = jnp.zeros((each - part.shape[0], LANES), F32)
                part = jnp.concatenate([part, empty], axis=0)
            parts.append(pltpu.roll(part, g * heads, 1) if g else part)
        return sum(parts[1:], parts[0])

    def unpack(value, count):
        each = value.shape[0]
        parts = []
        for g in range(groups):
            part = pltpu.roll(value, LANES - g * heads, 1) if g else value
            parts.append(part[0 : min(each, count - g * each), :])
        return jnp.concatenate(parts, axis=0)

    def at_dp(target):
        return (target, z)

    def peer(k):
        return lax.rem(me + 2 * k, dp)

    def source(k):
        return lax.rem(me + dp - 2 * k, dp)

    loads = [
        pltpu.make_async_copy(src, dst, in_sem.at[i])
        for i, (src, dst) in enumerate(((x_hbm, x_ref), (g_hbm, g_ref), (f_hbm, f_ref)))
    ]
    for load in loads:
        load.start()
    barrier = pltpu.get_barrier_semaphore()
    for k in range(1, dp):
        pl.semaphore_signal(
            barrier, inc=1, device_id=at_dp(lax.rem(me + k, dp)), device_id_type=MESH
        )
    for k in range(1, seq):
        pl.semaphore_signal(barrier, inc=1, device_id=(me, lax.rem(z + k, seq)), device_id_type=MESH)

    def block(index):
        return pl.ds(pl.multiple_of(index * rows, 16), rows)

    wpack[me, 0:rows, :] = wbc_ref[...]
    padded = -(-rows // LANES) * LANES
    wide = jnp.concatenate(
        [wdt_ref[...].astype(F32), jnp.zeros((LANES - heads, rows), F32)], axis=0
    )
    if padded > rows:
        wide = jnp.concatenate([wide, jnp.zeros((LANES, padded - rows), F32)], axis=1)
    wpack[me, rows:, :] = pack(wide.T[0:rows, :], share).astype(BF16)
    par[...] = jnp.zeros_like(par)
    par[0:1, 0:heads] = bias_ref[...]
    par[1:2, 0:heads] = decay_ref[...]
    par[2:3, 0:heads] = skip_ref[...]
    pl.semaphore_wait(barrier, dp + seq - 2)

    def ag_copy(k, owner, target):
        return pltpu.make_async_remote_copy(
            src_ref=wpack.at[owner], dst_ref=wpack.at[owner],
            send_sem=ag_send.at[k], recv_sem=ag_recv.at[k],
            device_id=at_dp(target), device_id_type=MESH,
        )

    def fw_copy(k, owner):
        return pltpu.make_async_remote_copy(
            src_ref=wpack.at[owner], dst_ref=wpack.at[owner],
            send_sem=fw_send.at[k], recv_sem=fw_recv.at[k],
            device_id=at_dp(sib), device_id_type=MESH,
        )

    for k in range(1, half):
        ag_copy(k, me, peer(k)).start()
    ag_copy(0, me, sib).start()
    for load in loads:
        load.wait()

    low_half = iota((length, LANES), 1) < head_size
    per_tile = LANES // head_size
    tile_count = inner // LANES

    def early_work(tile):
        ts = slice(tile * LANES, (tile + 1) * LANES)
        x_tile, g_full = x_ref[:, ts].astype(F32), g_ref[:, ts]
        for part in range(per_tile):
            mine = low_half if part == 0 else jnp.logical_not(low_half)
            x_part = jnp.where(mine, x_tile, 0.0).astype(BF16)
            m_s[tile * per_tile + part] = mm(x_part, g_full, NT)

    @pl.loop(0, width // CHUNK)
    def _(c):
        cs = pl.ds(pl.multiple_of(c * CHUNK, CHUNK), CHUNK)
        ft_s[cs, :] = f_ref[:, cs].T

    @pl.loop(0, chunks)
    def _(c):
        lane = c * CHUNK + iota((LANES, CHUNK), 1)
        hot = (iota((LANES, CHUNK), 0) == lane // head_size).astype(F32).astype(BF16)
        hot_s[c, 0:LANES, :] = hot
        hot_s[c, LANES:, :] = hot

    for k in range(1, half):
        for tile in range(tile_count * (k - 1) // (half - 1), tile_count * k // (half - 1)):
            early_work(tile)
        ag_copy(k, source(k), peer(k)).wait_recv()
        fw_copy(k, source(k)).start()
    ag_copy(0, sib, sib).wait_recv()
    for k in range(1, half):
        fw_copy(k, lax.rem(sib + dp - 2 * k, dp)).wait_recv()

    def fa_copy(k):
        target = lax.rem(me + k, dp)
        return pltpu.make_async_remote_copy(
            src_ref=ft_s.at[block(target)], dst_ref=ftin.at[me],
            send_sem=fa_send.at[k], recv_sem=fa_recv.at[k],
            device_id=at_dp(target), device_id_type=MESH,
        )

    for k in range(1, dp):
        fa_copy(k).start()
    ftin[me] = ft_s[block(me), :]

    @pl.loop(0, dp, unroll=4)
    def _(i):
        wall[block(i), 0:LANES] = wpack[i, 0:rows, :]
        wall[block(i), LANES:] = unpack(wpack[i, rows:, :].astype(F32), rows).astype(BF16)

    projection = mm(f_ref[...], wall[...])
    proj_s[...] = projection[:, :LANES]
    pre = projection[:, LANES:] + par[0:1, :]
    pre_s[...] = pre
    step = jnp.maximum(pre, 0.0) + jnp.log1p(jnp.exp(-jnp.abs(pre)))
    step_s[...] = step
    lower = (iota((length, length), 0) >= iota((length, length), 1)).astype(F32)
    cum = jnp.dot(
        lower, -par[1:2, :] * step, precision=HIGHEST, preferred_element_type=F32
    )
    cum_s[...] = cum
    cumt_s[...] = cum.T
    ecum_s[...] = jnp.exp(cum)
    toend_s[...] = jnp.exp(cum[length - 1 :, :] - cum)
    bct_s[...] = proj_s[...].T
    bt = bct_s[0:state, :]
    ct = bct_s[state:, :]
    bt_hi, bt_lo = halves(bt)
    ct_hi, ct_lo = halves(ct)
    bt3 = jnp.concatenate([bt_hi, bt_lo, bt_hi], axis=1)
    ct3 = jnp.concatenate([ct_hi, ct_lo, ct_hi], axis=1)
    b_rows = proj_s[:, 0:state]
    c_rows = proj_s[:, state:]
    inter_s[...] = jnp.dot(b_rows, ct, precision=HIGHEST, preferred_element_type=F32)

    def spread(value, c, exact=False):
        high, low = halves(value)
        result = mm(jnp.concatenate([high, low], axis=1), hot_s[c])
        if exact:
            rest = value - high.astype(F32) - low.astype(F32)
            result = result + mm(rest.astype(BF16), hot_s[c, 0:LANES, :])
        return result

    def lanes(c):
        if isinstance(c, int):
            return slice(c * CHUNK, (c + 1) * CHUNK)
        return pl.ds(pl.multiple_of(c * CHUNK, CHUNK), CHUNK)

    def chain_copy(way, c):
        src, dst = ((fout, fin), (bout, bin_))[way]
        to = (z + 1, z + last)[way]
        return pltpu.make_async_remote_copy(
            src_ref=src.at[c], dst_ref=dst.at[c],
            send_sem=ch_send.at[way, c], recv_sem=ch_recv.at[way, c],
            device_id=(me, lax.rem(to, seq)), device_id_type=MESH,
        )

    def local_work(c):
        cs = lanes(c)
        step_c = spread(step_s[...], c)
        ecum_c = spread(ecum_s[...], c)
        toend_c = spread(toend_s[...], c)
        ends = x_ref[:, cs].astype(F32) * step_c * toend_c
        weighted = g_ref[:, cs].astype(F32) * ecum_c
        step_w[:, cs] = step_c
        ecum_w[:, cs] = ecum_c
        toend_w[:, cs] = toend_c
        cum_w[:, cs] = spread(cum_s[...], c, exact=True)
        end_w[:, cs] = ends
        wgrad[:, cs] = weighted
        e_hi, e_lo = halves(ends)
        w_hi, w_lo = halves(weighted)
        left_s[c] = mm(bt3, jnp.concatenate([e_hi, e_hi, e_lo], axis=0))
        right_s[c] = mm(ct3, jnp.concatenate([w_hi, w_hi, w_lo], axis=0))

    def chain_start(c):
        for way, first in ((0, 0), (1, last)):
            @pl.when(z == first)
            def _():
                arrived, leaving, here = ((fin, fout, left_s), (bin_, bout, right_s))[way]
                arrived[c] = jnp.zeros((state, CHUNK), BF16)
                if seq > 1:
                    leaving[c] = here[c].astype(BF16)
                    chain_copy(way, c).start()

    def chain_hop(way, c):
        arrived, leaving, local = ((fin, fout, left_s), (bin_, bout, right_s))[way]
        chain_copy(way, c).wait_recv()

        @pl.when(z != (last, 0)[way])
        def _():
            decay = ecum_w[length - 1 :, lanes(c)]
            leaving[c] = (arrived[c].astype(F32) * decay + local[c]).astype(BF16)
            chain_copy(way, c).start()

    later = iota((length, length), 1) >= iota((length, length), 0)
    def by_head(tile):
        turned = pltpu.roll(tile, head_size, 1)
        return jnp.where(low_half, tile, turned), jnp.where(low_half, turned, tile)

    def tile_work(tile):
        ts = slice(tile * LANES, (tile + 1) * LANES)
        g_tile = g_ref[:, ts].astype(F32)
        inter = inter_s[...]
        cums, steps = by_head(cum_w[:, ts]), by_head(step_w[:, ts])
        mixes, grads, sums = [], [], []
        for part in range(per_tile):
            head = tile * per_tile + part
            gap = cumt_s[head : head + 1, :] - cums[part]
            weights = jnp.exp(jnp.where(later, gap, -1e30))
            mine = low_half if part == 0 else jnp.logical_not(low_half)
            g_part = jnp.where(mine, g_tile, 0.0).astype(BF16)
            shared = m_s[head] * steps[part] * weights
            sums.append(shared)
            rows_s[head : head + 1, :] = jnp.sum(shared * inter, axis=0, keepdims=True)
            mixes += list(halves(inter * weights))
            grads += [g_part, g_part]
        ig_acc[...] += sum(sums[1:], sums[0])
        sgrad[:, ts] = mm(jnp.concatenate(mixes, axis=1), jnp.concatenate(grads, axis=0))

    def reduce_heads(value, c):
        hot = hot_s[c, 0:LANES, :]
        high, low = halves(value)
        return mm(high, hot, NT) + mm(low, hot, NT)

    b_hi, b_lo = halves(b_rows)
    c_hi, c_lo = halves(c_rows)
    bpair = jnp.concatenate([b_hi, b_lo], axis=1)
    cpair = jnp.concatenate([c_hi, c_lo], axis=1)

    def carried_work(c):
        cs = lanes(c)
        state_in, state_grad = fin[c], bin_[c]
        weighted, ends = wgrad[:, cs], end_w[:, cs]
        inter_out = mm(cpair, jnp.concatenate([state_in, state_in], axis=0))
        reach = mm(bpair, jnp.concatenate([state_grad, state_grad], axis=0))
        w_hi, w_lo = halves(weighted)
        e_hi, e_lo = halves(ends)
        cg_s[...] += mm(w_hi, state_in, NT) + mm(w_lo, state_in, NT)
        bg_s[...] += mm(e_hi, state_grad, NT) + mm(e_lo, state_grad, NT)
        total = sgrad[:, cs] + toend_w[:, cs] * reach
        x_part, g_part = x_ref[:, cs].astype(F32), g_ref[:, cs].astype(F32)
        decay = ecum_w[length - 1 :, cs]
        product = state_grad.astype(F32) * state_in.astype(F32)
        at_end = jnp.sum(ends * reach, axis=0, keepdims=True) + decay * jnp.sum(
            product, axis=0, keepdims=True
        )
        stacked = jnp.concatenate(
            [weighted * inter_out, x_part * total, jnp.broadcast_to(at_end, (8, CHUNK))], axis=0
        )
        red_s[...] += reduce_heads(stacked, c)
        skip_c = spread(jnp.broadcast_to(par[2:3, :], (8, LANES)), c)[0:1, :]
        hg_ref[:, cs] = (g_part * skip_c + step_w[:, cs] * total).astype(BF16)

    ig_acc[...] = jnp.zeros_like(ig_acc)
    rows_s[...] = jnp.zeros_like(rows_s)
    cg_s[...] = jnp.zeros_like(cg_s)
    bg_s[...] = jnp.zeros_like(bg_s)
    red_s[...] = jnp.zeros_like(red_s)
    tiles = CHUNK // LANES

    for c in range(chunks):
        local_work(c)
        chain_start(c)

    lag = max(last - 1, 0)
    steps = chunks + lag
    budget = -(-(chunks * tiles + 2 * chunks) // steps)
    done = 0
    for s in range(steps):
        if seq > 1:
            forward, back = s - (z - 1), s - (last - 1 - z)

            @pl.when(jnp.logical_and(z > 0, jnp.logical_and(forward >= 0, forward < chunks)))
            def _():
                chain_hop(0, forward)

            @pl.when(jnp.logical_and(z < last, jnp.logical_and(back >= 0, back < chunks)))
            def _():
                chain_hop(1, back)

        due = budget if s < lag else max(budget - 2, 0)
        if s == steps - 1:
            due = chunks * tiles
        for tile in range(done, min(done + due, chunks * tiles)):
            tile_work(tile)
        done = min(done + due, chunks * tiles)
        if s >= lag:
            carried_work(s - lag)

    store_hg = pltpu.make_async_copy(hg_ref, hg_hbm, out_sem.at[0])
    store_hg.start()
    acc = ig_acc[...]
    c_grad = cg_s[...] + lax.dot_general(
        acc, b_rows, TN, precision=HIGHEST, preferred_element_type=F32
    )
    b_grad = bg_s[...] + jnp.dot(acc, c_rows, precision=HIGHEST, preferred_element_type=F32)
    pair = (pl.ds(0, length), pl.ds(length, part_rows))

    def gp_copy(p, k, owner, target):
        return pltpu.make_async_remote_copy(
            src_ref=gpin.at[owner, pair[p]], dst_ref=gpin.at[owner, pair[p]],
            send_sem=gp_send.at[p, k], recv_sem=gp_recv.at[p, k],
            device_id=at_dp(target), device_id_type=MESH,
        )

    def gf_copy(p, k, owner):
        return pltpu.make_async_remote_copy(
            src_ref=gpin.at[owner, pair[p]], dst_ref=gpin.at[owner, pair[p]],
            send_sem=gf_send.at[p, k], recv_sem=gf_recv.at[p, k],
            device_id=at_dp(sib), device_id_type=MESH,
        )

    def gp_start(p):
        for k in range(1, half):
            gp_copy(p, k, me, peer(k)).start()
        gp_copy(p, 0, me, sib).start()

    state_part = jnp.concatenate([b_grad, c_grad], axis=1).astype(BF16)
    gpin[me, 0:length, :] = state_part
    gp_start(0)
    step = step_s[...]
    direct = red_s[length : 2 * length, :]
    cum_grad = rows_s[...].T + red_s[0:length, :] - step * direct
    is_last = iota((length, LANES), 0) == length - 1
    cum_grad = cum_grad + jnp.where(is_last, red_s[2 * length : 2 * length + 1, :], 0.0)
    upper = later.astype(F32)
    decay_grad = jnp.dot(upper, cum_grad, precision=HIGHEST, preferred_element_type=F32)
    step_grad = direct - par[1:2, :] * decay_grad
    pre_grad = step_grad / (1.0 + jnp.exp(-pre_s[...]))
    gpin[me, length:, :] = pack(pre_grad, part_rows).astype(BF16)
    gp_start(1)
    gproj = jnp.concatenate([state_part, pre_grad.astype(BF16)], axis=1)
    for c in range(width // CHUNK):
        cs = slice(c * CHUNK, (c + 1) * CHUNK)
        ig_ref[:, cs] = mm(gproj, wall[cs, :], NT).astype(BF16)
    store_ig = pltpu.make_async_copy(ig_ref, ig_hbm, out_sem.at[1])
    store_ig.start()

    for k in range(1, dp):
        fa_copy(k).wait_recv()

    def gradient_of(index):
        steps = unpack(gpin[index, length:, :].astype(F32), length).astype(BF16)
        return mm(ftin[index], jnp.concatenate([gpin[index, 0:length, :], steps], axis=1))

    total = mm(ftin[me], gproj)
    for k in range(1, half):
        for p in range(2):
            gp_copy(p, k, source(k), peer(k)).wait_recv()
            gf_copy(p, k, source(k)).start()
        total = total + gradient_of(source(k))
    for p in range(2):
        gp_copy(p, 0, sib, sib).wait_recv()
    total = total + gradient_of(sib)
    for k in range(1, half):
        other = lax.rem(sib + dp - 2 * k, dp)
        for p in range(2):
            gf_copy(p, k, other).wait_recv()
        total = total + gradient_of(other)

    zout[0:rows, :] = total[:, 0:LANES].astype(BF16)
    zout[rows:packed, :] = pack(total[:, LANES:], share).astype(BF16)
    if owners * piece > packed:
        zout[packed:, :] = jnp.zeros((owners * piece - packed, LANES), BF16)

    def z_piece(index):
        return pl.ds(pl.multiple_of(index * piece, 16), piece)

    def to_z(k):
        return lax.rem(z + k, seq)

    def from_z(k):
        return lax.rem(z + seq - k, seq)

    def zr_copy(k):
        return pltpu.make_async_remote_copy(
            src_ref=zout.at[z_piece(to_z(k))], dst_ref=zin.at[k],
            send_sem=zr_send.at[k], recv_sem=zr_recv.at[k],
            device_id=(me, to_z(k)), device_id_type=MESH,
        )

    def za_copy(k, owner):
        return pltpu.make_async_remote_copy(
            src_ref=final.at[z_piece(owner)], dst_ref=final.at[z_piece(owner)],
            send_sem=za_send.at[k], recv_sem=za_recv.at[k],
            device_id=(me, to_z(k)), device_id_type=MESH,
        )

    owner_here = z < owners
    for k in range(1, seq):
        @pl.when(to_z(k) < owners)
        def _():
            zr_copy(k).start()

    @pl.when(owner_here)
    def _():
        mine = zout[z_piece(z), :].astype(F32)
        for k in range(1, seq):
            zr_copy(k).wait_recv()
            mine = mine + zin[k].astype(F32)
        final[z_piece(z), :] = (mine * scale).astype(BF16)
        for k in range(1, seq):
            za_copy(k, z).start()

    for k in range(1, seq):
        @pl.when(from_z(k) < owners)
        def _():
            za_copy(k, from_z(k)).wait_recv()

    bcg_ref[...] = final[0:rows, :].astype(F32)
    tail = unpack(final[rows:packed, :].astype(F32), rows)
    if padded > rows:
        tail = jnp.concatenate([tail, jnp.zeros((padded - rows, LANES), F32)], axis=0)
    dtg_ref[...] = tail.T[0:heads, 0:rows]

    store_hg.wait()
    store_ig.wait()
    ag_copy(0, me, sib).wait_send()
    for k in range(1, half):
        ag_copy(k, me, peer(k)).wait_send()
        fw_copy(k, source(k)).wait_send()
        for p in range(2):
            gp_copy(p, k, me, peer(k)).wait_send()
            gf_copy(p, k, source(k)).wait_send()
    for p in range(2):
        gp_copy(p, 0, me, sib).wait_send()
    for k in range(1, dp):
        fa_copy(k).wait_send()
    for k in range(1, seq):
        @pl.when(to_z(k) < owners)
        def _():
            zr_copy(k).wait_send()

    @pl.when(owner_here)
    def _():
        for k in range(1, seq):
            za_copy(k, z).wait_send()

    for way, final_one in ((0, last), (1, 0)):
        @pl.when(z != final_one)
        def _():
            @pl.loop(0, chunks)
            def _(c):
                chain_copy(way, c).wait_send()


def place(*refs):
    sources, targets, held, sem = refs[0:4], refs[4:8], refs[8:12], refs[12]
    slots = []
    for index, source in enumerate(sources):
        parts = 4 if source.dtype == BF16 else 1
        step = source.shape[0] // parts
        slots += [(index, slice(part * step, (part + 1) * step)) for part in range(parts)]
    loads, stores = [], []
    for slot, (index, part) in enumerate(slots):
        source, middle, target = sources[index].at[part], held[index].at[part], targets[index].at[part]
        loads.append(pltpu.make_async_copy(source, middle, sem.at[0, slot]))
        stores.append(pltpu.make_async_copy(middle, target, sem.at[1, slot]))
        loads[-1].start()
    for load, store in zip(loads, stores):
        load.wait()
        store.start()
    for store in stores:
        store.wait()


def body(dp, seq, features, head_inputs, out_grad, bc_weight, dt_weight, dt_bias, decay_rate, skip_gain):
    _, length, width = features.shape
    inner = head_inputs.shape[2]
    heads = dt_bias.shape[0]
    rows, both = bc_weight.shape
    state = both // 2
    half = dp // 2
    chunks = inner // CHUNK
    share = -(-rows // (16 * (LANES // heads))) * 16
    part_rows = -(-length // (16 * (LANES // heads))) * 16
    packed = rows + share
    piece = -(-packed // (16 * seq)) * 16
    owners = -(-packed // piece)
    scale = 1.0 / math.sqrt(dp * seq * length)
    vmem, dma = pltpu.VMEM, pltpu.SemaphoreType.DMA
    square = vmem((length, LANES), F32)
    broad = vmem((length, inner), F32)
    states = vmem((chunks, state, CHUNK), F32)
    wire = vmem((chunks, state, CHUNK), BF16)
    narrow = vmem((length, state), F32)
    scratch = dict(
        f_ref=vmem((length, width), BF16), x_ref=vmem((length, inner), BF16),
        g_ref=vmem((length, inner), BF16), in_sem=dma((3,)),
        ig_ref=vmem((length, width), BF16), hg_ref=vmem((length, inner), BF16), out_sem=dma((2,)),
        ft_s=vmem((width, length), BF16), m_s=vmem((heads, length, length), F32),
        cum_w=broad,
        wall=vmem((width, 2 * LANES), BF16), par=vmem((8, LANES), F32),
        pre_s=square, step_s=square, cum_s=square, cumt_s=square, ecum_s=square,
        toend_s=square, proj_s=square, bct_s=square, inter_s=square, rows_s=square,
        ig_acc=square,
        step_w=broad, ecum_w=broad, toend_w=broad, end_w=broad, wgrad=broad, sgrad=broad,
        left_s=states, right_s=states,
        fin=wire, bin_=wire, fout=wire, bout=wire,
        red_s=vmem((2 * length + 8, LANES), F32), bg_s=narrow, cg_s=narrow,
        hot_s=vmem((chunks, 2 * LANES, CHUNK), BF16), wpack=vmem((dp, packed, LANES), BF16),
        ftin=vmem((dp, rows, length), BF16), gpin=vmem((dp, length + part_rows, LANES), BF16),
        fa_send=dma((dp,)), fa_recv=dma((dp,)),
        zout=vmem((owners * piece, LANES), BF16), zin=vmem((seq, piece, LANES), BF16),
        final=vmem((owners * piece, LANES), BF16),
        ag_send=dma((half,)), ag_recv=dma((half,)), fw_send=dma((half,)), fw_recv=dma((half,)),
        ch_send=dma((2, chunks)), ch_recv=dma((2, chunks)),
        gp_send=dma((2, half)), gp_recv=dma((2, half)),
        gf_send=dma((2, half)), gf_recv=dma((2, half)),
        zr_send=dma((seq,)), zr_recv=dma((seq,)), za_send=dma((seq,)), za_recv=dma((seq,)),
    )
    whole = pl.BlockSpec(memory_space=pltpu.VMEM)
    results = pl.pallas_call(
        functools.partial(kernel, dp, seq, heads, scale),
        out_shape=(
            jax.ShapeDtypeStruct((length, width), BF16),
            jax.ShapeDtypeStruct((length, inner), BF16),
            jax.ShapeDtypeStruct((rows, both), F32),
            jax.ShapeDtypeStruct((heads, rows), F32),
        ),
        in_specs=[pl.BlockSpec(memory_space=pltpu.HBM)] * 3 + [whole] * 5,
        out_specs=(pl.BlockSpec(memory_space=pltpu.HBM),) * 2 + (whole,) * 2,
        scratch_shapes=scratch,
        compiler_params=pltpu.CompilerParams(
            collective_id=0, has_side_effects=True, vmem_limit_bytes=56 * 2**20
        ),
        name="mixer_backward",
    )(
        features[0], head_inputs[0], out_grad[0], bc_weight, dt_weight.T,
        dt_bias[None, :], decay_rate[None, :], skip_gain[None, :],
    )
    hbm = pl.BlockSpec(memory_space=pltpu.HBM)
    results = pl.pallas_call(
        place,
        out_shape=tuple(jax.ShapeDtypeStruct(part.shape, part.dtype) for part in results),
        in_specs=[hbm] * 4,
        out_specs=(hbm,) * 4,
        scratch_shapes=[vmem(part.shape, part.dtype) for part in results] + [dma((2, 10))],
        name="place_results",
    )(*results)
    input_grad, head_grad, bc_grad, dt_grad = results
    return input_grad[None], head_grad[None], bc_grad, dt_grad.T


def solution(mesh):
    tokens = P("dp", "seq", None)
    return jax.shard_map(
        functools.partial(body, mesh.shape["dp"], mesh.shape["seq"]),
        mesh=mesh,
        in_specs=(tokens, tokens, tokens, P("dp", None), P("dp", None), P(), P(), P()),
        out_specs=(tokens, tokens, P("dp", None), P("dp", None)),
        check_vma=False,
    )
```

```python
import functools
import math

import jax
import jax.numpy as jnp
from jax import lax
from jax.experimental import pallas as pl
from jax.experimental.pallas import tpu as pltpu
from jax.sharding import PartitionSpec as P

MESH = pl.DeviceIdType.MESH
F32, BF16 = jnp.float32, jnp.bfloat16
LANES = 128
CHUNK = 512
HIGHEST = lax.Precision.HIGHEST
NT = (((1,), (1,)), ((), ()))
TN = (((0,), (0,)), ((), ()))


def halves(value):
    high = value.astype(BF16)
    return high, (value - high.astype(F32)).astype(BF16)


def mm(left, right, dims=None):
    if dims is None:
        return jnp.dot(left, right, preferred_element_type=F32)
    return lax.dot_general(left, right, dims, preferred_element_type=F32)


def iota(shape, dim):
    return lax.broadcasted_iota(jnp.int32, shape, dim)


def kernel(
    dp, seq, heads, scale,
    f_hbm, x_hbm, g_hbm, wbc_ref, wdt_ref, bias_ref, decay_ref, skip_ref,
    ig_hbm, hg_hbm, bcg_ref, dtg_ref, *,
    ig_ref, hg_ref, out_sem,
    f_ref, x_ref, g_ref, in_sem, ft_s, m_s, cum_w, hot_s, wpack, ftin, gpin, fa_send, fa_recv,
    wall, par, pre_s, step_s, cum_s, cumt_s, ecum_s, toend_s, proj_s, bct_s, inter_s, rows_s,
    ig_acc, step_w, ecum_w, toend_w, end_w, wgrad, sgrad, left_s, right_s,
    fin, bin_, fout, bout, red_s, bg_s, cg_s,
    zout, zin, final,
    ag_send, ag_recv, fw_send, fw_recv, ch_send, ch_recv,
    gp_send, gp_recv, gf_send, gf_recv, zr_send, zr_recv, za_send, za_recv,
):
    me, z = lax.axis_index("dp"), lax.axis_index("seq")
    last = seq - 1
    half = dp // 2
    sib = me + 1 - 2 * lax.rem(me, 2)
    length, inner = x_ref.shape
    width = f_ref.shape[1]
    rows = wbc_ref.shape[0]
    state = wbc_ref.shape[1] // 2
    head_size = inner // heads
    chunks = inner // CHUNK
    groups = LANES // heads
    share = -(-rows // (16 * groups)) * 16
    packed = rows + share
    piece = -(-packed // (16 * seq)) * 16
    owners = -(-packed // piece)

    part_rows = -(-length // (16 * groups)) * 16

    def pack(value, each):
        value = jnp.where(iota(value.shape, 1) < heads, value, 0.0)
        parts = []
        for g in range(groups):
            part = value[g * each : min((g + 1) * each, value.shape[0]), :]
            if part.shape[0] < each:
                empty = jnp.zeros((each - part.shape[0], LANES), F32)
                part = jnp.concatenate([part, empty], axis=0)
            parts.append(pltpu.roll(part, g * heads, 1) if g else part)
        return sum(parts[1:], parts[0])

    def unpack(value, count):
        each = value.shape[0]
        parts = []
        for g in range(groups):
            part = pltpu.roll(value, LANES - g * heads, 1) if g else value
            parts.append(part[0 : min(each, count - g * each), :])
        return jnp.concatenate(parts, axis=0)

    def at_dp(target):
        return (target, z)

    def peer(k):
        return lax.rem(me + 2 * k, dp)

    def source(k):
        return lax.rem(me + dp - 2 * k, dp)

    loads = [
        pltpu.make_async_copy(src, dst, in_sem.at[i])
        for i, (src, dst) in enumerate(((x_hbm, x_ref), (g_hbm, g_ref), (f_hbm, f_ref)))
    ]
    for load in loads:
        load.start()
    barrier = pltpu.get_barrier_semaphore()
    for k in range(1, dp):
        pl.semaphore_signal(
            barrier, inc=1, device_id=at_dp(lax.rem(me + k, dp)), device_id_type=MESH
        )
    for k in range(1, seq):
        pl.semaphore_signal(barrier, inc=1, device_id=(me, lax.rem(z + k, seq)), device_id_type=MESH)

    def block(index):
        return pl.ds(pl.multiple_of(index * rows, 16), rows)

    wpack[me, 0:rows, :] = wbc_ref[...]
    padded = -(-rows // LANES) * LANES
    wide = jnp.concatenate(
        [wdt_ref[...].astype(F32), jnp.zeros((LANES - heads, rows), F32)], axis=0
    )
    if padded > rows:
        wide = jnp.concatenate([wide, jnp.zeros((LANES, padded - rows), F32)], axis=1)
    wpack[me, rows:, :] = pack(wide.T[0:rows, :], share).astype(BF16)
    par[...] = jnp.zeros_like(par)
    par[0:1, 0:heads] = bias_ref[...]
    par[1:2, 0:heads] = decay_ref[...]
    par[2:3, 0:heads] = skip_ref[...]
    pl.semaphore_wait(barrier, dp + seq - 2)

    def ag_copy(k, owner, target):
        return pltpu.make_async_remote_copy(
            src_ref=wpack.at[owner], dst_ref=wpack.at[owner],
            send_sem=ag_send.at[k], recv_sem=ag_recv.at[k],
            device_id=at_dp(target), device_id_type=MESH,
        )

    def fw_copy(k, owner):
        return pltpu.make_async_remote_copy(
            src_ref=wpack.at[owner], dst_ref=wpack.at[owner],
            send_sem=fw_send.at[k], recv_sem=fw_recv.at[k],
            device_id=at_dp(sib), device_id_type=MESH,
        )

    for k in range(1, half):
        ag_copy(k, me, peer(k)).start()
    ag_copy(0, me, sib).start()
    for load in loads:
        load.wait()

    low_half = iota((length, LANES), 1) < head_size
    per_tile = LANES // head_size
    tile_count = inner // LANES

    def early_work(tile):
        ts = slice(tile * LANES, (tile + 1) * LANES)
        x_tile, g_full = x_ref[:, ts].astype(F32), g_ref[:, ts]
        for part in range(per_tile):
            mine = low_half if part == 0 else jnp.logical_not(low_half)
            x_part = jnp.where(mine, x_tile, 0.0).astype(BF16)
            m_s[tile * per_tile + part] = mm(x_part, g_full, NT)

    @pl.loop(0, width // CHUNK)
    def _(c):
        cs = pl.ds(pl.multiple_of(c * CHUNK, CHUNK), CHUNK)
        ft_s[cs, :] = f_ref[:, cs].T

    @pl.loop(0, chunks)
    def _(c):
        lane = c * CHUNK + iota((LANES, CHUNK), 1)
        hot = (iota((LANES, CHUNK), 0) == lane // head_size).astype(F32).astype(BF16)
        hot_s[c, 0:LANES, :] = hot
        hot_s[c, LANES:, :] = hot

    for k in range(1, half):
        for tile in range(tile_count * (k - 1) // (half - 1), tile_count * k // (half - 1)):
            early_work(tile)
        ag_copy(k, source(k), peer(k)).wait_recv()
        fw_copy(k, source(k)).start()
    ag_copy(0, sib, sib).wait_recv()
    for k in range(1, half):
        fw_copy(k, lax.rem(sib + dp - 2 * k, dp)).wait_recv()

    def fa_copy(k):
        target = lax.rem(me + k, dp)
        return pltpu.make_async_remote_copy(
            src_ref=ft_s.at[block(target)], dst_ref=ftin.at[me],
            send_sem=fa_send.at[k], recv_sem=fa_recv.at[k],
            device_id=at_dp(target), device_id_type=MESH,
        )

    for k in range(1, dp):
        fa_copy(k).start()
    ftin[me] = ft_s[block(me), :]

    @pl.loop(0, dp, unroll=4)
    def _(i):
        wall[block(i), 0:LANES] = wpack[i, 0:rows, :]
        wall[block(i), LANES:] = unpack(wpack[i, rows:, :].astype(F32), rows).astype(BF16)

    projection = mm(f_ref[...], wall[...])
    proj_s[...] = projection[:, :LANES]
    pre = projection[:, LANES:] + par[0:1, :]
    pre_s[...] = pre
    step = jnp.maximum(pre, 0.0) + jnp.log1p(jnp.exp(-jnp.abs(pre)))
    step_s[...] = step
    lower = (iota((length, length), 0) >= iota((length, length), 1)).astype(F32)
    cum = jnp.dot(
        lower, -par[1:2, :] * step, precision=HIGHEST, preferred_element_type=F32
    )
    cum_s[...] = cum
    cumt_s[...] = cum.T
    ecum_s[...] = jnp.exp(cum)
    toend_s[...] = jnp.exp(cum[length - 1 :, :] - cum)
    bct_s[...] = proj_s[...].T
    bt = bct_s[0:state, :]
    ct = bct_s[state:, :]
    bt_hi, bt_lo = halves(bt)
    ct_hi, ct_lo = halves(ct)
    bt3 = jnp.concatenate([bt_hi, bt_lo, bt_hi], axis=1)
    ct3 = jnp.concatenate([ct_hi, ct_lo, ct_hi], axis=1)
    b_rows = proj_s[:, 0:state]
    c_rows = proj_s[:, state:]
    inter_s[...] = jnp.dot(b_rows, ct, precision=HIGHEST, preferred_element_type=F32)

    def spread(value, c, exact=False):
        high, low = halves(value)
        result = mm(jnp.concatenate([high, low], axis=1), hot_s[c])
        if exact:
            rest = value - high.astype(F32) - low.astype(F32)
            result = result + mm(rest.astype(BF16), hot_s[c, 0:LANES, :])
        return result

    def lanes(c):
        if isinstance(c, int):
            return slice(c * CHUNK, (c + 1) * CHUNK)
        return pl.ds(pl.multiple_of(c * CHUNK, CHUNK), CHUNK)

    def chain_copy(way, c):
        src, dst = ((fout, fin), (bout, bin_))[way]
        to = (z + 1, z + last)[way]
        return pltpu.make_async_remote_copy(
            src_ref=src.at[c], dst_ref=dst.at[c],
            send_sem=ch_send.at[way, c], recv_sem=ch_recv.at[way, c],
            device_id=(me, lax.rem(to, seq)), device_id_type=MESH,
        )

    def local_work(c):
        cs = lanes(c)
        step_c = spread(step_s[...], c)
        ecum_c = spread(ecum_s[...], c)
        toend_c = spread(toend_s[...], c)
        ends = x_ref[:, cs].astype(F32) * step_c * toend_c
        weighted = g_ref[:, cs].astype(F32) * ecum_c
        step_w[:, cs] = step_c
        ecum_w[:, cs] = ecum_c
        toend_w[:, cs] = toend_c
        cum_w[:, cs] = spread(cum_s[...], c, exact=True)
        end_w[:, cs] = ends
        wgrad[:, cs] = weighted
        e_hi, e_lo = halves(ends)
        w_hi, w_lo = halves(weighted)
        left_s[c] = mm(bt3, jnp.concatenate([e_hi, e_hi, e_lo], axis=0))
        right_s[c] = mm(ct3, jnp.concatenate([w_hi, w_hi, w_lo], axis=0))

    def chain_start(c):
        for way, first in ((0, 0), (1, last)):
            @pl.when(z == first)
            def _():
                arrived, leaving, here = ((fin, fout, left_s), (bin_, bout, right_s))[way]
                arrived[c] = jnp.zeros((state, CHUNK), BF16)
                if seq > 1:
                    leaving[c] = here[c].astype(BF16)
                    chain_copy(way, c).start()

    def chain_hop(way, c):
        arrived, leaving, local = ((fin, fout, left_s), (bin_, bout, right_s))[way]
        chain_copy(way, c).wait_recv()

        @pl.when(z != (last, 0)[way])
        def _():
            decay = ecum_w[length - 1 :, lanes(c)]
            leaving[c] = (arrived[c].astype(F32) * decay + local[c]).astype(BF16)
            chain_copy(way, c).start()

    later = iota((length, length), 1) >= iota((length, length), 0)
    def by_head(tile):
        turned = pltpu.roll(tile, head_size, 1)
        return jnp.where(low_half, tile, turned), jnp.where(low_half, turned, tile)

    def tile_work(tile):
        ts = slice(tile * LANES, (tile + 1) * LANES)
        g_tile = g_ref[:, ts].astype(F32)
        inter = inter_s[...]
        cums, steps = by_head(cum_w[:, ts]), by_head(step_w[:, ts])
        mixes, grads, sums = [], [], []
        for part in range(per_tile):
            head = tile * per_tile + part
            gap = cumt_s[head : head + 1, :] - cums[part]
            weights = jnp.exp(jnp.where(later, gap, -1e30))
            mine = low_half if part == 0 else jnp.logical_not(low_half)
            g_part = jnp.where(mine, g_tile, 0.0).astype(BF16)
            scaled = m_s[head] * steps[part]
            sums.append(scaled * weights)
            mixing = (inter * weights).astype(BF16)
            rows_s[head : head + 1, :] = jnp.sum(
                scaled * mixing.astype(F32), axis=0, keepdims=True
            )
            mixes.append(mixing)
            grads.append(g_part)
        ig_acc[...] += sum(sums[1:], sums[0])
        sgrad[:, ts] = mm(jnp.concatenate(mixes, axis=1), jnp.concatenate(grads, axis=0))

    def reduce_heads(value, c):
        hot = hot_s[c, 0:LANES, :]
        high, low = halves(value)
        return mm(high, hot, NT) + mm(low, hot, NT)

    b_hi, b_lo = halves(b_rows)
    c_hi, c_lo = halves(c_rows)
    bpair = jnp.concatenate([b_hi, b_lo], axis=1)
    cpair = jnp.concatenate([c_hi, c_lo], axis=1)

    def carried_work(c):
        cs = lanes(c)
        state_in, state_grad = fin[c], bin_[c]
        weighted, ends = wgrad[:, cs], end_w[:, cs]
        inter_out = mm(cpair, jnp.concatenate([state_in, state_in], axis=0))
        reach = mm(bpair, jnp.concatenate([state_grad, state_grad], axis=0))
        w_hi, w_lo = halves(weighted)
        e_hi, e_lo = halves(ends)
        cg_s[...] += mm(w_hi, state_in, NT) + mm(w_lo, state_in, NT)
        bg_s[...] += mm(e_hi, state_grad, NT) + mm(e_lo, state_grad, NT)
        total = sgrad[:, cs] + toend_w[:, cs] * reach
        x_part, g_part = x_ref[:, cs].astype(F32), g_ref[:, cs].astype(F32)
        decay = ecum_w[length - 1 :, cs]
        product = state_grad.astype(F32) * state_in.astype(F32)
        at_end = jnp.sum(ends * reach, axis=0, keepdims=True) + decay * jnp.sum(
            product, axis=0, keepdims=True
        )
        stacked = jnp.concatenate(
            [weighted * inter_out, x_part * total, jnp.broadcast_to(at_end, (8, CHUNK))], axis=0
        )
        red_s[...] += reduce_heads(stacked, c)
        skip_c = spread(jnp.broadcast_to(par[2:3, :], (8, LANES)), c)[0:1, :]
        hg_ref[:, cs] = (g_part * skip_c + step_w[:, cs] * total).astype(BF16)

    ig_acc[...] = jnp.zeros_like(ig_acc)
    rows_s[...] = jnp.zeros_like(rows_s)
    cg_s[...] = jnp.zeros_like(cg_s)
    bg_s[...] = jnp.zeros_like(bg_s)
    red_s[...] = jnp.zeros_like(red_s)
    tiles = CHUNK // LANES

    for c in range(chunks):
        local_work(c)
        chain_start(c)

    lag = max(last - 1, 0)
    steps = chunks + lag
    budget = -(-(chunks * tiles + 2 * chunks) // steps)
    done = 0
    for s in range(steps):
        if seq > 1:
            forward, back = s - (z - 1), s - (last - 1 - z)

            @pl.when(jnp.logical_and(z > 0, jnp.logical_and(forward >= 0, forward < chunks)))
            def _():
                chain_hop(0, forward)

            @pl.when(jnp.logical_and(z < last, jnp.logical_and(back >= 0, back < chunks)))
            def _():
                chain_hop(1, back)

        due = budget if s < lag else max(budget - 2, 0)
        if s == steps - 1:
            due = chunks * tiles
        for tile in range(done, min(done + due, chunks * tiles)):
            tile_work(tile)
        done = min(done + due, chunks * tiles)
        if s >= lag:
            carried_work(s - lag)

    store_hg = pltpu.make_async_copy(hg_ref, hg_hbm, out_sem.at[0])
    store_hg.start()
    acc = ig_acc[...]
    c_grad = cg_s[...] + lax.dot_general(
        acc, b_rows, TN, precision=HIGHEST, preferred_element_type=F32
    )
    b_grad = bg_s[...] + jnp.dot(acc, c_rows, precision=HIGHEST, preferred_element_type=F32)
    pair = (pl.ds(0, length), pl.ds(length, part_rows))

    def gp_copy(p, k, owner, target):
        return pltpu.make_async_remote_copy(
            src_ref=gpin.at[owner, pair[p]], dst_ref=gpin.at[owner, pair[p]],
            send_sem=gp_send.at[p, k], recv_sem=gp_recv.at[p, k],
            device_id=at_dp(target), device_id_type=MESH,
        )

    def gf_copy(p, k, owner):
        return pltpu.make_async_remote_copy(
            src_ref=gpin.at[owner, pair[p]], dst_ref=gpin.at[owner, pair[p]],
            send_sem=gf_send.at[p, k], recv_sem=gf_recv.at[p, k],
            device_id=at_dp(sib), device_id_type=MESH,
        )

    def gp_start(p):
        for k in range(1, half):
            gp_copy(p, k, me, peer(k)).start()
        gp_copy(p, 0, me, sib).start()

    state_part = jnp.concatenate([b_grad, c_grad], axis=1).astype(BF16)
    gpin[me, 0:length, :] = state_part
    gp_start(0)
    step = step_s[...]
    direct = red_s[length : 2 * length, :]
    cum_grad = rows_s[...].T + red_s[0:length, :] - step * direct
    is_last = iota((length, LANES), 0) == length - 1
    cum_grad = cum_grad + jnp.where(is_last, red_s[2 * length : 2 * length + 1, :], 0.0)
    upper = later.astype(F32)
    decay_grad = jnp.dot(upper, cum_grad, precision=HIGHEST, preferred_element_type=F32)
    step_grad = direct - par[1:2, :] * decay_grad
    pre_grad = step_grad / (1.0 + jnp.exp(-pre_s[...]))
    gpin[me, length:, :] = pack(pre_grad, part_rows).astype(BF16)
    gp_start(1)
    gproj = jnp.concatenate([state_part, pre_grad.astype(BF16)], axis=1)
    for c in range(width // CHUNK):
        cs = slice(c * CHUNK, (c + 1) * CHUNK)
        ig_ref[:, cs] = mm(gproj, wall[cs, :], NT).astype(BF16)
    store_ig = pltpu.make_async_copy(ig_ref, ig_hbm, out_sem.at[1])
    store_ig.start()

    for k in range(1, dp):
        fa_copy(k).wait_recv()

    def gradient_of(index):
        steps = unpack(gpin[index, length:, :].astype(F32), length).astype(BF16)
        return mm(ftin[index], jnp.concatenate([gpin[index, 0:length, :], steps], axis=1))

    total = mm(ftin[me], gproj)
    for k in range(1, half):
        for p in range(2):
            gp_copy(p, k, source(k), peer(k)).wait_recv()
            gf_copy(p, k, source(k)).start()
        total = total + gradient_of(source(k))
    for p in range(2):
        gp_copy(p, 0, sib, sib).wait_recv()
    total = total + gradient_of(sib)
    for k in range(1, half):
        other = lax.rem(sib + dp - 2 * k, dp)
        for p in range(2):
            gf_copy(p, k, other).wait_recv()
        total = total + gradient_of(other)

    zout[0:rows, :] = total[:, 0:LANES].astype(BF16)
    zout[rows:packed, :] = pack(total[:, LANES:], share).astype(BF16)
    if owners * piece > packed:
        zout[packed:, :] = jnp.zeros((owners * piece - packed, LANES), BF16)

    def z_piece(index):
        return pl.ds(pl.multiple_of(index * piece, 16), piece)

    def to_z(k):
        return lax.rem(z + k, seq)

    def from_z(k):
        return lax.rem(z + seq - k, seq)

    def zr_copy(k):
        return pltpu.make_async_remote_copy(
            src_ref=zout.at[z_piece(to_z(k))], dst_ref=zin.at[k],
            send_sem=zr_send.at[k], recv_sem=zr_recv.at[k],
            device_id=(me, to_z(k)), device_id_type=MESH,
        )

    def za_copy(k, owner):
        return pltpu.make_async_remote_copy(
            src_ref=final.at[z_piece(owner)], dst_ref=final.at[z_piece(owner)],
            send_sem=za_send.at[k], recv_sem=za_recv.at[k],
            device_id=(me, to_z(k)), device_id_type=MESH,
        )

    owner_here = z < owners
    for k in range(1, seq):
        @pl.when(to_z(k) < owners)
        def _():
            zr_copy(k).start()

    @pl.when(owner_here)
    def _():
        mine = zout[z_piece(z), :].astype(F32)
        for k in range(1, seq):
            zr_copy(k).wait_recv()
            mine = mine + zin[k].astype(F32)
        final[z_piece(z), :] = (mine * scale).astype(BF16)
        for k in range(1, seq):
            za_copy(k, z).start()

    for k in range(1, seq):
        @pl.when(from_z(k) < owners)
        def _():
            za_copy(k, from_z(k)).wait_recv()

    bcg_ref[...] = final[0:rows, :].astype(F32)
    tail = unpack(final[rows:packed, :].astype(F32), rows)
    if padded > rows:
        tail = jnp.concatenate([tail, jnp.zeros((padded - rows, LANES), F32)], axis=0)
    dtg_ref[...] = tail.T[0:heads, 0:rows]

    store_hg.wait()
    store_ig.wait()
    ag_copy(0, me, sib).wait_send()
    for k in range(1, half):
        ag_copy(k, me, peer(k)).wait_send()
        fw_copy(k, source(k)).wait_send()
        for p in range(2):
            gp_copy(p, k, me, peer(k)).wait_send()
            gf_copy(p, k, source(k)).wait_send()
    for p in range(2):
        gp_copy(p, 0, me, sib).wait_send()
    for k in range(1, dp):
        fa_copy(k).wait_send()
    for k in range(1, seq):
        @pl.when(to_z(k) < owners)
        def _():
            zr_copy(k).wait_send()

    @pl.when(owner_here)
    def _():
        for k in range(1, seq):
            za_copy(k, z).wait_send()

    for way, final_one in ((0, last), (1, 0)):
        @pl.when(z != final_one)
        def _():
            @pl.loop(0, chunks)
            def _(c):
                chain_copy(way, c).wait_send()


def place(*refs):
    sources, targets, held, sem = refs[0:4], refs[4:8], refs[8:12], refs[12]
    slots = []
    for index, source in enumerate(sources):
        parts = 4 if source.dtype == BF16 else 1
        step = source.shape[0] // parts
        slots += [(index, slice(part * step, (part + 1) * step)) for part in range(parts)]
    loads, stores = [], []
    for slot, (index, part) in enumerate(slots):
        source, middle, target = sources[index].at[part], held[index].at[part], targets[index].at[part]
        loads.append(pltpu.make_async_copy(source, middle, sem.at[0, slot]))
        stores.append(pltpu.make_async_copy(middle, target, sem.at[1, slot]))
        loads[-1].start()
    for load, store in zip(loads, stores):
        load.wait()
        store.start()
    for store in stores:
        store.wait()


def body(dp, seq, features, head_inputs, out_grad, bc_weight, dt_weight, dt_bias, decay_rate, skip_gain):
    _, length, width = features.shape
    inner = head_inputs.shape[2]
    heads = dt_bias.shape[0]
    rows, both = bc_weight.shape
    state = both // 2
    half = dp // 2
    chunks = inner // CHUNK
    share = -(-rows // (16 * (LANES // heads))) * 16
    part_rows = -(-length // (16 * (LANES // heads))) * 16
    packed = rows + share
    piece = -(-packed // (16 * seq)) * 16
    owners = -(-packed // piece)
    scale = 1.0 / math.sqrt(dp * seq * length)
    vmem, dma = pltpu.VMEM, pltpu.SemaphoreType.DMA
    square = vmem((length, LANES), F32)
    broad = vmem((length, inner), F32)
    states = vmem((chunks, state, CHUNK), F32)
    wire = vmem((chunks, state, CHUNK), BF16)
    narrow = vmem((length, state), F32)
    scratch = dict(
        f_ref=vmem((length, width), BF16), x_ref=vmem((length, inner), BF16),
        g_ref=vmem((length, inner), BF16), in_sem=dma((3,)),
        ig_ref=vmem((length, width), BF16), hg_ref=vmem((length, inner), BF16), out_sem=dma((2,)),
        ft_s=vmem((width, length), BF16), m_s=vmem((heads, length, length), F32),
        cum_w=broad,
        wall=vmem((width, 2 * LANES), BF16), par=vmem((8, LANES), F32),
        pre_s=square, step_s=square, cum_s=square, cumt_s=square, ecum_s=square,
        toend_s=square, proj_s=square, bct_s=square, inter_s=square, rows_s=square,
        ig_acc=square,
        step_w=broad, ecum_w=broad, toend_w=broad, end_w=broad, wgrad=broad, sgrad=broad,
        left_s=states, right_s=states,
        fin=wire, bin_=wire, fout=wire, bout=wire,
        red_s=vmem((2 * length + 8, LANES), F32), bg_s=narrow, cg_s=narrow,
        hot_s=vmem((chunks, 2 * LANES, CHUNK), BF16), wpack=vmem((dp, packed, LANES), BF16),
        ftin=vmem((dp, rows, length), BF16), gpin=vmem((dp, length + part_rows, LANES), BF16),
        fa_send=dma((dp,)), fa_recv=dma((dp,)),
        zout=vmem((owners * piece, LANES), BF16), zin=vmem((seq, piece, LANES), BF16),
        final=vmem((owners * piece, LANES), BF16),
        ag_send=dma((half,)), ag_recv=dma((half,)), fw_send=dma((half,)), fw_recv=dma((half,)),
        ch_send=dma((2, chunks)), ch_recv=dma((2, chunks)),
        gp_send=dma((2, half)), gp_recv=dma((2, half)),
        gf_send=dma((2, half)), gf_recv=dma((2, half)),
        zr_send=dma((seq,)), zr_recv=dma((seq,)), za_send=dma((seq,)), za_recv=dma((seq,)),
    )
    whole = pl.BlockSpec(memory_space=pltpu.VMEM)
    results = pl.pallas_call(
        functools.partial(kernel, dp, seq, heads, scale),
        out_shape=(
            jax.ShapeDtypeStruct((length, width), BF16),
            jax.ShapeDtypeStruct((length, inner), BF16),
            jax.ShapeDtypeStruct((rows, both), F32),
            jax.ShapeDtypeStruct((heads, rows), F32),
        ),
        in_specs=[pl.BlockSpec(memory_space=pltpu.HBM)] * 3 + [whole] * 5,
        out_specs=(pl.BlockSpec(memory_space=pltpu.HBM),) * 2 + (whole,) * 2,
        scratch_shapes=scratch,
        compiler_params=pltpu.CompilerParams(
            collective_id=0, has_side_effects=True, vmem_limit_bytes=56 * 2**20
        ),
        name="mixer_backward",
    )(
        features[0], head_inputs[0], out_grad[0], bc_weight, dt_weight.T,
        dt_bias[None, :], decay_rate[None, :], skip_gain[None, :],
    )
    hbm = pl.BlockSpec(memory_space=pltpu.HBM)
    results = pl.pallas_call(
        place,
        out_shape=tuple(jax.ShapeDtypeStruct(part.shape, part.dtype) for part in results),
        in_specs=[hbm] * 4,
        out_specs=(hbm,) * 4,
        scratch_shapes=[vmem(part.shape, part.dtype) for part in results] + [dma((2, 10))],
        name="place_results",
    )(*results)
    input_grad, head_grad, bc_grad, dt_grad = results
    return input_grad[None], head_grad[None], bc_grad, dt_grad.T


def solution(mesh):
    tokens = P("dp", "seq", None)
    return jax.shard_map(
        functools.partial(body, mesh.shape["dp"], mesh.shape["seq"]),
        mesh=mesh,
        in_specs=(tokens, tokens, tokens, P("dp", None), P("dp", None), P(), P(), P()),
        out_specs=(tokens, tokens, P("dp", None), P("dp", None)),
        check_vma=False,
    )
```
